32 devices in a mesh: rep: 8 (over y, x, core), shard: 4 (over z).
Axes of the slice: x: 2, y: 2, z: 4, core: 2. Of those that a mesh axis runs over, the one named last changes fastest.
Arguments:
- tokens: bfloat16 [32, 128, 768], P(('rep', 'shard')), may hold values from -6 to 6
- segment_ids: int32 [32, 128], P(('rep', 'shard')), may hold values from 0 to 3, never falling along the last dimension, each value on 1 to 64 neighbouring positions
- attn_gain: bfloat16 [768], P('shard'), may hold values from 0.5 to 1.5
- qkv_weight: bfloat16 [768, 2304], P('shard'), may hold values from -0.21875 to 0.21875
- attn_out_weight: bfloat16 [768, 768], P('shard'), may hold values from -1.75 to 1.75
- mlp_gain: bfloat16 [768], P('shard'), may hold values from 0.5 to 1.5
- in_weight: bfloat16 [768, 2304], P('shard'), may hold values from -0.21875 to 0.21875
- out_weight: bfloat16 [1152, 768], P('shard'), may hold values from -0.25 to 0.25
- cotangent: bfloat16 [32, 128, 768], P(('rep', 'shard')), may hold values from -6 to 6
Outputs:
- output: bfloat16 [32, 128, 768], P(('rep', 'shard'))
- grad_tokens: float32 [32, 128, 768], P(('rep', 'shard'))
- grad_attn_gain: float32 [768], P('shard')
- grad_qkv_weight: float32 [768, 2304], P('shard')
- grad_attn_out_weight: float32 [768, 768], P('shard')
- grad_mlp_gain: float32 [768], P('shard')
- grad_in_weight: float32 [768, 2304], P('shard')
- grad_out_weight: float32 [1152, 768], P('shard')
The draws below stay inside these ranges and needn't reach their ends.
Inputs may be any that keep to these rules, and one draw needn't show every extreme that they name: `segment_ids`: in each block the ids never fall; every id of 0 to 3 marks 1 to 64 consecutive tokens, and some id exactly 64.
All inputs are finite; a program needn't handle non-finite values.
Results may differ from the reference program's by a relative error of at most 0.013.
The reference program's roundings to bfloat16 on the way count: a program that leaves them out, or rounds other values in their place, can miss the bound.
Values may be sent and summed in bfloat16 or wider, within the bound.
No kernel may reach another device: no remote copies, remote signals or barrier semaphores. Data moves between devices by JAX's collectives and lax.ppermute only.
A program may use at most 128 MiB of HBM per device.

```python
import math
import jax
import jax.numpy as jnp
import numpy as np
from jax import lax

D = 768
H = 12
HD = 64
FF = 1152
BLK = 128
DOCS = 4
BLOCKS = 32


def block_levels(own_key, dims, split, least, largest):
    level = 1.0
    for dim, blocks in split:
        steps = jax.random.uniform(jax.random.fold_in(jax.random.fold_in(own_key, 6), dim), (blocks,), jnp.float32, least / len(split), largest / len(split))
        level = level * jnp.repeat(jnp.exp(steps), dims[dim] // blocks).reshape((-1,) + (1,) * (len(dims) - 1 - dim))
    return level


def split_up(count, total, limit, slope):
    weights = [(1 << 20) // math.isqrt(grade ** slope) + 1 for grade in range(2, count + 1)]
    spare, counts = total - limit - (count - 1), [1] * (count - 1)
    while spare > 0:
        candidates = [i for i in range(count - 1) if counts[i] < limit]
        pool, budget = sum([weights[i] for i in candidates]), spare
        for i in candidates:
            extra = min(limit - counts[i], max(1, budget * weights[i] // pool), spare)
            counts[i] = counts[i] + extra
            spare = spare - extra
    return np.array([limit] + counts)


def ragged_sizes(key, amount, total, bound, slope):
    if amount == 2:
        one = jax.random.randint(key, (), max(1, total - bound), min(bound, total - 1) + 1)
        return jnp.stack([one, total - one])
    tallies = jnp.asarray(split_up(amount, total, bound, slope), jnp.int32)
    pairs = (amount - 1) // 2
    donor, sink = tallies[1:1 + 2 * pairs:2], tallies[2:2 + 2 * pairs:2]
    slack = jnp.minimum(donor - 1, bound - sink)
    passed = jax.random.randint(jax.random.fold_in(key, 1), (pairs,), 0, 1 << 20) % (slack + 1)
    tallies = tallies.at[1:1 + 2 * pairs:2].set(donor - passed).at[2:2 + 2 * pairs:2].set(sink + passed)
    return tallies[jax.random.permutation(jax.random.fold_in(key, 2), amount)]


def gaussian(key, dims, spread, bound, split=(), kind=jnp.bfloat16):
    entries = jax.random.normal(key, dims, jnp.float32) * spread
    if len(split) > 0:
        entries = block_levels(key, dims, split, -0.22, 0.18) * entries
    return jnp.clip(entries, min=-bound, max=bound).astype(kind)


def setup_inputs(seed: int = 0) -> dict:
    streams_of = jax.random.split(jax.random.key(seed), 10)
    return {
        "tokens": gaussian(streams_of[0], (BLOCKS, BLK, D), 1.0, 6.0, ((0, 32),)),
        "segment_ids": jax.vmap(lambda own: jnp.searchsorted(jnp.cumsum(ragged_sizes(own, DOCS, BLK, BLK // 2, 2)), jnp.arange(BLK), side="right"))(jax.random.split(streams_of[1], BLOCKS)).reshape((BLOCKS, BLK)).astype(jnp.int32),
        "attn_gain": jnp.clip(1.0 + 0.1 * jax.random.normal(streams_of[2], (D,), jnp.float32), 0.5, 1.5).astype(jnp.bfloat16),
        "qkv_weight": gaussian(streams_of[3], (D, 3 * D), D ** -0.5, 0.21875, ((0, 4),)),
        "attn_out_weight": gaussian(streams_of[4], (D, D), (max(D // 64, 1)) ** -0.5, 1.75, ((0, 4),)),
        "mlp_gain": jnp.clip(1.0 + 0.1 * jax.random.normal(streams_of[5], (D,), jnp.float32), 0.5, 1.5).astype(jnp.bfloat16),
        "in_weight": gaussian(streams_of[6], (D, 2 * FF), D ** -0.5, 0.21875, ((0, 4),)),
        "out_weight": gaussian(streams_of[7], (FF, D), (FF // 2) ** -0.5, 0.25, ((0, 4),)),
        "cotangent": gaussian(streams_of[8], (BLOCKS, BLK, D), 1.0, 6.0, ((0, 32),)),
    }


highest = lax.Precision.HIGHEST
rope_base = 160000.0
epsilon = 1e-05

@jax.custom_vjp
def low(v):
    return lax.optimization_barrier(v.astype(jnp.bfloat16)).astype(jnp.float32)

@jax.custom_vjp
def low_back(v):
    return v

def low_keep(v):
    return (low(v), None)

def low_pass(kept, grad):
    return (grad,)

def back_keep(v):
    return (v, None)

def back_low(kept, grad):
    return (low(grad),)
low.defvjp(low_keep, low_pass)
low_back.defvjp(back_keep, back_low)

def both_ways(values_in):
    return low(low_back(values_in))

def layer_norm(activations, gain_vector):
    mean_row = lax.optimization_barrier(jnp.mean(activations, axis=-1, keepdims=True))
    centred = activations - mean_row
    variance = lax.optimization_barrier(jnp.mean(centred * centred, axis=-1, keepdims=True))
    return centred * lax.rsqrt(variance + epsilon) * gain_vector

def rope_tables(segment_row):
    length = segment_row.shape[0]
    positions_all = jnp.arange(length, dtype=jnp.int32)
    changes = jnp.concatenate([jnp.ones((1,), bool), segment_row[1:] != segment_row[:-1]])
    starts_at = lax.cummax(jnp.where(changes, positions_all, 0).astype(jnp.int32))
    position = (positions_all - starts_at).astype(jnp.float32)
    frequency = rope_base ** (-jnp.arange(0, HD, 2, dtype=jnp.float32) / HD)
    angles = position[:, None] * frequency[None, :]
    cosine = jnp.concatenate([jnp.cos(angles), jnp.cos(angles)], axis=-1)
    sine_table = jnp.concatenate([jnp.sin(angles), jnp.sin(angles)], axis=-1)
    return (cosine, sine_table)

def rotate(vector, cosine, sine_table):
    half_size = vector.shape[-1] // 2
    turned = jnp.concatenate([-vector[..., half_size:], vector[..., :half_size]], axis=-1)
    return vector * cosine[:, None, :] + turned * sine_table[:, None, :]

def attend(pair):
    projected, segment_row = pair
    length = projected.shape[0]
    cosine, sine_table = rope_tables(segment_row)
    queries = low(rotate(projected[:, :D].reshape(length, H, HD), cosine, sine_table))
    key_rows = low(rotate(projected[:, D:2 * D].reshape(length, H, HD), cosine, sine_table))
    value_rows = low(projected[:, 2 * D:].reshape(length, H, HD))
    scores = jnp.einsum('qhd,khd->hqk', queries, key_rows, precision=highest) * HD ** (-0.5)
    scores = low_back(scores)
    same_doc = segment_row[:, None] == segment_row[None, :]
    masked = jnp.where(same_doc[None], scores, -1000000000.0)
    probs = low(jax.nn.softmax(masked, axis=-1))
    attended = jnp.einsum('hqk,khd->qhd', probs, value_rows, precision=highest)
    return attended.reshape(length, D)

def forward(tokens, attn_gain, qkv_weight, attn_out_weight, mlp_gain, in_weight, out_weight, segment_ids):
    flat_rows = tokens.reshape(-1, D)
    normed_one = low(layer_norm(flat_rows, attn_gain))
    projected = low_back(jnp.dot(normed_one, qkv_weight, precision=highest))
    projected = projected.reshape(BLOCKS, BLK, 3 * D)
    attended = lax.map(jax.checkpoint(attend), (projected, segment_ids))
    attended = both_ways(attended.reshape(-1, D))
    middle = flat_rows + low_back(jnp.dot(attended, attn_out_weight, precision=highest))
    normed_two = low(layer_norm(middle, mlp_gain))
    gate_up = low_back(jnp.dot(normed_two, in_weight, precision=highest))
    hidden = both_ways(jax.nn.gelu(gate_up[:, :FF], approximate=False) * gate_up[:, FF:])
    result = middle + low_back(jnp.dot(hidden, out_weight, precision=highest))
    return result.reshape(tokens.shape)

def reference(tokens, segment_ids, attn_gain, qkv_weight, attn_out_weight, mlp_gain, in_weight, out_weight, cotangent):

    def closed(tok_f, gain_one, qkv_f, attn_f, gain_two, in_f, out_f):
        return forward(tok_f, gain_one, qkv_f, attn_f, gain_two, in_f, out_f, segment_ids)
    result, pullback = jax.vjp(closed, tokens.astype(jnp.float32), attn_gain.astype(jnp.float32), qkv_weight.astype(jnp.float32), attn_out_weight.astype(jnp.float32), mlp_gain.astype(jnp.float32), in_weight.astype(jnp.float32), out_weight.astype(jnp.float32))
    grads = pullback(cotangent.astype(jnp.float32))
    return (result.astype(jnp.bfloat16), grads[0], grads[1], grads[2], grads[3], grads[4], grads[5], grads[6])
```

```python
import functools
import jax
import jax.numpy as jnp
from jax import lax
from jax.experimental import pallas as pl
from jax.experimental.pallas import tpu as pltpu
from jax.sharding import PartitionSpec as P

HD = 64


rope_base = 160000.0
epsilon = 1e-05


def layer_norm(activations, gain_vector):
    mean_row = jnp.mean(activations, axis=-1, keepdims=True)
    centred = activations - mean_row
    variance = jnp.mean(centred * centred, axis=-1, keepdims=True)
    return centred * lax.rsqrt(variance + epsilon) * gain_vector


def rope_tables(segment_row):
    length = segment_row.shape[0]
    positions_all = jnp.arange(length, dtype=jnp.int32)
    changes = jnp.concatenate([jnp.ones((1,), bool), segment_row[1:] != segment_row[:-1]])
    starts_at = lax.cummax(jnp.where(changes, positions_all, 0))
    position = (positions_all - starts_at).astype(jnp.float32)
    frequency = rope_base ** (-jnp.arange(0, HD, 2, dtype=jnp.float32) / HD)
    angles = position[:, None] * frequency[None, :]
    cosine = jnp.concatenate([jnp.cos(angles), jnp.cos(angles)], axis=-1)
    sine_table = jnp.concatenate([jnp.sin(angles), jnp.sin(angles)], axis=-1)
    return (cosine, sine_table)


def rotate(vector, cosine, sine_table):
    half_size = vector.shape[-1] // 2
    turned = jnp.concatenate([-vector[..., half_size:], vector[..., :half_size]], axis=-1)
    return vector * cosine[:, None, :] + turned * sine_table[:, None, :]


def unrotate(gradient, cosine, sine_table):
    half_size = gradient.shape[-1] // 2
    sined = gradient * sine_table[:, None, :]
    turned = jnp.concatenate([sined[..., half_size:], -sined[..., :half_size]], axis=-1)
    return gradient * cosine[:, None, :] + turned


def gated_gelu(gate_up):
    hidden_width = gate_up.shape[1] // 2
    return jax.nn.gelu(gate_up[:, :hidden_width], approximate=False) * gate_up[:, hidden_width:]


def pick(array, index, axis=0):
    return lax.dynamic_index_in_dim(array, index, axis, keepdims=False)


class Place:
    def __init__(self, shards, reps):
        self.shards, self.planes = shards, reps // 2
        self.shard = lax.axis_index("shard")
        rep = lax.axis_index("rep")
        self.plane, self.core = rep // 2, rep % 2
        self.reps = reps

    def from_core(self, array):
        return lax.ppermute(array, "rep", [(r, r ^ 1) for r in range(self.reps)])

    def from_plane(self, array, other):
        return lax.ppermute(array, "rep", [(r, r ^ (2 * other)) for r in range(self.reps)])

    def from_shard(self, array, ahead):
        return lax.ppermute(
            array, "shard", [((s + ahead) % self.shards, s) for s in range(self.shards)]
        )

    def to_shard(self, array, ahead):
        return lax.ppermute(
            array, "shard", [(s, (s + ahead) % self.shards) for s in range(self.shards)]
        )

    def plane_gather(self, array):
        found = {0: array}
        half = array.shape[-2] // 2
        for j in range(1, self.planes):
            low = j & -j
            if low == j:
                found[j] = self.from_plane(array, j)
            else:
                first = self.from_plane(found[low][..., :half, :], j ^ low)
                second = self.from_plane(found[j ^ low][..., half:, :], low)
                found[j] = jnp.concatenate([first, second], axis=-2)
        return [found[j] for j in range(self.planes)]

    def plane_swap(self, array):
        rows, columns = array.shape
        parts = array.reshape(rows, self.planes, columns // self.planes).transpose(1, 0, 2)
        found = [pick(parts, self.plane)]
        for j in range(1, self.planes):
            found.append(self.from_plane(pick(parts, self.plane ^ j), j))
        return jnp.concatenate(found, axis=0)


def join_kernel(shards, planes, where_ref, own_ref, *refs):
    mine, other, out_ref = refs[:planes], refs[planes : 2 * planes], refs[2 * planes]
    shard, plane, core = where_ref[0], where_ref[1], where_ref[2]
    half = out_ref.shape[-1] // 2
    out_ref[shard] = own_ref[...]
    for j in range(planes):
        for d in range(1, shards):
            row = lax.rem(shard + d, shards)
            column = lax.bitwise_xor(plane, j)
            first = jnp.where(core == 0, mine[j][d - 1], other[j][d - 1])
            second = jnp.where(core == 0, other[j][d - 1], mine[j][d - 1])
            out_ref[row, column, :, :half] = first
            out_ref[row, column, :, half:] = second


def gather_weight(place, where, weight):
    rows, columns = weight.shape
    height = rows // place.planes
    blocks = weight.reshape(place.planes, height, columns)
    piece = pick(blocks, place.plane)
    piece = jnp.where(place.core == 0, piece[:, : columns // 2], piece[:, columns // 2 :])
    column = jnp.stack([place.from_shard(piece, d) for d in range(1, place.shards)])
    mine = place.plane_gather(column)
    other = [place.from_core(block) for block in mine]
    whole = pl.pallas_call(
        functools.partial(join_kernel, place.shards, place.planes),
        out_shape=jax.ShapeDtypeStruct(
            (place.shards, place.planes, height, columns), weight.dtype
        ),
        in_specs=[pl.BlockSpec(memory_space=pltpu.SMEM)]
        + [pl.BlockSpec(memory_space=pltpu.VMEM)] * (1 + 2 * place.planes),
        out_specs=pl.BlockSpec(memory_space=pltpu.VMEM),
        compiler_params=pltpu.CompilerParams(vmem_limit_bytes=24 * 2**20),
        cost_estimate=pl.CostEstimate(
            flops=0, bytes_accessed=4 * weight.size * place.shards, transcendentals=0
        ),
    )(where, blocks, *mine, *other)
    return whole.reshape(place.shards * rows, columns)


def gather_gains(place, gains):
    whole = jnp.zeros((place.shards,) + gains.shape, gains.dtype)
    for d in range(place.shards):
        block = place.from_shard(gains, d) if d else gains
        whole = lax.dynamic_update_index_in_dim(
            whole, block, (place.shard + d) % place.shards, 0
        )
    return whole.transpose(1, 0, 2).reshape(gains.shape[0], -1)


def spread_kernel(planes, where_ref, mine_ref, other_ref, out_ref, scratch):
    plane, core = where_ref[1], where_ref[2]
    for j in range(planes):
        column = lax.bitwise_xor(plane, j)
        scratch[column, core] = mine_ref[j].astype(jnp.float32)
        scratch[column, 1 - core] = other_ref[j].astype(jnp.float32)
    height, width = scratch.shape[2:]
    for column in range(planes):
        for half in range(2):
            out_ref[
                half * height : (half + 1) * height, column * width : (column + 1) * width
            ] = scratch[column, half]


def reduce_weight(place, where, left, right):
    grad = lax.dot_general(
        left, right, (((0,), (0,)), ((), ())), preferred_element_type=jnp.float32
    )
    rows, width = grad.shape
    height = rows // place.shards // 2
    grad = grad.reshape(place.shards, 2, height, width)
    other = place.from_core(pick(grad, 1 - place.core, 1).astype(jnp.bfloat16))
    grad = (pick(grad, place.core, 1) + other.astype(jnp.float32)).astype(jnp.bfloat16)
    total = pick(grad, place.shard).astype(jnp.float32)
    for d in range(1, place.shards):
        sent = pick(grad, (place.shard + d) % place.shards)
        total = total + place.to_shard(sent, d).astype(jnp.float32)
    mine = jnp.stack(place.plane_gather(total.astype(jnp.bfloat16)))
    other = place.from_core(mine)
    return pl.pallas_call(
        functools.partial(spread_kernel, place.planes),
        out_shape=jax.ShapeDtypeStruct((2 * height, place.planes * width), jnp.float32),
        in_specs=[pl.BlockSpec(memory_space=pltpu.SMEM)]
        + [pl.BlockSpec(memory_space=pltpu.VMEM)] * 2,
        out_specs=pl.BlockSpec(memory_space=pltpu.VMEM),
        scratch_shapes=[pltpu.VMEM((place.planes, 2, height, width), jnp.float32)],
        compiler_params=pltpu.CompilerParams(vmem_limit_bytes=24 * 2**20),
    )(where, mine, other)


def reduce_gain(place, grad):
    grad = grad + place.from_core(grad)
    j = 1
    while j < place.planes:
        grad = grad + place.from_plane(grad, j)
        j *= 2
    blocks = grad.reshape(place.shards, -1)
    total = pick(blocks, place.shard)
    for d in range(1, place.shards):
        total = total + place.to_shard(pick(blocks, (place.shard + d) % place.shards), d)
    return total


def body(
    shards,
    reps,
    tokens,
    segment_ids,
    attn_gain,
    qkv_weight,
    attn_out_weight,
    mlp_gain,
    in_weight,
    out_weight,
    cotangent,
):
    model_width = qkv_weight.shape[1] // 3
    head_count = model_width // HD
    block_len = tokens.shape[1]
    score_scale = HD ** (-0.5)
    inputs = tokens[0].astype(jnp.float32)
    segments = segment_ids[0]
    cosine, sine_table = rope_tables(segments)
    same_doc = segments[:, None] == segments[None, :]
    place = Place(shards, reps)
    where = jnp.stack([place.shard, place.plane, place.core]).astype(jnp.int32)
    gain_attn, gain_mlp = gather_gains(place, jnp.stack([attn_gain, mlp_gain]))
    weight_qkv = gather_weight(place, where, qkv_weight)
    weight_attn = gather_weight(place, where, attn_out_weight)
    weight_in = gather_weight(place, where, in_weight)
    weight_out = gather_weight(place, where, out_weight)
    normed_one, norm_one_back = jax.vjp(layer_norm, inputs, gain_attn.astype(jnp.float32))
    normed_one_low = normed_one.astype(jnp.bfloat16)
    projected = jnp.dot(normed_one_low, weight_qkv, preferred_element_type=jnp.float32)
    queries = rotate(
        projected[:, :model_width].reshape(block_len, head_count, HD), cosine, sine_table
    ).astype(jnp.bfloat16)
    key_rows = rotate(
        projected[:, model_width : 2 * model_width].reshape(block_len, head_count, HD),
        cosine,
        sine_table,
    ).astype(jnp.bfloat16)
    value_rows = (
        projected[:, 2 * model_width :].reshape(block_len, head_count, HD).astype(jnp.bfloat16)
    )

    def masked_scores():
        raw_scores = (
            jnp.einsum("qhd,khd->hqk", queries, key_rows, preferred_element_type=jnp.float32)
            * score_scale
        )
        return jnp.where(same_doc[None], raw_scores, -1000000000.0)

    masked = masked_scores()
    row_max = jnp.max(masked, axis=-1, keepdims=True)
    exponent = jnp.exp(masked - row_max)
    row_total = jnp.sum(exponent, axis=-1, keepdims=True)
    log_total = row_max + jnp.log(row_total)
    probs_low = (exponent / row_total).astype(jnp.bfloat16)
    attended = jnp.einsum("hqk,khd->qhd", probs_low, value_rows, preferred_element_type=jnp.float32)
    attended_low = attended.reshape(block_len, model_width).astype(jnp.bfloat16)
    middle = inputs + jnp.dot(attended_low, weight_attn, preferred_element_type=jnp.float32)
    normed_two, norm_two_back = jax.vjp(layer_norm, middle, gain_mlp.astype(jnp.float32))
    normed_two_low = normed_two.astype(jnp.bfloat16)
    gate_up = jnp.dot(normed_two_low, weight_in, preferred_element_type=jnp.float32)
    hidden, gelu_back = jax.vjp(gated_gelu, gate_up)
    hidden_low = hidden.astype(jnp.bfloat16)
    result = middle + jnp.dot(hidden_low, weight_out, preferred_element_type=jnp.float32)
    upstream = cotangent[0].astype(jnp.float32)
    upstream_low = upstream.astype(jnp.bfloat16)
    out_weight_g = reduce_weight(
        place,
        where,
        jnp.concatenate(place.plane_gather(hidden_low)),
        place.plane_swap(upstream_low),
    )
    grad_hidden = jnp.einsum(
        "rd,fd->rf", upstream_low, weight_out, preferred_element_type=jnp.float32
    )
    grad_hidden = lax.optimization_barrier(grad_hidden.astype(jnp.bfloat16)).astype(jnp.float32)
    grad_gate_up = gelu_back(grad_hidden)[0].astype(jnp.bfloat16)
    in_weight_g = reduce_weight(
        place,
        where,
        jnp.concatenate(place.plane_gather(normed_two_low)),
        place.plane_swap(grad_gate_up),
    )
    grad_normed_two = jnp.einsum(
        "rk,dk->rd", grad_gate_up, weight_in, preferred_element_type=jnp.float32
    )
    grad_middle_part, grad_gain_mlp = norm_two_back(grad_normed_two)
    grad_middle = upstream + grad_middle_part
    mlp_gain_g = reduce_gain(place, grad_gain_mlp)
    middle_low = grad_middle.astype(jnp.bfloat16)
    attn_out_g = reduce_weight(
        place,
        where,
        jnp.concatenate(place.plane_gather(attended_low)),
        place.plane_swap(middle_low),
    )
    grad_attended = jnp.einsum(
        "rd,cd->rc", middle_low, weight_attn, preferred_element_type=jnp.float32
    )
    grad_attended = grad_attended.astype(jnp.bfloat16).reshape(block_len, head_count, HD)
    grad_probs = jnp.einsum(
        "qhd,khd->hqk", grad_attended, value_rows, preferred_element_type=jnp.float32
    )
    probs_again = jnp.exp(masked_scores() - log_total)
    weighted = jnp.sum(probs_again * grad_probs, axis=-1, keepdims=True)
    grad_scores = (probs_again * (grad_probs - weighted)).astype(jnp.bfloat16)
    grad_queries = (
        jnp.einsum("hqk,khd->qhd", grad_scores, key_rows, preferred_element_type=jnp.float32)
        * score_scale
    )
    grad_keys = (
        jnp.einsum("hqk,qhd->khd", grad_scores, queries, preferred_element_type=jnp.float32)
        * score_scale
    )
    grad_values = jnp.einsum(
        "hqk,qhd->khd", probs_low, grad_attended, preferred_element_type=jnp.float32
    )
    grad_projected = jnp.concatenate(
        [
            unrotate(grad_queries, cosine, sine_table).reshape(block_len, model_width),
            unrotate(grad_keys, cosine, sine_table).reshape(block_len, model_width),
            grad_values.reshape(block_len, model_width),
        ],
        axis=-1,
    ).astype(jnp.bfloat16)
    qkv_weight_g = reduce_weight(
        place,
        where,
        jnp.concatenate(place.plane_gather(normed_one_low)),
        place.plane_swap(grad_projected),
    )
    grad_normed_one = jnp.einsum(
        "rk,dk->rd", grad_projected, weight_qkv, preferred_element_type=jnp.float32
    )
    grad_input_part, grad_gain_attn = norm_one_back(grad_normed_one)
    grad_inputs = grad_middle + grad_input_part
    attn_gain_g = reduce_gain(place, grad_gain_attn)
    return (
        result.astype(jnp.bfloat16)[None],
        grad_inputs[None],
        attn_gain_g,
        qkv_weight_g,
        attn_out_g,
        mlp_gain_g,
        in_weight_g,
        out_weight_g,
    )


def solution(mesh):
    return jax.shard_map(
        functools.partial(body, mesh.shape["shard"], mesh.shape["rep"]),
        mesh=mesh,
        in_specs=(
            P(("rep", "shard"), None, None),
            P(("rep", "shard"), None),
            P("shard"),
            P("shard", None),
            P("shard", None),
            P("shard"),
            P("shard", None),
            P("shard", None),
            P(("rep", "shard"), None, None),
        ),
        out_specs=(
            P(("rep", "shard"), None, None),
            P(("rep", "shard"), None, None),
            P("shard"),
            P("shard", None),
            P("shard", None),
            P("shard"),
            P("shard", None),
            P("shard", None),
        ),
        check_vma=False,
    )
```

```python
import functools
import jax
import jax.numpy as jnp
from jax import lax
from jax.experimental import pallas as pl
from jax.experimental.pallas import tpu as pltpu
from jax.sharding import PartitionSpec as P

HD = 64


rope_base = 160000.0
epsilon = 1e-05


def layer_norm(activations, gain_vector):
    mean_row = jnp.mean(activations, axis=-1, keepdims=True)
    centred = activations - mean_row
    variance = jnp.mean(centred * centred, axis=-1, keepdims=True)
    return centred * lax.rsqrt(variance + epsilon) * gain_vector


def rope_tables(segment_row):
    length = segment_row.shape[0]
    positions_all = jnp.arange(length, dtype=jnp.int32)
    changes = jnp.concatenate([jnp.ones((1,), bool), segment_row[1:] != segment_row[:-1]])
    starts_at = lax.cummax(jnp.where(changes, positions_all, 0))
    position = (positions_all - starts_at).astype(jnp.float32)
    frequency = rope_base ** (-jnp.arange(0, HD, 2, dtype=jnp.float32) / HD)
    angles = position[:, None] * frequency[None, :]
    cosine = jnp.concatenate([jnp.cos(angles), jnp.cos(angles)], axis=-1)
    sine_table = jnp.concatenate([jnp.sin(angles), jnp.sin(angles)], axis=-1)
    return (cosine, sine_table)


def rotate(vector, cosine, sine_table):
    half_size = vector.shape[-1] // 2
    turned = jnp.concatenate([-vector[..., half_size:], vector[..., :half_size]], axis=-1)
    return vector * cosine[:, None, :] + turned * sine_table[:, None, :]


def unrotate(gradient, cosine, sine_table):
    half_size = gradient.shape[-1] // 2
    sined = gradient * sine_table[:, None, :]
    turned = jnp.concatenate([sined[..., half_size:], -sined[..., :half_size]], axis=-1)
    return gradient * cosine[:, None, :] + turned


def gated_gelu(gate_up):
    hidden_width = gate_up.shape[1] // 2
    return jax.nn.gelu(gate_up[:, :hidden_width], approximate=False) * gate_up[:, hidden_width:]


def pick(array, index, axis=0):
    return lax.dynamic_index_in_dim(array, index, axis, keepdims=False)


class Place:
    def __init__(self, shards, reps):
        self.shards, self.planes = shards, reps // 2
        self.bits = self.planes.bit_length() - 1
        if self.planes != 1 << self.bits or self.bits % 2 or shards % 2:
            raise ValueError("mesh sizes")
        pairs = range(0, self.bits, 2)
        self.orders = ([i + k for i in pairs for k in (0, 1)], [i + k for i in pairs for k in (1, 0)])
        rep = lax.axis_index("rep")
        self.shard, self.plane, self.core = lax.axis_index("shard"), rep // 2, rep % 2
        self.first = self.core == 0

    def permute(self, array, source):
        flat = lambda s, p, c: (2 * p + c) * self.shards + s
        pairs = []
        for p in range(self.planes):
            for c in range(2):
                for s in range(self.shards):
                    from_s, from_p = source(s, p, c)
                    pairs.append((flat(from_s % self.shards, from_p, c), flat(s, p, c)))
        return lax.ppermute(array, ("rep", "shard"), pairs)

    def from_core(self, array):
        return lax.ppermute(array, "rep", [(r, r ^ 1) for r in range(2 * self.planes)])

    def from_bit(self, array, step):
        return self.permute(array, lambda s, p, c: (s, p ^ (1 << self.orders[c][step])))

    def bit(self, step):
        at = jnp.where(self.first, self.orders[0][step], self.orders[1][step])
        return (self.plane >> at) & 1

    def both(self, mine, other):
        return jnp.where(self.first, mine, other), jnp.where(self.first, other, mine)


def join_kernel(shards, planes, chunks, where_ref, *refs):
    count = len(chunks)
    shard, plane, core = where_ref[0], where_ref[1], where_ref[2]
    owns, outs = refs[:count], refs[count + 5 :]
    column, mine, other, mine_far, other_far = refs[count : count + 5]
    inner, total, width = column.shape[1], column.shape[2], column.shape[-1]
    half = total // 2
    for own, out in zip(owns, outs):
        out[shard] = own[...]
    for d in range(shards - 1):
        row = lax.rem(shard + d + 1, shards)
        for i in range(inner):
            at = 0
            for out, chunk in zip(outs, chunks):
                for k in range(chunk):
                    lanes = slice(k * width, (k + 1) * width)
                    a, b = mine[d, i, at], other[d, i, at]
                    if at < half:
                        far = jnp.where(core == 0, mine_far[d, i, at], other_far[d, i, at])
                    else:
                        far = jnp.where(
                            core == 0, other_far[d, i, at - half], mine_far[d, i, at - half]
                        )
                    out[row, plane ^ i, :, lanes] = column[d, i, at]
                    out[row, plane ^ (inner + i), :, lanes] = jnp.where(core == 0, a, b)
                    out[row, plane ^ (2 * inner + i), :, lanes] = jnp.where(core == 0, b, a)
                    out[row, plane ^ (3 * inner + i), :, lanes] = far
                    at += 1


def gather_weights(place, where, weights, width):
    height = weights[0].shape[0] // place.planes
    chunks = [weight.shape[1] // width for weight in weights]
    blocks = [weight.reshape(place.planes, height, weight.shape[1]) for weight in weights]
    piece = jnp.concatenate(
        [
            pick(block, place.plane).reshape(height, chunk, width).transpose(1, 0, 2)
            for block, chunk in zip(blocks, chunks)
        ]
    )
    half = sum(chunks) // 2
    middle = place.shards // 2
    found = {}
    for d in range(1, middle):
        mine = place.permute(piece, lambda s, p, c: (s + d if c == 0 else s - d, p))
        found[d], found[place.shards - d] = place.both(mine, place.from_core(mine))
    part = jnp.where(place.first, piece[:half], piece[half:])
    mine = place.permute(part, lambda s, p, c: (s + middle, p))
    found[middle] = jnp.concatenate(place.both(mine, place.from_core(mine)))
    column = jnp.stack([found[d] for d in range(1, place.shards)])[:, None]
    for level in range(0, place.bits, 2):
        mine = place.from_bit(column, level)
        other = place.from_core(mine)
        part = jnp.where(place.first, mine[:, :, :half], mine[:, :, half:])
        mine_far = place.from_bit(part, level + 1)
        other_far = place.from_core(mine_far)
        if level + 2 < place.bits:
            far = jnp.concatenate(place.both(mine_far, other_far), axis=2)
            column = jnp.concatenate([column, *place.both(mine, other), far], axis=1)
    wholes = pl.pallas_call(
        functools.partial(join_kernel, place.shards, place.planes, chunks),
        out_shape=[
            jax.ShapeDtypeStruct((place.shards,) + block.shape, block.dtype) for block in blocks
        ],
        in_specs=[pl.BlockSpec(memory_space=pltpu.SMEM)]
        + [pl.BlockSpec(memory_space=pltpu.VMEM)] * (5 + len(blocks)),
        out_specs=[pl.BlockSpec(memory_space=pltpu.VMEM)] * len(blocks),
        compiler_params=pltpu.CompilerParams(vmem_limit_bytes=32 * 2**20),
        cost_estimate=pl.CostEstimate(
            flops=0,
            bytes_accessed=4 * place.shards * sum(block.size for block in blocks),
            transcendentals=0,
        ),
    )(where, *blocks, column, mine, other, mine_far, other_far)
    return [
        whole.reshape(place.shards * weight.shape[0], weight.shape[1])
        for whole, weight in zip(wholes, weights)
    ]


def gather_gains(place, gains):
    whole = jnp.zeros((place.shards,) + gains.shape, gains.dtype)
    for d in range(place.shards):
        block = place.permute(gains, lambda s, p, c: (s + d, p)) if d else gains
        whole = lax.dynamic_update_index_in_dim(
            whole, block, (place.shard + d) % place.shards, 0
        )
    return whole.transpose(1, 0, 2).reshape(gains.shape[0], -1)


def share_left(place, left):
    tokens, columns = left.shape
    parts = left.reshape(tokens, place.shards, 2, -1).transpose(2, 0, 1, 3)
    parts = parts.reshape(2, tokens, columns // 2)
    return jnp.concatenate([parts, place.from_core(parts)], axis=1)


def share_right(place, right):
    half = right.shape[1] // 2
    kept, sent = place.both(right[:, :half], right[:, half:])
    return jnp.concatenate([kept, place.from_core(sent)])


def partial_grads(place, lefts, rights):
    bit = place.bit(0)
    kept = [pick(left, bit) for left in lefts] + rights
    sent = [pick(left, 1 - bit) for left in lefts] + rights
    order = sorted(range(len(kept)), key=lambda i: kept[i].shape[1] % 128)
    got = place.from_bit(jnp.concatenate([sent[i] for i in order], axis=1), 0)
    arrived, at = {}, 0
    for i in order:
        arrived[i] = got[:, at : at + kept[i].shape[1]]
        at += kept[i].shape[1]
    count = len(lefts)
    product = lambda a, b: lax.dot_general(
        a, b, (((0,), (0,)), ((), ())), preferred_element_type=jnp.float32
    )
    return [
        product(kept[i], kept[count + i]) + product(arrived[i], arrived[count + i])
        for i in range(count)
    ]


def spread_kernel(orders, bits, planes, heights, chunks, where_ref, mine_ref, other_ref, *outs):
    plane, core = where_ref[1], where_ref[2]
    width = mine_ref.shape[-1]
    starts = []
    for order in orders:
        start = 0
        for step, at in enumerate(order):
            start = start + (((plane >> at) & 1) << (bits - 1 - step))
        starts.append(start)
    for p in range(planes):
        at = 0
        for out, height, chunk in zip(outs, heights, chunks):
            for k in range(chunk):
                rows = slice(at, at + height)
                a = mine_ref[p, rows].astype(jnp.float32)
                b = other_ref[p, rows].astype(jnp.float32)
                lanes = slice(k * width, (k + 1) * width)
                far = slice((chunk + k) * width, (chunk + k + 1) * width)
                out[p ^ starts[0], :, lanes] = jnp.where(core == 0, a, b)
                out[p ^ starts[1], :, far] = jnp.where(core == 0, b, a)
                at += height


def finish_grads(place, where, grads, width):
    chunks = [grad.shape[1] // width for grad in grads]
    heights = [grad.shape[0] // place.shards for grad in grads]
    packed = jnp.concatenate(
        [
            grad.reshape(place.shards, place.planes // 2, -1, chunk, width)
            .transpose(0, 1, 3, 2, 4)
            .reshape(place.shards, place.planes // 2, -1, width)
            for grad, chunk in zip(grads, chunks)
        ],
        axis=2,
    )
    heights = [height * 2 // place.planes for height in heights]
    for step in range(1, place.bits):
        parts = packed.reshape(place.shards, 2, -1, packed.shape[2], width)
        sent = pick(parts, 1 - place.bit(step), 1).astype(jnp.bfloat16)
        got = place.from_bit(sent, step)
        packed = pick(parts, place.bit(step), 1) + got.astype(jnp.float32)
    packed = packed.reshape(place.shards, -1, width)
    low = packed.astype(jnp.bfloat16)
    total = pick(packed, place.shard)
    for d in range(1, place.shards):
        sent = pick(low, (place.shard + d) % place.shards)
        total = total + place.permute(sent, lambda s, p, c: (s - d, p)).astype(jnp.float32)
    mine = total.astype(jnp.bfloat16)[None]
    for step in reversed(range(place.bits)):
        mine = jnp.concatenate([mine, place.from_bit(mine, step)])
    other = place.from_core(mine)
    outs = pl.pallas_call(
        functools.partial(
            spread_kernel, place.orders, place.bits, place.planes, heights, chunks
        ),
        out_shape=[
            jax.ShapeDtypeStruct((place.planes, height, 2 * chunk * width), jnp.float32)
            for height, chunk in zip(heights, chunks)
        ],
        in_specs=[pl.BlockSpec(memory_space=pltpu.SMEM)]
        + [pl.BlockSpec(memory_space=pltpu.VMEM)] * 2,
        out_specs=[pl.BlockSpec(memory_space=pltpu.VMEM)] * len(grads),
        compiler_params=pltpu.CompilerParams(vmem_limit_bytes=32 * 2**20),
    )(where, mine, other)
    return [out.reshape(-1, out.shape[2]) for out in outs]


def reduce_gains(place, grad):
    grad = grad + place.from_core(grad)
    for step in range(place.bits):
        grad = grad + place.from_bit(grad, step)
    blocks = grad.reshape(grad.shape[0], place.shards, -1)
    total = pick(blocks, place.shard, 1)
    for d in range(1, place.shards):
        sent = pick(blocks, (place.shard + d) % place.shards, 1)
        total = total + place.permute(sent, lambda s, p, c: (s - d, p))
    return total


def body(
    shards,
    reps,
    tokens,
    segment_ids,
    attn_gain,
    qkv_weight,
    attn_out_weight,
    mlp_gain,
    in_weight,
    out_weight,
    cotangent,
):
    model_width = qkv_weight.shape[1] // 3
    head_count = model_width // HD
    block_len = tokens.shape[1]
    score_scale = HD ** (-0.5)
    inputs = tokens[0].astype(jnp.float32)
    segments = segment_ids[0]
    cosine, sine_table = rope_tables(segments)
    same_doc = segments[:, None] == segments[None, :]
    place = Place(shards, reps)
    where = jnp.stack([place.shard, place.plane, place.core]).astype(jnp.int32)
    width = model_width // 2
    gain_attn, gain_mlp = gather_gains(place, jnp.stack([attn_gain, mlp_gain]))
    (weight_qkv,) = gather_weights(place, where, [qkv_weight], width)
    weight_attn, weight_in = gather_weights(place, where, [attn_out_weight, in_weight], width)
    (weight_out,) = gather_weights(place, where, [out_weight], width)
    normed_one, norm_one_back = jax.vjp(layer_norm, inputs, gain_attn.astype(jnp.float32))
    normed_one_low = normed_one.astype(jnp.bfloat16)
    projected = jnp.dot(normed_one_low, weight_qkv, preferred_element_type=jnp.float32)
    queries = rotate(
        projected[:, :model_width].reshape(block_len, head_count, HD), cosine, sine_table
    ).astype(jnp.bfloat16)
    key_rows = rotate(
        projected[:, model_width : 2 * model_width].reshape(block_len, head_count, HD),
        cosine,
        sine_table,
    ).astype(jnp.bfloat16)
    value_rows = (
        projected[:, 2 * model_width :].reshape(block_len, head_count, HD).astype(jnp.bfloat16)
    )

    def masked_scores():
        raw_scores = (
            jnp.einsum("qhd,khd->hqk", queries, key_rows, preferred_element_type=jnp.float32)
            * score_scale
        )
        return jnp.where(same_doc[None], raw_scores, -1000000000.0)

    masked = masked_scores()
    row_max = jnp.max(masked, axis=-1, keepdims=True)
    exponent = jnp.exp(masked - row_max)
    row_total = jnp.sum(exponent, axis=-1, keepdims=True)
    log_total = row_max + jnp.log(row_total)
    probs_low = (exponent / row_total).astype(jnp.bfloat16)
    attended = jnp.einsum("hqk,khd->qhd", probs_low, value_rows, preferred_element_type=jnp.float32)
    attended_low = attended.reshape(block_len, model_width).astype(jnp.bfloat16)
    middle = inputs + jnp.dot(attended_low, weight_attn, preferred_element_type=jnp.float32)
    normed_two, norm_two_back = jax.vjp(layer_norm, middle, gain_mlp.astype(jnp.float32))
    normed_two_low = normed_two.astype(jnp.bfloat16)
    gate_up = jnp.dot(normed_two_low, weight_in, preferred_element_type=jnp.float32)
    hidden, gelu_back = jax.vjp(gated_gelu, gate_up)
    hidden_low = hidden.astype(jnp.bfloat16)
    result = middle + jnp.dot(hidden_low, weight_out, preferred_element_type=jnp.float32)
    upstream = cotangent[0].astype(jnp.float32)
    upstream_low = upstream.astype(jnp.bfloat16)
    grad_hidden = jnp.einsum(
        "rd,fd->rf", upstream_low, weight_out, preferred_element_type=jnp.float32
    )
    grad_hidden = lax.optimization_barrier(grad_hidden.astype(jnp.bfloat16)).astype(jnp.float32)
    grad_gate_up = gelu_back(grad_hidden)[0].astype(jnp.bfloat16)
    in_part, out_part = partial_grads(
        place,
        [share_left(place, normed_two_low), share_left(place, hidden_low)],
        [share_right(place, grad_gate_up), share_right(place, upstream_low)],
    )
    grad_normed_two = jnp.einsum(
        "rk,dk->rd", grad_gate_up, weight_in, preferred_element_type=jnp.float32
    )
    grad_middle_part, grad_gain_mlp = norm_two_back(grad_normed_two)
    grad_middle = upstream + grad_middle_part
    middle_low = grad_middle.astype(jnp.bfloat16)
    (attn_part,) = partial_grads(
        place, [share_left(place, attended_low)], [share_right(place, middle_low)]
    )
    in_weight_g, attn_out_g, out_weight_g = finish_grads(
        place, where, [in_part, attn_part, out_part], width
    )
    grad_attended = jnp.einsum(
        "rd,cd->rc", middle_low, weight_attn, preferred_element_type=jnp.float32
    )
    grad_attended = grad_attended.astype(jnp.bfloat16).reshape(block_len, head_count, HD)
    grad_probs = jnp.einsum(
        "qhd,khd->hqk", grad_attended, value_rows, preferred_element_type=jnp.float32
    )
    probs_again = jnp.exp(masked_scores() - log_total)
    weighted = jnp.sum(probs_again * grad_probs, axis=-1, keepdims=True)
    grad_scores = (probs_again * (grad_probs - weighted)).astype(jnp.bfloat16)
    grad_queries = (
        jnp.einsum("hqk,khd->qhd", grad_scores, key_rows, preferred_element_type=jnp.float32)
        * score_scale
    )
    grad_keys = (
        jnp.einsum("hqk,qhd->khd", grad_scores, queries, preferred_element_type=jnp.float32)
        * score_scale
    )
    grad_values = jnp.einsum(
        "hqk,qhd->khd", probs_low, grad_attended, preferred_element_type=jnp.float32
    )
    grad_projected = jnp.concatenate(
        [
            unrotate(grad_queries, cosine, sine_table).reshape(block_len, model_width),
            unrotate(grad_keys, cosine, sine_table).reshape(block_len, model_width),
            grad_values.reshape(block_len, model_width),
        ],
        axis=-1,
    ).astype(jnp.bfloat16)
    (qkv_part,) = partial_grads(
        place, [share_left(place, normed_one_low)], [share_right(place, grad_projected)]
    )
    (qkv_weight_g,) = finish_grads(place, where, [qkv_part], width)
    grad_normed_one = jnp.einsum(
        "rk,dk->rd", grad_projected, weight_qkv, preferred_element_type=jnp.float32
    )
    grad_input_part, grad_gain_attn = norm_one_back(grad_normed_one)
    grad_inputs = grad_middle + grad_input_part
    attn_gain_g, mlp_gain_g = reduce_gains(place, jnp.stack([grad_gain_attn, grad_gain_mlp]))
    return (
        result.astype(jnp.bfloat16)[None],
        grad_inputs[None],
        attn_gain_g,
        qkv_weight_g,
        attn_out_g,
        mlp_gain_g,
        in_weight_g,
        out_weight_g,
    )


def solution(mesh):
    return jax.shard_map(
        functools.partial(body, mesh.shape["shard"], mesh.shape["rep"]),
        mesh=mesh,
        in_specs=(
            P(("rep", "shard"), None, None),
            P(("rep", "shard"), None),
            P("shard"),
            P("shard", None),
            P("shard", None),
            P("shard"),
            P("shard", None),
            P("shard", None),
            P(("rep", "shard"), None, None),
        ),
        out_specs=(
            P(("rep", "shard"), None, None),
            P(("rep", "shard"), None, None),
            P("shard"),
            P("shard", None),
            P("shard", None),
            P("shard"),
            P("shard", None),
            P("shard", None),
        ),
        check_vma=False,
    )
```

```python
import functools
import math

import jax
import jax.numpy as jnp
from jax import lax
from jax.experimental import pallas as pl
from jax.experimental.pallas import tpu as pltpu
from jax.sharding import PartitionSpec as P

HD = 64
PAIR = 2 * HD


rope_base = 160000.0
epsilon = 1e-05
VMEM = pl.BlockSpec(memory_space=pltpu.VMEM)
SMEM = pl.BlockSpec(memory_space=pltpu.SMEM)
ANY = pl.BlockSpec(memory_space=pl.ANY)
SHARD, PLANE, CORE, ACT, SUM = range(5)
f32, bf16 = jnp.float32, jnp.bfloat16


def like(shape, dtype):
    return jax.ShapeDtypeStruct(tuple(shape), dtype)


def call(kernel, where, operands, outs, scratch=(), after=(), cost=1.0):
    count, late = len(operands), len(operands) + len(after)

    def inner(where_ref, *refs):
        kernel(where_ref, *refs[:count], *refs[late:])

    return pl.pallas_call(
        inner,
        out_shape=list(outs),
        in_specs=[SMEM] + [VMEM] * count + [ANY] * len(after),
        out_specs=[VMEM] * len(outs),
        scratch_shapes=list(scratch),
        compiler_params=pltpu.CompilerParams(vmem_limit_bytes=32 * 2**20),
        cost_estimate=pl.CostEstimate(
            flops=0, bytes_accessed=int(cost * 3.5e6), transcendentals=0
        ),
    )(where, *operands, *after)


class Place:
    def __init__(self, shards, reps):
        self.shards, self.planes = shards, reps // 2
        self.bits = self.planes.bit_length() - 1
        if self.planes != 1 << self.bits or self.bits % 2 or shards % 2:
            raise ValueError("mesh sizes")
        pairs = range(0, self.bits, 2)
        self.orders = tuple([i + k for i in pairs for k in turn] for turn in ((0, 1), (1, 0)))
        rep = lax.axis_index("rep")
        self.shard, self.plane, self.core = lax.axis_index("shard"), rep // 2, rep % 2
        self.first = self.core == 0
        self.where = jnp.stack(
            [self.shard, self.plane, self.core, self.bit(0), self.bit(1)]
        ).astype(jnp.int32)

    def permute(self, array, source):
        flat = lambda s, p, c: (2 * p + c) * self.shards + s
        pairs = []
        for p in range(self.planes):
            for c in range(2):
                for s in range(self.shards):
                    from_s, from_p = source(s, p, c)
                    pairs.append((flat(from_s % self.shards, from_p, c), flat(s, p, c)))
        return lax.ppermute(array, ("rep", "shard"), pairs)

    def from_core(self, array):
        return lax.ppermute(array, "rep", [(r, r ^ 1) for r in range(2 * self.planes)])

    def from_bit(self, array, step):
        return self.permute(array, lambda s, p, c: (s, p ^ (1 << self.orders[c][step])))

    def bit(self, step):
        at = jnp.where(self.first, self.orders[0][step], self.orders[1][step])
        return (self.plane >> at) & 1

    def both(self, mine, other):
        return jnp.where(self.first, mine, other), jnp.where(self.first, other, mine)


def pick(array, index, axis=0):
    return lax.dynamic_index_in_dim(array, index, axis, keepdims=False)


def piece_kernel(width, where, *refs):
    blocks, piece, part = refs[:-2], refs[-2], refs[-1]
    half = part.shape[0]
    at = 0
    for block in blocks:
        for k in range(block.shape[2] // width):
            value = block[where[PLANE], :, k * width : (k + 1) * width]
            piece[at] = value

            @pl.when(where[CORE] == at // half)
            def _(value=value, at=at):
                part[at % half] = value

            at += 1


def column_kernel(shards, where, *refs):
    count = shards // 2
    mine, other, ahead, behind = refs[:count], refs[count : 2 * count], refs[-2], refs[-1]
    total = mine[0].shape[0] if count > 1 else 2 * mine[-1].shape[0]
    half = total // 2

    def fill(core):
        for k in range(total):
            out = ahead if k // half == core else behind
            for d in range(1, count):
                out[0, d - 1, k % half] = (other if core else mine)[d - 1][k]
                out[0, shards - d - 1, k % half] = (mine if core else other)[d - 1][k]
            out[0, count - 1, k % half] = (mine if k // half == core else other)[-1][k % half]

    for core in range(2):
        pl.when(where[CORE] == core)(functools.partial(fill, core))


def join_kernel(shards, chunks, where, *refs):
    count = len(chunks)
    owns, outs = refs[:count], refs[count + 8 :]
    ahead, behind, mine_a, mine_b, mine_far, other_a, other_b, other_far = refs[
        count : count + 8
    ]
    inner, half, width = ahead.shape[0], ahead.shape[2], ahead.shape[-1]
    shard, plane = where[SHARD], where[PLANE]
    for own, out in zip(owns, outs):
        out[shard] = own[...]

    def fill(core):
        mine, other = (mine_a, mine_b), (other_a, other_b)
        low, high = (other, mine) if core else (mine, other)
        far = (other_far, mine_far) if core else (mine_far, other_far)
        for d in range(shards - 1):
            row = lax.rem(shard + d + 1, shards)
            for i in range(inner):
                at = 0
                for out, chunk in zip(outs, chunks):
                    for k in range(chunk):
                        lanes = slice(k * width, (k + 1) * width)
                        side, rest = at // half, at % half
                        own = (ahead, behind)[side ^ core]
                        out[row, plane ^ i, :, lanes] = own[i, d, rest]
                        out[row, plane ^ (inner + i), :, lanes] = low[side][i, d, rest]
                        out[row, plane ^ (2 * inner + i), :, lanes] = high[1 - side][i, d, rest]
                        out[row, plane ^ (3 * inner + i), :, lanes] = far[side][i, d, rest]
                        at += 1

    for core in range(2):
        pl.when(where[CORE] == core)(functools.partial(fill, core))


def gather_weights(place, weights, width, after=()):
    shards, planes = place.shards, place.planes
    height = weights[0].shape[0] // planes
    chunks = [weight.shape[1] // width for weight in weights]
    half = sum(chunks) // 2
    blocks = [weight.reshape(planes, height, weight.shape[1]) for weight in weights]
    piece, part = call(
        functools.partial(piece_kernel, width),
        place.where,
        blocks,
        [like((2 * half, height, width), bf16), like((half, height, width), bf16)],
        after=after,
    )
    mine = [
        place.permute(piece, lambda s, p, c, d=d: (s - d if c else s + d, p))
        for d in range(1, shards // 2)
    ]
    mine.append(place.permute(part, lambda s, p, c: (s + shards // 2, p)))
    other = [place.from_core(array) for array in mine]
    sides = [like((1, shards - 1, half, height, width), bf16)] * 2
    ahead, behind = call(
        functools.partial(column_kernel, shards), place.where, mine + other, sides
    )
    for level in range(0, place.bits, 2):
        mine_a = place.from_bit(ahead, level)
        mine_far = place.from_bit(mine_a, level + 1)
        mine_b = place.from_bit(behind, level)
        other_a, other_far, other_b = (
            place.from_core(mine_a),
            place.from_core(mine_far),
            place.from_core(mine_b),
        )
        if level + 2 < place.bits:
            first = place.first
            join = lambda *parts: jnp.concatenate(parts, axis=2)
            whole = jnp.concatenate(
                [
                    jnp.where(first, join(ahead, behind), join(behind, ahead)),
                    jnp.where(first, join(mine_a, mine_b), join(other_a, other_b)),
                    jnp.where(first, join(other_b, other_a), join(mine_b, mine_a)),
                    jnp.where(first, join(mine_far, other_far), join(other_far, mine_far)),
                ]
            )
            ahead, behind = place.both(whole[:, :, :half], whole[:, :, half:])
    wholes = call(
        functools.partial(join_kernel, shards, chunks),
        place.where,
        blocks + [ahead, behind, mine_a, mine_b, mine_far, other_a, other_b, other_far],
        [like((shards,) + block.shape, bf16) for block in blocks],
        cost=2.0,
    )
    wholes = [
        whole.reshape(shards * weight.shape[0], weight.shape[1])
        for whole, weight in zip(wholes, weights)
    ]
    return wholes, mine[-1]


def gains_kernel(shards, where, *refs):
    parts, outs, scratch = refs[:shards], refs[shards:-1], refs[-1]
    size = scratch.shape[2]
    for d in range(shards):
        scratch[lax.rem(where[SHARD] + d, shards)] = parts[d][...].astype(f32)
    for i, out in enumerate(outs):
        for s in range(shards):
            out[:, s * size : (s + 1) * size] = scratch[s, i : i + 1]


def gather_gains(place, gains):
    shards = place.shards
    parts = [gains] + [
        place.permute(gains, lambda s, p, c, d=d: (s + d, p)) for d in range(1, shards)
    ]
    return call(
        functools.partial(gains_kernel, shards),
        place.where,
        parts,
        [like((1, shards * gains.shape[1]), f32)] * gains.shape[0],
        scratch=[pltpu.VMEM((shards,) + gains.shape, f32)],
    )


def rope_tables(segment_row):
    length = segment_row.shape[0]
    positions_all = jnp.arange(length, dtype=jnp.int32)
    changes = jnp.concatenate([jnp.ones((1,), bool), segment_row[1:] != segment_row[:-1]])
    starts_at = lax.cummax(jnp.where(changes, positions_all, 0))
    position = (positions_all - starts_at).astype(jnp.float32)
    frequency = rope_base ** (-jnp.arange(0, HD, 2, dtype=jnp.float32) / HD)
    angles = position[:, None] * frequency[None, :]
    cosine, sine = jnp.cos(angles), jnp.sin(angles)
    return (
        jnp.concatenate([cosine, cosine] * 2, axis=-1),
        jnp.concatenate([-sine, sine] * 2, axis=-1),
    )


def lane_of(array):
    return lax.broadcasted_iota(jnp.int32, array.shape, len(array.shape) - 1)


def swap_halves(array):
    lane = lane_of(array)
    return jnp.where(
        lane % HD < HD // 2,
        pltpu.roll(array, PAIR - HD // 2, 1),
        pltpu.roll(array, HD // 2, 1),
    )


def only(array, head):
    return jnp.where(lane_of(array) // HD == head, array, jnp.zeros_like(array))


def dot(left, right, left_axis=1, right_axis=0):
    return lax.dot_general(
        left, right, (((left_axis,), (right_axis,)), ((), ())), preferred_element_type=f32
    )


def normalise(values):
    centred = values - jnp.mean(values, axis=-1, keepdims=True)
    scale = lax.rsqrt(jnp.mean(centred * centred, axis=-1, keepdims=True) + epsilon)
    return centred * scale, scale


def norm_back(values, gain, grad):
    normal, scale = normalise(values)
    scaled = grad * gain
    inner = jnp.mean(scaled * normal, axis=-1, keepdims=True)
    back = scale * (scaled - jnp.mean(scaled, axis=-1, keepdims=True) - normal * inner)
    return back, jnp.sum(grad * normal, axis=0, keepdims=True)


def split_shards(array, out, shards):
    size = array.shape[1] // shards // 2
    for half in range(2):
        out[half] = jnp.concatenate(
            [array[:, (2 * s + half) * size : (2 * s + half + 1) * size] for s in range(shards)],
            axis=1,
        )


def norm_kernel(shards, where, tokens, gain, normed, parts):
    value = (normalise(tokens[...].astype(f32))[0] * gain[...]).astype(bf16)
    normed[...] = value
    split_shards(value, parts, shards)


def attend_kernel(
    shards, where, normed, weight, cosine, sine, across, down, queries, keys, values, attended,
    parts, probs, projected,
):
    width = normed.shape[1]
    projected[...] = dot(normed[...], weight[...])
    same = across[...] == down[...]
    for pair in range(width // PAIR):
        lanes = slice(pair * PAIR, (pair + 1) * PAIR)

        def turned(start):
            vector = projected[:, start + pair * PAIR : start + (pair + 1) * PAIR]
            return (vector * cosine[...] + swap_halves(vector) * sine[...]).astype(bf16)

        query, key = turned(0), turned(width)
        value = projected[:, 2 * width + pair * PAIR : 2 * width + (pair + 1) * PAIR].astype(bf16)
        queries[:, lanes], keys[:, lanes], values[:, lanes] = query, key, value
        total = 0.0
        for head in range(2):
            scores = dot(only(query, head), key, 1, 1) * HD**-0.5
            scores = jnp.where(same, scores, -1000000000.0)
            exponent = jnp.exp(scores - jnp.max(scores, axis=-1, keepdims=True))
            prob = exponent / jnp.sum(exponent, axis=-1, keepdims=True)
            probs[2 * pair + head] = prob
            total = total + dot(prob.astype(bf16), only(value, head))
        attended[:, lanes] = total.astype(bf16)
    split_shards(attended[...], parts, shards)


def hidden_kernel(
    shards, where, tokens, attended, weight_attn, gain, weight_in, middle, normed_parts, by_gate,
    by_up, hidden, hidden_parts,
):
    value = tokens[...].astype(f32) + dot(attended[...], weight_attn[...])
    middle[...] = value
    normed = (normalise(value)[0] * gain[...]).astype(bf16)
    split_shards(normed, normed_parts, shards)
    size = hidden.shape[1]
    gate, up = dot(normed, weight_in[:, :size]), dot(normed, weight_in[:, size:])
    below = 0.5 * (1.0 + lax.erf(gate * math.sqrt(0.5)))
    active = gate * below
    by_up[...] = active
    by_gate[...] = up * (
        below + gate * jnp.exp(-0.5 * gate * gate) * (1.0 / math.sqrt(2.0 * math.pi))
    )
    low = (active * up).astype(bf16)
    hidden[...] = low
    split_shards(low, hidden_parts, shards)


def output_kernel(
    where, middle, hidden, weight_out, cotangent, by_gate, by_up, output, grad_halves, grad_sent
):
    output[...] = (middle[...] + dot(hidden[...], weight_out[...])).astype(bf16)
    grad = dot(cotangent[...], weight_out[...], 1, 1).astype(bf16).astype(f32)
    grad_halves[0] = (grad * by_gate[...]).astype(bf16)
    grad_halves[1] = (grad * by_up[...]).astype(bf16)
    grad_sent[...] = grad_halves[1 - where[CORE]]


def middle_kernel(
    where, grad_halves, weight_in, middle, gain, cotangent, weight_attn, grad_middle, low_halves,
    low_sent, grad_attended, grad_gain,
):
    size = grad_halves.shape[2]
    grad = dot(grad_halves[0], weight_in[:, :size], 1, 1)
    grad = grad + dot(grad_halves[1], weight_in[:, size:], 1, 1)
    back, gain_part = norm_back(middle[...], gain[...], grad)
    grad_gain[...] = gain_part
    total = cotangent[...].astype(f32) + back
    grad_middle[...] = total
    low = total.astype(bf16)
    half = low.shape[1] // 2
    low_halves[0], low_halves[1] = low[:, :half], low[:, half:]
    low_sent[...] = low_halves[1 - where[CORE]]
    grad_attended[...] = dot(low, weight_attn[...], 1, 1).astype(bf16)


def attend_back_kernel(
    where, grad_attended, queries, keys, values, probs, cosine, sine, grad_halves, grad_sent
):
    width = queries.shape[1]
    half = grad_halves.shape[2]

    def store(start, grad):
        side, rest = divmod(start, half)
        grad_halves[side, :, rest : rest + PAIR] = grad.astype(bf16)

    for pair in range(width // PAIR):
        lanes = slice(pair * PAIR, (pair + 1) * PAIR)
        query, key, value = queries[:, lanes], keys[:, lanes], values[:, lanes]
        above = grad_attended[:, lanes]
        by_query, by_key, by_value = 0.0, 0.0, 0.0
        for head in range(2):
            own = only(above, head)
            grad = dot(own, value, 1, 1)
            prob = probs[2 * pair + head]
            weighted = jnp.sum(prob * grad, axis=-1, keepdims=True)
            grad = (prob * (grad - weighted)).astype(bf16)
            by_query = by_query + dot(grad, only(key, head))
            by_key = by_key + dot(grad, only(query, head), 0, 0)
            by_value = by_value + dot(prob.astype(bf16), own, 0, 0)

        def back(grad):
            grad = grad * HD**-0.5
            return grad * cosine[...] - swap_halves(grad) * sine[...]

        store(pair * PAIR, back(by_query))
        store(width + pair * PAIR, back(by_key))
        store(2 * width + pair * PAIR, by_value)
    grad_sent[...] = grad_halves[1 - where[CORE]]


def tokens_kernel(where, grad_halves, weight, tokens, gain, grad_middle, grad_tokens, grad_gain):
    half = grad_halves.shape[2]
    grad = dot(grad_halves[0], weight[:, :half], 1, 1)
    grad = grad + dot(grad_halves[1], weight[:, half:], 1, 1)
    back, gain_part = norm_back(tokens[...].astype(f32), gain[...], grad)
    grad_gain[...] = gain_part
    grad_tokens[...] = grad_middle[...] + back


def message_kernel(where, *refs):
    sources, out = refs[:-1], refs[-1]
    rows = out.shape[0] // 2
    at = 0
    for own, other in zip(sources[::2], sources[1::2]):
        size = own.shape[-1]
        lanes = slice(at, at + size)
        if len(other.shape) == 3:
            out[:rows, lanes] = own[1 - where[ACT]]
            out[rows:, lanes] = other[1 - where[ACT]]
        else:
            out[:rows, lanes] = own[where[CORE]]
            out[rows:, lanes] = other[...]
        at += size


def send_factors(place, factors):
    rows = 2 * factors[0][0].shape[1]
    columns = sum(own.shape[-1] for own, _ in factors)
    flat = [array for pair in factors for array in pair]
    (message,) = call(message_kernel, place.where, flat, [like((rows, columns), bf16)])
    return place.from_bit(message, 0)


def grads_kernel(shards, planes, plan, where, *refs):
    sources, messages = plan["sources"], plan["messages"]
    pairs = [refs[2 * i : 2 * i + 2] for i in range(sources)]
    arrived = refs[2 * sources : 2 * sources + messages]
    sent, kept = refs[2 * sources + messages : 2 * sources + messages + 2]
    scratch = refs[2 * sources + messages + 2 :]
    width = kept.shape[-1]

    def factor(place, left):
        index, message, lane = place
        own, other = pairs[index]
        size = own.shape[-1]
        far = arrived[message][:, lane : lane + size]
        if left:
            parts = [own[where[ACT]], other[where[ACT]], far]
        else:
            parts = [own[where[CORE]], other[...], far]
        return jnp.concatenate(parts, axis=0)

    for (left, right), grad in zip(plan["grads"], scratch):
        grad[...] = dot(factor(left, True), factor(right, False), 0, 0)

    def fill(bit):
        at = 0
        for grad in scratch:
            height = grad.shape[0] // shards // (planes // 2)
            for k in range(grad.shape[1] // width):
                for s in range(shards):
                    for j in range(planes // 2):
                        side, rest = divmod(j, planes // 4)
                        row = (s * (planes // 2) + j) * height
                        block = grad[row : row + height, k * width : (k + 1) * width]
                        if side == bit:
                            kept[s, rest, at : at + height] = block
                        else:
                            sent[s, rest, at : at + height] = block.astype(bf16)
                at += height

    for bit in range(2):
        pl.when(where[SUM] == bit)(functools.partial(fill, bit))


def total_kernel(shards, where, kept, got, *outs):
    own, sends = outs[0], outs[1:]
    shard = where[SHARD]
    own[...] = kept[shard, 0] + got[shard, 0].astype(f32)
    for d, send in enumerate(sends):
        row = lax.rem(shard + d + 1, shards)
        send[...] = (kept[row, 0] + got[row, 0].astype(f32)).astype(bf16)


def round_kernel(where, own, *refs):
    total = own[...]
    for array in refs[:-1]:
        total = total + array[...].astype(f32)
    refs[-1][...] = total.astype(bf16)


def spread_kernel(orders, bits, heights, chunks, where, *refs):
    planes = 1 << bits
    mine, other, outs = refs[:planes], refs[planes : 2 * planes], refs[2 * planes :]
    width = mine[0].shape[-1]
    starts = []
    for order in orders:
        start = 0
        for step, at in enumerate(order):
            start = start + (((where[PLANE] >> at) & 1) << (bits - 1 - step))
        starts.append(start)

    def fill(core):
        first, second = (other, mine) if core else (mine, other)
        for p in range(planes):
            at = 0
            for out, height, chunk in zip(outs, heights, chunks):
                for k in range(chunk):
                    rows = slice(at, at + height)
                    near = slice(k * width, (k + 1) * width)
                    far = slice((chunk + k) * width, (chunk + k + 1) * width)
                    out[p ^ starts[0], :, near] = first[p][rows].astype(f32)
                    out[p ^ starts[1], :, far] = second[p][rows].astype(f32)
                    at += height

    for core in range(2):
        pl.when(where[CORE] == core)(functools.partial(fill, core))


def reduce_weights(place, width, sources, messages, grads, after=()):
    shards, planes = place.shards, place.planes
    found = {}
    for number, (_, inside) in enumerate(messages):
        lane = 0
        for index in inside:
            found[index] = (index, number, lane)
            lane += sources[index][0].shape[-1]
    plan = {
        "sources": len(sources),
        "messages": len(messages),
        "grads": [(found[left], found[right]) for left, right in grads],
    }
    shapes = [
        (sources[left][0].shape[-1], sources[right][0].shape[-1]) for left, right in grads
    ]
    heights = [rows // shards // (planes // 2) for rows, _ in shapes]
    chunks = [columns // width for _, columns in shapes]
    total = sum(height * chunk for height, chunk in zip(heights, chunks))
    packed = (shards, planes // 4, total, width)
    sent, kept = call(
        functools.partial(grads_kernel, shards, planes, plan),
        place.where,
        [array for pair in sources for array in pair] + [array for array, _ in messages],
        [like(packed, bf16), like(packed, f32)],
        scratch=[pltpu.VMEM(shape, f32) for shape in shapes],
        after=after,
        cost=4.0,
    )
    got = place.from_bit(sent, 1)
    for step in range(2, place.bits):
        whole = (kept + got.astype(f32)).reshape(shards, 2, -1, total, width)
        kept = pick(whole, place.bit(step), 1)
        got = place.from_bit(pick(whole, 1 - place.bit(step), 1).astype(bf16), step)
    own, *sends = call(
        functools.partial(total_kernel, shards),
        place.where,
        [kept, got],
        [like((total, width), f32)] + [like((total, width), bf16)] * (shards - 1),
    )
    arrived = [
        place.permute(send, lambda s, p, c, d=d: (s - d - 1, p)) for d, send in enumerate(sends)
    ]
    mine = list(call(round_kernel, place.where, [own, *arrived], [like((total, width), bf16)]))
    for step in reversed(range(place.bits)):
        mine = mine + [place.from_bit(array, step) for array in mine]
    other = [place.from_core(array) for array in mine]
    outs = call(
        functools.partial(spread_kernel, place.orders, place.bits, heights, chunks),
        place.where,
        mine + other,
        [
            like((planes, height, 2 * chunk * width), f32)
            for height, chunk in zip(heights, chunks)
        ],
        cost=2.0,
    )
    return [out.reshape(-1, out.shape[2]) for out in outs]


def reduce_gains(place, grad):
    grad = grad + place.from_core(grad)
    for step in range(place.bits):
        grad = grad + place.from_bit(grad, step)
    blocks = grad.reshape(grad.shape[0], place.shards, -1)
    total = pick(blocks, place.shard, 1)
    for d in range(1, place.shards):
        sent = pick(blocks, (place.shard + d) % place.shards, 1)
        total = total + place.permute(sent, lambda s, p, c, d=d: (s - d, p))
    return total


def body(
    shards,
    reps,
    tokens,
    segment_ids,
    attn_gain,
    qkv_weight,
    attn_out_weight,
    mlp_gain,
    in_weight,
    out_weight,
    cotangent,
):
    place = Place(shards, reps)
    where = place.where
    tokens, segments, cotangent = tokens[0], segment_ids[0], cotangent[0]
    length, model = tokens.shape
    heads, size = model // HD, out_weight.shape[0] * shards
    width = model // 2
    rows = lambda columns, kind=bf16: like((length, columns), kind)
    halves = lambda columns: like((2, length, columns // 2), bf16)
    cosine, sine = rope_tables(segments)

    (weight_qkv,), passed = gather_weights(place, [qkv_weight], width)
    gain_attn, gain_mlp = gather_gains(place, jnp.stack([attn_gain, mlp_gain]))
    (weight_attn, weight_in), passed = gather_weights(
        place, [attn_out_weight, in_weight], width, after=[passed]
    )
    (weight_out,), _ = gather_weights(place, [out_weight], width, after=[passed])

    cotangent_halves = cotangent.reshape(length, 2, width).transpose(1, 0, 2)
    cotangent_other = place.from_core(pick(cotangent_halves, 1 - place.core))
    normed_one, one_parts = call(
        functools.partial(norm_kernel, shards),
        where,
        [tokens, gain_attn],
        [rows(model), halves(model)],
    )
    one_factor = (one_parts, place.from_core(one_parts))
    one_arrived = send_factors(place, [one_factor])

    queries, keys, values, attended, attended_parts, probs = call(
        functools.partial(attend_kernel, shards),
        where,
        [normed_one, weight_qkv, cosine, sine, segments[:, None], segments[None, :]],
        [rows(model)] * 4 + [halves(model), like((heads, length, length), f32)],
        scratch=[pltpu.VMEM((length, 3 * model), f32)],
        after=[one_arrived, cotangent_other],
        cost=9.0,
    )
    middle, two_parts, by_gate, by_up, hidden, hidden_parts = call(
        functools.partial(hidden_kernel, shards),
        where,
        [tokens, attended, weight_attn, gain_mlp, weight_in],
        [rows(model, f32), halves(model), rows(size, f32), rows(size, f32), rows(size), halves(size)],
        cost=6.0,
    )
    output, gate_up_halves, gate_up_sent = call(
        output_kernel,
        where,
        [middle, hidden, weight_out, cotangent, by_gate, by_up],
        [rows(model), halves(2 * size), rows(size)],
        cost=4.0,
    )
    factors = [
        (two_parts, place.from_core(two_parts)),
        (gate_up_halves, place.from_core(gate_up_sent)),
        (cotangent_halves, cotangent_other),
        (hidden_parts, place.from_core(hidden_parts)),
    ]
    arrived = send_factors(place, factors)
    grad_middle, low_halves, low_sent, grad_attended, mlp_gain_part = call(
        middle_kernel,
        where,
        [gate_up_halves, weight_in, middle, gain_mlp, cotangent, weight_attn],
        [rows(model, f32), halves(model), rows(width), rows(model), like((1, model), f32)],
        cost=6.0,
    )
    attn_factors = [
        (attended_parts, place.from_core(attended_parts)),
        (low_halves, place.from_core(low_sent)),
    ]
    attn_arrived = send_factors(place, attn_factors)
    projected_halves, projected_sent = call(
        attend_back_kernel,
        where,
        [grad_attended, queries, keys, values, probs, cosine, sine],
        [halves(3 * model), rows(3 * model // 2)],
        cost=9.0,
    )
    projected_factor = (projected_halves, place.from_core(projected_sent))
    projected_arrived = send_factors(place, [projected_factor])
    in_weight_g, attn_out_g, out_weight_g = reduce_weights(
        place,
        width,
        factors + attn_factors,
        [(arrived, [0, 1, 2, 3]), (attn_arrived, [4, 5])],
        [(0, 1), (4, 5), (3, 2)],
        after=[projected_halves],
    )
    (qkv_weight_g,) = reduce_weights(
        place,
        width,
        [one_factor, projected_factor],
        [(one_arrived, [0]), (projected_arrived, [1])],
        [(0, 1)],
    )
    grad_tokens, attn_gain_part = call(
        tokens_kernel,
        where,
        [projected_halves, weight_qkv, tokens, gain_attn, grad_middle],
        [rows(model, f32), like((1, model), f32)],
        cost=5.0,
    )
    attn_gain_g, mlp_gain_g = reduce_gains(
        place, jnp.concatenate([attn_gain_part, mlp_gain_part])
    )
    return (
        output[None],
        grad_tokens[None],
        attn_gain_g,
        qkv_weight_g,
        attn_out_g,
        mlp_gain_g,
        in_weight_g,
        out_weight_g,
    )


def solution(mesh):
    return jax.shard_map(
        functools.partial(body, mesh.shape["shard"], mesh.shape["rep"]),
        mesh=mesh,
        in_specs=(
            P(("rep", "shard"), None, None),
            P(("rep", "shard"), None),
            P("shard"),
            P("shard", None),
            P("shard", None),
            P("shard"),
            P("shard", None),
            P("shard", None),
            P(("rep", "shard"), None, None),
        ),
        out_specs=(
            P(("rep", "shard"), None, None),
            P(("rep", "shard"), None, None),
            P("shard"),
            P("shard", None),
            P("shard", None),
            P("shard"),
            P("shard", None),
            P("shard", None),
        ),
        check_vma=False,
    )
```

```python
import functools
import math

import jax
import jax.numpy as jnp
from jax import lax
from jax.experimental import pallas as pl
from jax.experimental.pallas import tpu as pltpu
from jax.sharding import PartitionSpec as P

HD = 64
PAIR = 2 * HD


rope_base = 160000.0
epsilon = 1e-05
VMEM = pl.BlockSpec(memory_space=pltpu.VMEM)
SMEM = pl.BlockSpec(memory_space=pltpu.SMEM)
ANY = pl.BlockSpec(memory_space=pl.ANY)
SHARD, PLANE, CORE, ACT, SUM = range(5)
GAIN_ROWS = 16
f32, bf16 = jnp.float32, jnp.bfloat16


def like(shape, dtype):
    return jax.ShapeDtypeStruct(tuple(shape), dtype)


def padded_bytes(array):
    *lead, rows, columns = array.shape
    tile = 8 * 4 // array.dtype.itemsize
    return (
        math.prod(lead) * -(-rows // tile) * tile * -(-columns // 128) * 128 * array.dtype.itemsize
    )


def call(kernel, where, operands, outs, scratch=(), after=(), cost=1.0):
    count, late = len(operands), len(operands) + len(after)
    room = sum(padded_bytes(array) for array in [*operands, *outs, *scratch])

    def inner(where_ref, *refs):
        kernel(where_ref, *refs[:count], *refs[late:])

    return pl.pallas_call(
        inner,
        out_shape=list(outs),
        in_specs=[SMEM] + [VMEM] * count + [ANY] * len(after),
        out_specs=[VMEM] * len(outs),
        scratch_shapes=list(scratch),
        compiler_params=pltpu.CompilerParams(vmem_limit_bytes=room + 6 * 2**20),
        cost_estimate=pl.CostEstimate(
            flops=0, bytes_accessed=int(cost * 3.5e6), transcendentals=0
        ),
    )(where, *operands, *after)


class Place:
    def __init__(self, shards, reps):
        self.shards, self.planes = shards, reps // 2
        self.bits = self.planes.bit_length() - 1
        if self.planes != 1 << self.bits or self.bits % 2 or shards % 2:
            raise ValueError("mesh sizes")
        pairs = range(0, self.bits, 2)
        self.orders = tuple([i + k for i in pairs for k in turn] for turn in ((0, 1), (1, 0)))
        rep = lax.axis_index("rep")
        self.shard, self.plane, self.core = lax.axis_index("shard"), rep // 2, rep % 2
        self.first = self.core == 0
        self.where = jnp.stack(
            [self.shard, self.plane, self.core, self.bit(0), self.bit(1)]
        ).astype(jnp.int32)

    def permute(self, array, source):
        flat = lambda s, p, c: (2 * p + c) * self.shards + s
        pairs = []
        for p in range(self.planes):
            for c in range(2):
                for s in range(self.shards):
                    from_s, from_p = source(s, p, c)
                    pairs.append((flat(from_s % self.shards, from_p, c), flat(s, p, c)))
        return lax.ppermute(array, ("rep", "shard"), pairs)

    def from_core(self, array):
        return lax.ppermute(array, "rep", [(r, r ^ 1) for r in range(2 * self.planes)])

    def from_bit(self, array, step):
        return self.permute(array, lambda s, p, c: (s, p ^ (1 << self.orders[c][step])))

    def bit(self, step):
        at = jnp.where(self.first, self.orders[0][step], self.orders[1][step])
        return (self.plane >> at) & 1

    def both(self, mine, other):
        return jnp.where(self.first, mine, other), jnp.where(self.first, other, mine)


def pick(array, index, axis=0):
    return lax.dynamic_index_in_dim(array, index, axis, keepdims=False)


def piece_kernel(width, with_gains, where, *refs):
    blocks, piece, part = refs[:-2], refs[-2], refs[-1]
    if with_gains:
        *blocks, gains = blocks
        rows, columns = gains.shape
        piece[piece.shape[0] - 1, :rows, :columns] = gains[...]
        part[part.shape[0] - 1, :rows, :columns] = gains[...]
    half = part.shape[0] - with_gains
    at = 0
    for block in blocks:
        for k in range(block.shape[2] // width):
            value = block[where[PLANE], :, k * width : (k + 1) * width]
            piece[at] = value

            @pl.when(where[CORE] == at // half)
            def _(value=value, at=at):
                part[at % half] = value

            at += 1


def column_kernel(shards, with_gains, where, *refs):
    count = shards // 2
    mine, other = refs[:count], refs[count : 2 * count]
    refs = refs[2 * count :]
    gains = None
    if with_gains:
        gains, refs = refs[0], refs[1:]
    ahead, behind = refs[:2]
    half = ahead.shape[2]

    def fill(core):
        near, far = (other, mine) if core else (mine, other)
        for k in range(2 * half):
            out = ahead if k // half == core else behind
            for d in range(1, count):
                out[0, d - 1, k % half] = near[d - 1][k]
                out[0, shards - d - 1, k % half] = far[d - 1][k]
            out[0, count - 1, k % half] = (mine if k // half == core else other)[-1][k % half]
        if with_gains:
            found = refs[-1]
            rows, columns = gains.shape
            found[where[SHARD]] = gains[...].astype(f32)

            def keep(d, value):
                found[lax.rem(where[SHARD] + d, shards)] = value[:rows, :columns].astype(f32)

            for d in range(1, count):
                keep(d, near[d - 1][2 * half])
                keep(shards - d, far[d - 1][2 * half])
            keep(count, mine[-1][half])

    for core in range(2):
        pl.when(where[CORE] == core)(functools.partial(fill, core))
    if with_gains:
        found = refs[-1]
        size = found.shape[2]
        for i, out in enumerate(refs[2:-1]):
            for s in range(shards):
                out[:, s * size : (s + 1) * size] = found[s, i : i + 1]


def join_kernel(shards, chunks, where, *refs):
    count = len(chunks)
    owns, outs = refs[:count], refs[count + 8 :]
    ahead, behind, mine_a, mine_b, mine_far, other_a, other_b, other_far = refs[
        count : count + 8
    ]
    inner, half, width = ahead.shape[0], ahead.shape[2], ahead.shape[-1]
    shard, plane = where[SHARD], where[PLANE]
    for own, out in zip(owns, outs):
        out[shard] = own[...]

    def fill(core):
        mine, other = (mine_a, mine_b), (other_a, other_b)
        low, high = (other, mine) if core else (mine, other)
        far = (other_far, mine_far) if core else (mine_far, other_far)
        for d in range(shards - 1):
            row = lax.rem(shard + d + 1, shards)
            for i in range(inner):
                at = 0
                for out, chunk in zip(outs, chunks):
                    for k in range(chunk):
                        lanes = slice(k * width, (k + 1) * width)
                        side, rest = at // half, at % half
                        own = (ahead, behind)[side ^ core]
                        out[row, plane ^ i, :, lanes] = own[i, d, rest]
                        out[row, plane ^ (inner + i), :, lanes] = low[side][i, d, rest]
                        out[row, plane ^ (2 * inner + i), :, lanes] = high[1 - side][i, d, rest]
                        out[row, plane ^ (3 * inner + i), :, lanes] = far[side][i, d, rest]
                        at += 1

    for core in range(2):
        pl.when(where[CORE] == core)(functools.partial(fill, core))


def gather_weights(place, weights, width, gains=None, after=(), between=()):
    shards, planes = place.shards, place.planes
    height = weights[0].shape[0] // planes
    chunks = [weight.shape[1] // width for weight in weights]
    half = sum(chunks) // 2
    blocks = [weight.reshape(planes, height, weight.shape[1]) for weight in weights]
    extra = [] if gains is None else [gains]
    with_gains = len(extra)
    piece, part = call(
        functools.partial(piece_kernel, width, with_gains),
        place.where,
        blocks + extra,
        [
            like((2 * half + with_gains, height, width), bf16),
            like((half + with_gains, height, width), bf16),
        ],
        after=after,
    )
    mine = [
        place.permute(piece, lambda s, p, c, d=d: (s - d if c else s + d, p))
        for d in range(1, shards // 2)
    ]
    mine.append(place.permute(part, lambda s, p, c: (s + shards // 2, p)))
    other = [place.from_core(array) for array in mine]
    outs = [like((1, shards - 1, half, height, width), bf16)] * 2
    scratch = []
    if extra:
        outs = outs + [like((1, shards * gains.shape[1]), f32)] * gains.shape[0]
        scratch = [pltpu.VMEM((shards,) + gains.shape, f32)]
    ahead, behind, *gains = call(
        functools.partial(column_kernel, shards, with_gains),
        place.where,
        mine + other + extra,
        outs,
        scratch=scratch,
        after=between,
    )
    free = ahead
    for level in range(0, place.bits, 2):
        mine_a = place.from_bit(ahead, level)
        mine_far = place.from_bit(mine_a, level + 1)
        mine_b = place.from_bit(behind, level)
        other_a, other_far, other_b = (
            place.from_core(mine_a),
            place.from_core(mine_far),
            place.from_core(mine_b),
        )
        if level + 2 < place.bits:
            first = place.first
            join = lambda *parts: jnp.concatenate(parts, axis=2)
            whole = jnp.concatenate(
                [
                    jnp.where(first, join(ahead, behind), join(behind, ahead)),
                    jnp.where(first, join(mine_a, mine_b), join(other_a, other_b)),
                    jnp.where(first, join(other_b, other_a), join(mine_b, mine_a)),
                    jnp.where(first, join(mine_far, other_far), join(other_far, mine_far)),
                ]
            )
            ahead, behind = place.both(whole[:, :, :half], whole[:, :, half:])
    wholes = call(
        functools.partial(join_kernel, shards, chunks),
        place.where,
        blocks + [ahead, behind, mine_a, mine_b, mine_far, other_a, other_b, other_far],
        [like((shards,) + block.shape, bf16) for block in blocks],
        cost=2.0,
    )
    wholes = [
        whole.reshape(shards * weight.shape[0], weight.shape[1])
        for whole, weight in zip(wholes, weights)
    ]
    return wholes, gains, (free, mine_a)


def lane_of(array):
    return lax.broadcasted_iota(jnp.int32, array.shape, len(array.shape) - 1)


def swap_halves(array):
    lane = lane_of(array)
    return jnp.where(
        lane % HD < HD // 2,
        pltpu.roll(array, PAIR - HD // 2, 1),
        pltpu.roll(array, HD // 2, 1),
    )


def only(array, head):
    return jnp.where(lane_of(array) // HD == head, array, jnp.zeros_like(array))


def dot(left, right, left_axis=1, right_axis=0):
    return lax.dot_general(
        left, right, (((left_axis,), (right_axis,)), ((), ())), preferred_element_type=f32
    )


def normalise(values):
    centred = values - jnp.mean(values, axis=-1, keepdims=True)
    scale = lax.rsqrt(jnp.mean(centred * centred, axis=-1, keepdims=True) + epsilon)
    return centred * scale, scale


def norm_back(values, gain, grad):
    normal, scale = normalise(values)
    scaled = grad * gain
    inner = jnp.mean(scaled * normal, axis=-1, keepdims=True)
    back = scale * (scaled - jnp.mean(scaled, axis=-1, keepdims=True) - normal * inner)
    return back, jnp.sum(grad * normal, axis=0, keepdims=True)


def split_shards(array, out, shards):
    size = array.shape[1] // shards // 2
    for half in range(2):
        out[half, :, : shards * size] = jnp.concatenate(
            [array[:, (2 * s + half) * size : (2 * s + half + 1) * size] for s in range(shards)],
            axis=1,
        )


def start_kernel(
    shards, where, tokens, gain, cotangent, across, down, normed, parts, halves, sent, cosine, sine
):
    value = (normalise(tokens[...].astype(f32))[0] * gain[...]).astype(bf16)
    normed[...] = value
    split_shards(value, parts, shards)
    width = halves.shape[2]
    for half in range(2):
        halves[half] = cotangent[:, half * width : (half + 1) * width]
    sent[...] = halves[1 - where[CORE]]
    same = across[...] == down[...]
    before = lane_of(same) < lax.broadcasted_iota(jnp.int32, same.shape, 0)
    position = jnp.sum(jnp.where(same & before, 1.0, 0.0), axis=1, keepdims=True)
    lane = lax.broadcasted_iota(jnp.int32, cosine.shape, 1)
    frequency = jnp.exp((lane % (HD // 2)).astype(f32) * (-2.0 / HD * math.log(rope_base)))
    angles = position * frequency
    cosine[...] = jnp.cos(angles)
    turn = jnp.sin(angles)
    sine[...] = jnp.where(lane % HD < HD // 2, -turn, turn)


def attend_kernel(
    shards, where, normed, weight, cosine, sine, across, down, queries, keys, values, attended,
    parts, probs, projected,
):
    width = normed.shape[1]
    projected[...] = dot(normed[...], weight[...])
    same = across[...] == down[...]
    for pair in range(width // PAIR):
        lanes = slice(pair * PAIR, (pair + 1) * PAIR)

        def turned(start):
            vector = projected[:, start + pair * PAIR : start + (pair + 1) * PAIR]
            return (vector * cosine[...] + swap_halves(vector) * sine[...]).astype(bf16)

        query, key = turned(0), turned(width)
        value = projected[:, 2 * width + pair * PAIR : 2 * width + (pair + 1) * PAIR].astype(bf16)
        queries[:, lanes], keys[:, lanes], values[:, lanes] = query, key, value
        total = 0.0
        for head in range(2):
            scores = dot(only(query, head), key, 1, 1) * HD**-0.5
            scores = jnp.where(same, scores, -1000000000.0)
            exponent = jnp.exp(scores - jnp.max(scores, axis=-1, keepdims=True))
            prob = exponent / jnp.sum(exponent, axis=-1, keepdims=True)
            probs[2 * pair + head] = prob
            total = total + dot(prob.astype(bf16), only(value, head))
        attended[:, lanes] = total.astype(bf16)
    split_shards(attended[...], parts, shards)


def hidden_kernel(
    shards, where, tokens, attended, weight_attn, gain, weight_in, middle, normed_parts, by_gate,
    by_up, hidden, hidden_parts,
):
    value = tokens[...].astype(f32) + dot(attended[...], weight_attn[...])
    middle[...] = value
    normed = (normalise(value)[0] * gain[...]).astype(bf16)
    split_shards(normed, normed_parts, shards)
    size = hidden.shape[1]
    gate, up = dot(normed, weight_in[:, :size]), dot(normed, weight_in[:, size:])
    below = 0.5 * (1.0 + lax.erf(gate * math.sqrt(0.5)))
    active = gate * below
    by_up[...] = active
    by_gate[...] = up * (
        below + gate * jnp.exp(-0.5 * gate * gate) * (1.0 / math.sqrt(2.0 * math.pi))
    )
    low = (active * up).astype(bf16)
    hidden[...] = low
    split_shards(low, hidden_parts, shards)


def output_kernel(
    where, middle, hidden, weight_out, cotangent, by_gate, by_up, output, grad_halves, grad_sent
):
    output[...] = (middle[...] + dot(hidden[...], weight_out[...])).astype(bf16)
    grad = dot(cotangent[...], weight_out[...], 1, 1).astype(bf16).astype(f32)
    grad_halves[0] = (grad * by_gate[...]).astype(bf16)
    grad_halves[1] = (grad * by_up[...]).astype(bf16)
    grad_sent[...] = grad_halves[1 - where[CORE]]


def middle_kernel(
    where, grad_halves, weight_in, middle, gain, cotangent, weight_attn, grad_middle, low_halves,
    low_sent, grad_attended, grad_gain,
):
    size = grad_halves.shape[2]
    grad = dot(grad_halves[0], weight_in[:, :size], 1, 1)
    grad = grad + dot(grad_halves[1], weight_in[:, size:], 1, 1)
    back, gain_part = norm_back(middle[...], gain[...], grad)
    grad_gain[...] = gain_part
    total = cotangent[...].astype(f32) + back
    grad_middle[...] = total
    low = total.astype(bf16)
    half = low.shape[1] // 2
    low_halves[0], low_halves[1] = low[:, :half], low[:, half:]
    low_sent[...] = low_halves[1 - where[CORE]]
    grad_attended[...] = dot(low, weight_attn[...], 1, 1).astype(bf16)


def attend_back_kernel(
    where, grad_attended, queries, keys, values, probs, cosine, sine, grad_halves, grad_sent
):
    width = queries.shape[1]
    half = grad_halves.shape[2]

    def store(start, grad):
        side, rest = divmod(start, half)
        grad_halves[side, :, rest : rest + PAIR] = grad.astype(bf16)

    for pair in range(width // PAIR):
        lanes = slice(pair * PAIR, (pair + 1) * PAIR)
        query, key, value = queries[:, lanes], keys[:, lanes], values[:, lanes]
        above = grad_attended[:, lanes]
        by_query, by_key, by_value = 0.0, 0.0, 0.0
        for head in range(2):
            own = only(above, head)
            grad = dot(own, value, 1, 1)
            prob = probs[2 * pair + head]
            weighted = jnp.sum(prob * grad, axis=-1, keepdims=True)
            grad = (prob * (grad - weighted)).astype(bf16)
            by_query = by_query + dot(grad, only(key, head))
            by_key = by_key + dot(grad, only(query, head), 0, 0)
            by_value = by_value + dot(prob.astype(bf16), own, 0, 0)

        def back(grad):
            grad = grad * HD**-0.5
            return grad * cosine[...] - swap_halves(grad) * sine[...]

        store(pair * PAIR, back(by_query))
        store(width + pair * PAIR, back(by_key))
        store(2 * width + pair * PAIR, by_value)
    grad_sent[...] = grad_halves[1 - where[CORE]]


def tokens_kernel(where, grad_halves, weight, tokens, gain, grad_middle, grad_tokens, grad_gain):
    half = grad_halves.shape[2]
    grad = dot(grad_halves[0], weight[:, :half], 1, 1)
    grad = grad + dot(grad_halves[1], weight[:, half:], 1, 1)
    back, gain_part = norm_back(tokens[...].astype(f32), gain[...], grad)
    grad_gain[...] = gain_part
    grad_tokens[...] = grad_middle[...] + back


def message_kernel(where, *refs):
    sources, out = refs[:-1], refs[-1]
    rows = out.shape[0] // 2
    at = 0
    for own, other in zip(sources[::2], sources[1::2]):
        size = own.shape[-1]
        lanes = slice(at, at + size)
        if len(other.shape) == 3:
            out[:rows, lanes] = own[1 - where[ACT]]
            out[rows:, lanes] = other[1 - where[ACT]]
        else:
            out[:rows, lanes] = own[where[CORE]]
            out[rows:, lanes] = other[...]
        at += size


def send_factors(place, factors):
    rows = 2 * factors[0][0].shape[1]
    columns = sum(own.shape[-1] for own, _ in factors)
    flat = [array for pair in factors for array in pair]
    (message,) = call(message_kernel, place.where, flat, [like((rows, columns), bf16)])
    return message, place.from_bit(message, 0)


def chip_factor(own, other, index):
    far = other[index] if len(other.shape) == 3 else other[...]
    return jnp.concatenate([own[index], far], axis=0)


def near_grad_kernel(shards, where, left, left_other, right, right_other, own, *refs):
    sends, grad = refs[:-1], refs[-1]
    height = grad.shape[1] // 2
    factor = chip_factor(right, right_other, where[CORE])
    for half in range(2):
        value = dot(chip_factor(left, left_other, half), factor, 0, 0)
        for s in range(shards):
            grad[s, half * height : (half + 1) * height] = value[s * height : (s + 1) * height]
    own[...] = grad[where[SHARD]]
    for d, send in enumerate(sends):
        send[...] = grad[lax.rem(where[SHARD] + d + 1, shards)].astype(bf16)


def near_grad(place, left, right, height, after=()):
    shape, width = (height, right[0].shape[2]), right[0].shape[2]
    own, *sends = call(
        functools.partial(near_grad_kernel, place.shards),
        place.where,
        [*left, *right],
        [like(shape, f32)] + [like(shape, bf16)] * (place.shards - 1),
        scratch=[pltpu.VMEM((place.shards, height, width), f32)],
        after=after,
        cost=2.0,
    )
    return [own] + [
        place.permute(send, lambda s, p, c, d=d: (s - d - 1, p)) for d, send in enumerate(sends)
    ]


def halve_kernel(counts, heights, where, *refs):
    kept, sent = refs[-2:]
    at, totals = 0, []
    for count in counts:
        total = refs[at][...]
        for ref in refs[at + 1 : at + count]:
            total = total + ref[...].astype(f32)
        at += count
        totals.append(total)
    if len(totals) == 1:
        total, totals, row = totals[0], [], 0
        for height in heights:
            totals.append(total[row : row + height])
            row += height
    bit = where[SUM + 1]

    def fill(side):
        row = 0
        for total, height in zip(totals, heights):
            half = height // 2
            kept[row : row + half] = total[side * half : (side + 1) * half]
            sent[row : row + half] = total[(1 - side) * half : (2 - side) * half].astype(bf16)
            row += half

    for side in range(2):
        pl.when(bit == side)(functools.partial(fill, side))


def far_grad_kernel(shards, planes, where, left, left_other, right, right_other, *refs):
    *messages, sent, kept, grad = refs
    width = kept.shape[-1]
    size = left.shape[2]
    if len(messages) == 2:
        left_far, right_far = messages[0][...], messages[1][...]
    else:
        left_far, right_far = messages[0][:, :size], messages[0][:, size:]
    grad[...] = dot(
        jnp.concatenate([chip_factor(left, left_other, where[ACT]), left_far], axis=0),
        jnp.concatenate([chip_factor(right, right_other, where[CORE]), right_far], axis=0),
        0,
        0,
    )
    height = grad.shape[0] // shards // (planes // 2)

    def fill(bit):
        for k in range(grad.shape[1] // width):
            rows = slice(k * height, (k + 1) * height)
            for s in range(shards):
                for j in range(planes // 2):
                    side, rest = divmod(j, planes // 4)
                    row = (s * (planes // 2) + j) * height
                    block = grad[row : row + height, k * width : (k + 1) * width]
                    if side == bit:
                        kept[s, rest, rows] = block
                    else:
                        sent[s, rest, rows] = block.astype(bf16)

    for bit in range(2):
        pl.when(where[SUM] == bit)(functools.partial(fill, bit))


def total_kernel(shards, where, kept, got, *refs):
    if len(refs) > shards:
        *gains, own, own_gains = refs[:4]
        sends, found = refs[4:-1], refs[-1]
        size = found.shape[2]
        for i, gain in enumerate(gains):
            for s in range(shards):
                found[s, i : i + 1] = gain[:, s * size : (s + 1) * size]
        own_gains[...] = found[where[SHARD]]
    else:
        own, sends, found = refs[0], refs[1:], None
    shard, first = where[SHARD], sends[0].shape[0] - own.shape[0]
    own[...] = kept[shard, 0] + got[shard, 0].astype(f32)
    for d, send in enumerate(sends):
        row = lax.rem(shard + d + 1, shards)
        send[first:] = (kept[row, 0] + got[row, 0].astype(f32)).astype(bf16)
        if found is not None:
            send[:2, :size] = found[row].astype(bf16)


def far_grad(place, width, left, right, messages, gains=(), after=()):
    shards, planes = place.shards, place.planes
    rows, columns = left[0].shape[2], right[0].shape[2]
    total = rows // shards // (planes // 2) * (columns // width)
    packed = (shards, planes // 4, total, width)
    sent, kept = call(
        functools.partial(far_grad_kernel, shards, planes),
        place.where,
        [*left, *right, *messages],
        [like(packed, bf16), like(packed, f32)],
        scratch=[pltpu.VMEM((rows, columns), f32)],
        after=after,
        cost=3.0,
    )
    got = place.from_bit(sent, 1)
    for step in range(2, place.bits):
        whole = (kept + got.astype(f32)).reshape(shards, 2, -1, total, width)
        kept = pick(whole, place.bit(step), 1)
        got = place.from_bit(pick(whole, 1 - place.bit(step), 1).astype(bf16), step)
    outs, scratch = [like((total, width), f32)], []
    if gains:
        size = gains[0].shape[1] // shards
        outs.append(like((len(gains), size), f32))
        scratch.append(pltpu.VMEM((shards, len(gains), size), f32))
    own = call(
        functools.partial(total_kernel, shards),
        place.where,
        [kept, got, *gains],
        outs + [like((total + GAIN_ROWS * bool(gains), width), bf16)] * (shards - 1),
        scratch=scratch,
    )
    own, sends = list(own[: len(outs)]), own[len(outs) :]
    return own, [
        place.permute(send, lambda s, p, c, d=d: (s - d - 1, p)) for d, send in enumerate(sends)
    ], sent


def round_kernel(counts, first, where, *refs):
    out, at, row = refs[-1], 0, first
    for count in counts:
        total = refs[at][...]
        for ref in refs[at + 1 : at + count]:
            total = total + ref[first:].astype(f32)
        out[row : row + total.shape[0]] = total.astype(bf16)
        row += total.shape[0]
        at += count
    if first:
        total = refs[at][...]
        rows, columns = total.shape
        for ref in refs[1 : counts[0]]:
            total = total + ref[:rows, :columns].astype(f32)
        out[:rows, :columns] = total.astype(bf16)


def spread_kernel(orders, bits, first, heights, chunks, where, *refs):
    planes = 1 << bits
    mine, other, outs = refs[:planes], refs[planes : 2 * planes], refs[2 * planes :]
    width = mine[0].shape[-1]
    starts = []
    for order in orders:
        start = 0
        for step, at in enumerate(order):
            start = start + (((where[PLANE] >> at) & 1) << (bits - 1 - step))
        starts.append(start)

    def fill(core):
        arrays = (other, mine) if core else (mine, other)
        for p in range(planes):
            at = first
            for out, height, chunk in zip(outs, heights, chunks):
                for k in range(chunk):
                    rows = slice(at, at + height)
                    for side in range(2):
                        lanes = slice((side * chunk + k) * width, (side * chunk + k + 1) * width)
                        out[p ^ starts[side], :, lanes] = arrays[side][p][rows].astype(f32)
                    at += height
            if first:
                rows, columns = outs[-2].shape
                for side in range(2):
                    outs[-1][side, p ^ starts[side]] = arrays[side][p][:rows, :columns].astype(f32)

    for core in range(2):
        pl.when(where[CORE] == core)(functools.partial(fill, core))
    if first:
        total = 0.0
        for side in range(2):
            for p in range(planes):
                total = total + outs[-1][side, p]
        outs[-2][...] = total


def spread_grads(place, width, groups, heights, chunks, gains=None):
    planes = place.planes
    first = 0 if gains is None else GAIN_ROWS
    total = sum(height * chunk for height, chunk in zip(heights, chunks))
    extra = [] if gains is None else [gains]
    mine = list(
        call(
            functools.partial(round_kernel, [len(group) for group in groups], first),
            place.where,
            [array for group in groups for array in group] + extra,
            [like((first + total, width), bf16)],
        )
    )
    for step in reversed(range(place.bits)):
        mine = mine + [place.from_bit(array, step) for array in mine]
    other = [place.from_core(array) for array in mine]
    outs = call(
        functools.partial(spread_kernel, place.orders, place.bits, first, heights, chunks),
        place.where,
        mine + other,
        [
            like((planes, height, 2 * chunk * width), f32)
            for height, chunk in zip(heights, chunks)
        ]
        + [like(array.shape, f32) for array in extra],
        scratch=[pltpu.VMEM((2, planes) + array.shape, f32) for array in extra],
        cost=2.0,
    )
    count = len(heights)
    return [out.reshape(-1, out.shape[2]) for out in outs[:count]], list(outs[count:])


def body(
    shards,
    reps,
    tokens,
    segment_ids,
    attn_gain,
    qkv_weight,
    attn_out_weight,
    mlp_gain,
    in_weight,
    out_weight,
    cotangent,
):
    place = Place(shards, reps)
    where = place.where
    tokens, segments, cotangent = tokens[0], segment_ids[0], cotangent[0]
    length, model = tokens.shape
    heads, size = model // HD, out_weight.shape[0] * shards
    width = model // 2
    rows = lambda columns, kind=bf16: like((length, columns), kind)
    halves = lambda columns: like((2, length, columns // 2), bf16)
    padded = like((2, length, -(-size // 2 // 128) * 128), bf16)

    (weight_qkv,), (gain_attn, gain_mlp), (free, through) = gather_weights(
        place, [qkv_weight], width, gains=jnp.stack([attn_gain, mlp_gain])
    )
    (weight_attn, weight_in), _, (free, through) = gather_weights(
        place, [attn_out_weight, in_weight], width, after=[free], between=[through]
    )
    (weight_out,), _, _ = gather_weights(
        place, [out_weight], width, after=[free], between=[through]
    )

    across, down = segments[:, None], segments[None, :]
    normed_one, one_parts, cotangent_halves, cotangent_sent, cosine, sine = call(
        functools.partial(start_kernel, shards),
        where,
        [tokens, gain_attn, cotangent, across, down],
        [rows(model), halves(model), halves(model), rows(width)] + [rows(PAIR, f32)] * 2,
        cost=2.0,
    )
    cotangent_factor = (cotangent_halves, place.from_core(cotangent_sent))
    one_factor = (one_parts, place.from_core(one_parts))
    _, one_arrived = send_factors(place, [one_factor])

    queries, keys, values, attended, attended_parts, probs = call(
        functools.partial(attend_kernel, shards),
        where,
        [normed_one, weight_qkv, cosine, sine, across, down],
        [rows(model)] * 4 + [halves(model), like((heads, length, length), f32)],
        scratch=[pltpu.VMEM((length, 3 * model), f32)],
        after=[one_arrived, cotangent_factor[1]],
        cost=5.0,
    )
    attended_factor = (attended_parts, place.from_core(attended_parts))
    middle, two_parts, by_gate, by_up, hidden, hidden_parts = call(
        functools.partial(hidden_kernel, shards),
        where,
        [tokens, attended, weight_attn, gain_mlp, weight_in],
        [rows(model, f32), halves(model), rows(size, f32), rows(size, f32), rows(size), padded],
        after=[attended_factor[1]],
        cost=4.0,
    )
    two_factor = (two_parts, place.from_core(two_parts))
    hidden_factor = (hidden_parts, place.from_core(hidden_parts))
    out_group = near_grad(place, hidden_factor, cotangent_factor, size // shards)
    output, gate_up_halves, gate_up_sent = call(
        output_kernel,
        where,
        [middle, hidden, weight_out, cotangent, by_gate, by_up],
        [rows(model), halves(2 * size), rows(size)],
        after=[out_group[0]],
        cost=4.0,
    )
    gate_up_factor = (gate_up_halves, place.from_core(gate_up_sent))
    message, in_arrived = send_factors(place, [two_factor, gate_up_factor])
    grad_middle, low_halves, low_sent, grad_attended, mlp_gain_part = call(
        middle_kernel,
        where,
        [gate_up_halves, weight_in, middle, gain_mlp, cotangent, weight_attn],
        [rows(model, f32), halves(model), rows(width), rows(model), like((1, model), f32)],
        after=[message],
        cost=4.0,
    )
    low_factor = (low_halves, place.from_core(low_sent))
    projected_halves, projected_sent = call(
        attend_back_kernel,
        where,
        [grad_attended, queries, keys, values, probs, cosine, sine],
        [halves(3 * model), rows(3 * model // 2)],
        cost=5.0,
    )
    projected_factor = (projected_halves, place.from_core(projected_sent))
    message, projected_arrived = send_factors(place, [projected_factor])
    in_own, in_got, in_sent = far_grad(
        place, width, two_factor, gate_up_factor, [in_arrived], after=[message]
    )
    attn_group = near_grad(place, attended_factor, low_factor, model // shards, after=[in_sent])
    grad_tokens, attn_gain_part = call(
        tokens_kernel,
        where,
        [projected_halves, weight_qkv, tokens, gain_attn, grad_middle],
        [rows(model, f32), like((1, model), f32)],
        after=[attn_group[0]],
        cost=4.0,
    )
    (qkv_own, gains), qkv_got, _ = far_grad(
        place,
        width,
        one_factor,
        projected_factor,
        [one_arrived, projected_arrived],
        gains=[attn_gain_part, mlp_gain_part],
    )
    groups, heights = [attn_group, out_group], [model // shards, size // shards]
    for step in range(place.bits):
        total = sum(heights) // 2
        kept, sent = call(
            functools.partial(halve_kernel, [len(group) for group in groups], heights),
            jnp.concatenate([where, place.bit(step).astype(jnp.int32)[None]]),
            [array for group in groups for array in group],
            [like((total, width), f32), like((total, width), bf16)],
        )
        groups, heights = [[kept, place.from_bit(sent, step)]], [h // 2 for h in heights]
    chunks = [size // width, 1, 1]
    heights = [model // shards // place.planes] + heights
    (in_weight_g, attn_out_g, out_weight_g), _ = spread_grads(
        place, width, [in_own + in_got] + groups, heights, chunks
    )
    (qkv_weight_g,), (gains_g,) = spread_grads(
        place,
        width,
        [[qkv_own] + qkv_got],
        [model // shards // place.planes],
        [3 * model // 2 // width],
        gains=gains,
    )
    return (
        output[None],
        grad_tokens[None],
        gains_g[0],
        qkv_weight_g,
        attn_out_g,
        gains_g[1],
        in_weight_g,
        out_weight_g,
    )


def solution(mesh):
    return jax.shard_map(
        functools.partial(body, mesh.shape["shard"], mesh.shape["rep"]),
        mesh=mesh,
        in_specs=(
            P(("rep", "shard"), None, None),
            P(("rep", "shard"), None),
            P("shard"),
            P("shard", None),
            P("shard", None),
            P("shard"),
            P("shard", None),
            P("shard", None),
            P(("rep", "shard"), None, None),
        ),
        out_specs=(
            P(("rep", "shard"), None, None),
            P(("rep", "shard"), None, None),
            P("shard"),
            P("shard", None),
            P("shard", None),
            P("shard"),
            P("shard", None),
            P("shard", None),
        ),
        check_vma=False,
    )
```

```python
import functools
import math

import jax
import jax.numpy as jnp
from jax import lax
from jax.experimental import pallas as pl
from jax.experimental.pallas import tpu as pltpu
from jax.sharding import PartitionSpec as P

HD = 64
PAIR = 2 * HD


rope_base = 160000.0
epsilon = 1e-05
VMEM = pl.BlockSpec(memory_space=pltpu.VMEM)
SMEM = pl.BlockSpec(memory_space=pltpu.SMEM)
ANY = pl.BlockSpec(memory_space=pl.ANY)
SHARD, PLANE, CORE, ACT, SUM = range(5)
GAIN_ROWS = 16
f32, bf16 = jnp.float32, jnp.bfloat16


def like(shape, dtype):
    return jax.ShapeDtypeStruct(tuple(shape), dtype)


def padded_bytes(array):
    *lead, rows, columns = array.shape
    tile = 8 * 4 // array.dtype.itemsize
    return (
        math.prod(lead) * -(-rows // tile) * tile * -(-columns // 128) * 128 * array.dtype.itemsize
    )


def call(kernel, where, operands, outs, scratch=(), after=(), cost=1.0):
    count, late = len(operands), len(operands) + len(after)
    room = sum(padded_bytes(array) for array in [*operands, *outs, *scratch])

    def inner(where_ref, *refs):
        kernel(where_ref, *refs[:count], *refs[late:])

    return pl.pallas_call(
        inner,
        out_shape=list(outs),
        in_specs=[SMEM] + [VMEM] * count + [ANY] * len(after),
        out_specs=[VMEM] * len(outs),
        scratch_shapes=list(scratch),
        compiler_params=pltpu.CompilerParams(vmem_limit_bytes=room + 6 * 2**20),
        cost_estimate=pl.CostEstimate(
            flops=int(cost * 1.1e9), bytes_accessed=0, transcendentals=0
        ),
    )(where, *operands, *after)


class Place:
    def __init__(self, shards, reps):
        self.shards, self.planes = shards, reps // 2
        self.bits = self.planes.bit_length() - 1
        if self.planes != 1 << self.bits or self.bits % 2 or shards % 2:
            raise ValueError("mesh sizes")
        pairs = range(0, self.bits, 2)
        self.orders = tuple([i + k for i in pairs for k in turn] for turn in ((0, 1), (1, 0)))
        rep = lax.axis_index("rep")
        self.shard, self.plane, self.core = lax.axis_index("shard"), rep // 2, rep % 2
        self.first = self.core == 0
        self.where = jnp.stack(
            [self.shard, self.plane, self.core, self.bit(0), self.bit(1)]
        ).astype(jnp.int32)

    def permute(self, array, source):
        flat = lambda s, p, c: (2 * p + c) * self.shards + s
        pairs = []
        for p in range(self.planes):
            for c in range(2):
                for s in range(self.shards):
                    from_s, from_p = source(s, p, c)
                    pairs.append((flat(from_s % self.shards, from_p, c), flat(s, p, c)))
        return lax.ppermute(array, ("rep", "shard"), pairs)

    def from_core(self, array):
        return lax.ppermute(array, "rep", [(r, r ^ 1) for r in range(2 * self.planes)])

    def from_bit(self, array, step):
        return self.permute(array, lambda s, p, c: (s, p ^ (1 << self.orders[c][step])))

    def bit(self, step):
        at = jnp.where(self.first, self.orders[0][step], self.orders[1][step])
        return (self.plane >> at) & 1

    def both(self, mine, other):
        return jnp.where(self.first, mine, other), jnp.where(self.first, other, mine)


def pick(array, index, axis=0):
    return lax.dynamic_index_in_dim(array, index, axis, keepdims=False)


def segments(blocks, width, height):
    found, at = [], 0
    for number, block in enumerate(blocks):
        for k in range(block.shape[2] // width):
            row, left = 0, block.shape[1]
            while left:
                rows = min(left, height - at % height)
                lanes = slice(k * width, (k + 1) * width)
                found.append((at // height, at % height, number, lanes, row, rows))
                at, row, left = at + rows, row + rows, left - rows
    return found


def piece_kernel(width, with_gains, where, *refs):
    blocks, piece, part = refs[:-2], refs[-2], refs[-1]
    if with_gains:
        *blocks, gains = blocks
        rows, columns = gains.shape
        piece[piece.shape[0] - 1, :rows, :columns] = gains[...]
        part[part.shape[0] - 1, :rows, :columns] = gains[...]
    more = part.shape[0] - with_gains
    less = piece.shape[0] - with_gains - more
    for chunk, first, number, lanes, row, rows in segments(blocks, width, piece.shape[1]):
        piece[chunk, first : first + rows] = blocks[number][where[PLANE], row : row + rows, lanes]
    for i in range(more):
        part[i] = piece[i + less * where[CORE]]


def column_kernel(shards, with_gains, where, *refs):
    count = shards // 2
    mine, other = refs[:count], refs[count : 2 * count]
    refs = refs[2 * count :]
    gains = None
    if with_gains:
        gains, refs = refs[0], refs[1:]
    ahead, behind = refs[:2]
    more, less = ahead.shape[2], behind.shape[2]

    def fill(core):
        near, far = (other, mine) if core else (mine, other)
        first, second = (other[-1], mine[-1]) if core else (mine[-1], other[-1])

        def put(out, i, k):
            for d in range(1, count):
                out[0, d - 1, i] = near[d - 1][k]
                out[0, shards - d - 1, i] = far[d - 1][k]
            out[0, count - 1, i] = first[k] if k < more else second[k - less]

        for i in range(more):
            put(ahead, i, i + less * core)
        for i in range(less):
            put(behind, i, i if core else i + more)
        if with_gains:
            found = refs[-1]
            rows, columns = gains.shape
            found[where[SHARD]] = gains[...].astype(f32)

            def keep(d, value):
                found[lax.rem(where[SHARD] + d, shards)] = value[:rows, :columns].astype(f32)

            for d in range(1, count):
                keep(d, near[d - 1][more + less])
                keep(shards - d, far[d - 1][more + less])
            keep(count, mine[-1][more])

    for core in range(2):
        pl.when(where[CORE] == core)(functools.partial(fill, core))
    if with_gains:
        found = refs[-1]
        size = found.shape[2]
        for i, out in enumerate(refs[2:-1]):
            for s in range(shards):
                out[:, s * size : (s + 1) * size] = found[s, i : i + 1]


def pass_kernel(where, *refs):
    half = len(refs) // 2
    for source, out in zip(refs[:half], refs[half:]):
        out[...] = source[...]


def join_kernel(shards, where, *refs):
    count = (len(refs) - 8) // 2
    owns, outs = refs[:count], refs[count + 8 :]
    ahead, behind, mine_a, mine_b, mine_far, other_a, other_b, other_far = refs[
        count : count + 8
    ]
    inner, more, height, width = ahead.shape[0], ahead.shape[2], *ahead.shape[3:]
    less = behind.shape[2]
    shard, plane = where[SHARD], where[PLANE]
    for own, out in zip(owns, outs):
        out[shard] = own[...]

    def fill(core):
        mine, other = (mine_a, mine_b), (other_a, other_b)
        low, high = (other, mine) if core else (mine, other)
        far = (other_far, mine_far) if core else (mine_far, other_far)

        def put(d, i, chunk, first, number, lanes, row, rows):
            def read(pair, order):
                early = chunk < more if order == 0 else chunk >= less
                at = chunk - less * order if early else chunk - more * (1 - order)
                return pair[0 if early else 1][i, d, at, first : first + rows]

            out, shard_at = outs[number], lax.rem(shard + d + 1, shards)
            spot = slice(row, row + rows)
            out[shard_at, plane ^ i, spot, lanes] = read((ahead, behind), core)
            out[shard_at, plane ^ (inner + i), spot, lanes] = read(low, 0)
            out[shard_at, plane ^ (2 * inner + i), spot, lanes] = read(high, 1)
            at = chunk if chunk < more else chunk - less
            source = far[0 if chunk < more else 1]
            out[shard_at, plane ^ (3 * inner + i), spot, lanes] = source[
                i, d, at, first : first + rows
            ]

        for d in range(shards - 1):
            for i in range(inner):
                for segment in segments(owns, width, height):
                    put(d, i, *segment)

    for core in range(2):
        pl.when(where[CORE] == core)(functools.partial(fill, core))


def pieces(place, weights, width, gains=None):
    blocks = [weight.reshape(place.planes, -1, weight.shape[1]) for weight in weights]
    height = min(block.shape[1] for block in blocks)
    total = sum(block.shape[1] * block.shape[2] for block in blocks) // width // height
    extra = [] if gains is None else [gains]
    piece, part = call(
        functools.partial(piece_kernel, width, len(extra)),
        place.where,
        blocks + extra,
        [
            like((total + len(extra), height, width), bf16),
            like(((total + 1) // 2 + len(extra), height, width), bf16),
        ],
    )
    return blocks, extra, total, piece, part


def from_shards(place, piece, part):
    found = [
        place.permute(piece, lambda s, p, c, d=d: (s - d if c else s + d, p))
        for d in range(1, place.shards // 2)
    ]
    return found + [place.permute(part, lambda s, p, c: (s + place.shards // 2, p))]


def hold(place, arrays, after):
    outs = [like(array.shape, array.dtype) for array in arrays]
    return list(call(pass_kernel, place.where, arrays, outs, after=after))


def finish_gather(place, blocks, extra, total, mine, after=(), relay=(), late=()):
    shards = place.shards
    height, width = mine[-1].shape[1:]
    less, more = total // 2, (total + 1) // 2
    with_gains = len(extra)
    other = [place.from_core(array) for array in mine]
    outs = [like((1, shards - 1, count, height, width), bf16) for count in (more, less)]
    scratch = []
    if extra:
        count, size = extra[0].shape
        outs = outs + [like((1, shards * size), f32)] * count
        scratch = [pltpu.VMEM((shards, count, size), f32)]
    ahead, behind, *gains = call(
        functools.partial(column_kernel, shards, with_gains),
        place.where,
        mine + other + extra,
        outs,
        scratch=scratch,
        after=after,
    )
    for level in range(0, place.bits, 2):
        mine_a = place.from_bit(ahead, level)
        if relay:
            (mine_a,) = hold(place, [mine_a], after=relay)
        mine_far = place.from_bit(mine_a, level + 1)
        mine_b = place.from_bit(behind, level)
        other_a, other_far, other_b = (
            place.from_core(mine_a),
            place.from_core(mine_far),
            place.from_core(mine_b),
        )
        if level + 2 < place.bits:
            first = place.first
            join = lambda *parts: jnp.concatenate(parts, axis=2)
            whole = jnp.concatenate(
                [
                    jnp.where(first, join(ahead, behind), join(behind, ahead)),
                    jnp.where(first, join(mine_a, mine_b), join(other_a, other_b)),
                    jnp.where(first, join(other_b, other_a), join(mine_b, mine_a)),
                    jnp.where(
                        first,
                        join(mine_far, other_far[:, :, more - less :]),
                        join(other_far, mine_far[:, :, more - less :]),
                    ),
                ]
            )
            ahead = jnp.where(first, whole[:, :, :more], whole[:, :, less:])
            behind = jnp.where(first, whole[:, :, more:], whole[:, :, :less])
    wholes = call(
        functools.partial(join_kernel, shards),
        place.where,
        blocks + [ahead, behind, mine_a, mine_b, mine_far, other_a, other_b, other_far],
        [like((shards,) + block.shape, bf16) for block in blocks],
        after=late,
        cost=2.0,
    )
    wholes = [whole.reshape(-1, whole.shape[3]) for whole in wholes]
    return wholes, gains, [mine_a, mine_b, mine_far]


def lane_of(array):
    return lax.broadcasted_iota(jnp.int32, array.shape, len(array.shape) - 1)


def swap_halves(array):
    lane = lane_of(array)
    return jnp.where(
        lane % HD < HD // 2,
        pltpu.roll(array, PAIR - HD // 2, 1),
        pltpu.roll(array, HD // 2, 1),
    )


def only(array, head):
    return jnp.where(lane_of(array) // HD == head, array, jnp.zeros_like(array))


def dot(left, right, left_axis=1, right_axis=0):
    return lax.dot_general(
        left, right, (((left_axis,), (right_axis,)), ((), ())), preferred_element_type=f32
    )


def normalise(values):
    centred = values - jnp.mean(values, axis=-1, keepdims=True)
    scale = lax.rsqrt(jnp.mean(centred * centred, axis=-1, keepdims=True) + epsilon)
    return centred * scale, scale


def norm_back(values, gain, grad):
    normal, scale = normalise(values)
    scaled = grad * gain
    inner = jnp.mean(scaled * normal, axis=-1, keepdims=True)
    back = scale * (scaled - jnp.mean(scaled, axis=-1, keepdims=True) - normal * inner)
    return back, jnp.sum(grad * normal, axis=0, keepdims=True)


def split_shards(array, out, shards):
    size = array.shape[1] // shards // 2
    for half in range(2):
        out[half, :, : shards * size] = jnp.concatenate(
            [array[:, (2 * s + half) * size : (2 * s + half + 1) * size] for s in range(shards)],
            axis=1,
        )


def start_kernel(
    shards, where, tokens, gain, cotangent, across, down, normed, parts, halves, sent, cosine, sine
):
    value = (normalise(tokens[...].astype(f32))[0] * gain[...]).astype(bf16)
    normed[...] = value
    split_shards(value, parts, shards)
    width = halves.shape[2]
    for half in range(2):
        halves[half] = cotangent[:, half * width : (half + 1) * width]
    sent[...] = halves[1 - where[CORE]]
    same = across[...] == down[...]
    before = lane_of(same) < lax.broadcasted_iota(jnp.int32, same.shape, 0)
    position = jnp.sum(jnp.where(same & before, 1.0, 0.0), axis=1, keepdims=True)
    lane = lax.broadcasted_iota(jnp.int32, cosine.shape, 1)
    frequency = jnp.exp((lane % (HD // 2)).astype(f32) * (-2.0 / HD * math.log(rope_base)))
    angles = position * frequency
    cosine[...] = jnp.cos(angles)
    turn = jnp.sin(angles)
    sine[...] = jnp.where(lane % HD < HD // 2, -turn, turn)


def attend_kernel(
    shards, where, normed, weight, cosine, sine, across, down, queries, keys, values, attended,
    parts, probs, projected,
):
    width = normed.shape[1]
    projected[...] = dot(normed[...], weight[...])
    same = across[...] == down[...]
    for pair in range(width // PAIR):
        lanes = slice(pair * PAIR, (pair + 1) * PAIR)

        def turned(start):
            vector = projected[:, start + pair * PAIR : start + (pair + 1) * PAIR]
            return (vector * cosine[...] + swap_halves(vector) * sine[...]).astype(bf16)

        query, key = turned(0), turned(width)
        value = projected[:, 2 * width + pair * PAIR : 2 * width + (pair + 1) * PAIR].astype(bf16)
        queries[:, lanes], keys[:, lanes], values[:, lanes] = query, key, value
        total = 0.0
        for head in range(2):
            scores = dot(only(query, head), key, 1, 1) * HD**-0.5
            scores = jnp.where(same, scores, -1000000000.0)
            exponent = jnp.exp(scores - jnp.max(scores, axis=-1, keepdims=True))
            prob = exponent / jnp.sum(exponent, axis=-1, keepdims=True)
            probs[2 * pair + head] = prob
            total = total + dot(prob.astype(bf16), only(value, head))
        attended[:, lanes] = total.astype(bf16)
    split_shards(attended[...], parts, shards)


def hidden_kernel(
    shards, where, tokens, attended, weight_attn, gain, weight_in, middle, normed_parts, by_gate,
    by_up, hidden, hidden_parts,
):
    value = tokens[...].astype(f32) + dot(attended[...], weight_attn[...])
    middle[...] = value
    normed = (normalise(value)[0] * gain[...]).astype(bf16)
    split_shards(normed, normed_parts, shards)
    size = hidden.shape[1]
    gate, up = dot(normed, weight_in[:, :size]), dot(normed, weight_in[:, size:])
    below = 0.5 * (1.0 + lax.erf(gate * math.sqrt(0.5)))
    active = gate * below
    by_up[...] = active
    by_gate[...] = up * (
        below + gate * jnp.exp(-0.5 * gate * gate) * (1.0 / math.sqrt(2.0 * math.pi))
    )
    low = (active * up).astype(bf16)
    hidden[...] = low
    split_shards(low, hidden_parts, shards)


def output_kernel(
    where, middle, hidden, weight_out, cotangent, by_gate, by_up, output, grad_halves, grad_kept,
    grad_sent,
):
    output[...] = (middle[...] + dot(hidden[...], weight_out[...])).astype(bf16)
    grad = dot(cotangent[...], weight_out[...], 1, 1).astype(bf16).astype(f32)
    grad_halves[0] = (grad * by_gate[...]).astype(bf16)
    grad_halves[1] = (grad * by_up[...]).astype(bf16)
    grad_kept[...] = grad_halves[where[CORE]]
    grad_sent[...] = grad_halves[1 - where[CORE]]


def middle_kernel(
    where, grad_halves, weight_in, middle, gain, cotangent, weight_attn, grad_middle, low_halves,
    low_sent, grad_attended, grad_gain,
):
    size = grad_halves.shape[2]
    grad = dot(grad_halves[0], weight_in[:, :size], 1, 1)
    grad = grad + dot(grad_halves[1], weight_in[:, size:], 1, 1)
    back, gain_part = norm_back(middle[...], gain[...], grad)
    grad_gain[...] = gain_part
    total = cotangent[...].astype(f32) + back
    grad_middle[...] = total
    low = total.astype(bf16)
    half = low.shape[1] // 2
    low_halves[0], low_halves[1] = low[:, :half], low[:, half:]
    low_sent[...] = low_halves[1 - where[CORE]]
    grad_attended[...] = dot(low, weight_attn[...], 1, 1).astype(bf16)


def attend_back_kernel(
    where, grad_attended, queries, keys, values, probs, cosine, sine, grad_halves, grad_kept,
    grad_sent,
):
    width = queries.shape[1]
    half = grad_halves.shape[2]

    def store(start, grad):
        side, rest = divmod(start, half)
        grad_halves[side, :, rest : rest + PAIR] = grad.astype(bf16)

    for pair in range(width // PAIR):
        lanes = slice(pair * PAIR, (pair + 1) * PAIR)
        query, key, value = queries[:, lanes], keys[:, lanes], values[:, lanes]
        above = grad_attended[:, lanes]
        by_query, by_key, by_value = 0.0, 0.0, 0.0
        for head in range(2):
            own = only(above, head)
            grad = dot(own, value, 1, 1)
            prob = probs[2 * pair + head]
            weighted = jnp.sum(prob * grad, axis=-1, keepdims=True)
            grad = (prob * (grad - weighted)).astype(bf16)
            by_query = by_query + dot(grad, only(key, head))
            by_key = by_key + dot(grad, only(query, head), 0, 0)
            by_value = by_value + dot(prob.astype(bf16), own, 0, 0)

        def back(grad):
            grad = grad * HD**-0.5
            return grad * cosine[...] - swap_halves(grad) * sine[...]

        store(pair * PAIR, back(by_query))
        store(width + pair * PAIR, back(by_key))
        store(2 * width + pair * PAIR, by_value)
    grad_kept[...] = grad_halves[where[CORE]]
    grad_sent[...] = grad_halves[1 - where[CORE]]


def tokens_kernel(where, grad_halves, weight, tokens, gain, grad_middle, grad_tokens, grad_gain):
    half = grad_halves.shape[2]
    grad = dot(grad_halves[0], weight[:, :half], 1, 1)
    grad = grad + dot(grad_halves[1], weight[:, half:], 1, 1)
    back, gain_part = norm_back(tokens[...].astype(f32), gain[...], grad)
    grad_gain[...] = gain_part
    grad_tokens[...] = grad_middle[...] + back


def message_kernel(where, own, other, out):
    rows = out.shape[0] // 2
    out[:rows] = own[1 - where[ACT]]
    out[rows:] = other[1 - where[ACT]]


def left_from_chip(place, left, after=()):
    _, rows, columns = left[0].shape
    (message,) = call(
        message_kernel, place.where, left, [like((2 * rows, columns), bf16)], after=after
    )
    return message, place.from_bit(message, 0)


def right_from_chip(place, kept, other):
    return place.from_bit(kept, 0), place.from_bit(other, 0)


def chip_factor(own, other, index):
    far = other[index] if len(other.shape) == 3 else other[...]
    return jnp.concatenate([own[index], far], axis=0)


def near_grad_kernel(shards, where, left, left_other, right, right_other, own, *refs):
    sends, grad = refs[:-1], refs[-1]
    height = grad.shape[1] // 2
    factor = chip_factor(right, right_other, where[CORE])
    for half in range(2):
        value = dot(chip_factor(left, left_other, half), factor, 0, 0)
        for s in range(shards):
            grad[s, half * height : (half + 1) * height] = value[s * height : (s + 1) * height]
    own[...] = grad[where[SHARD]]
    for d, send in enumerate(sends):
        send[...] = grad[lax.rem(where[SHARD] + d + 1, shards)].astype(bf16)


def near_grad(place, left, right, height, after=()):
    shape, width = (height, right[0].shape[2]), right[0].shape[2]
    own, *sends = call(
        functools.partial(near_grad_kernel, place.shards),
        place.where,
        [*left, *right],
        [like(shape, f32)] + [like(shape, bf16)] * (place.shards - 1),
        scratch=[pltpu.VMEM((place.shards, height, width), f32)],
        after=after,
        cost=2.0,
    )
    return [own] + [
        place.permute(send, lambda s, p, c, d=d: (s - d - 1, p)) for d, send in enumerate(sends)
    ]


def halve_kernel(counts, heights, where, *refs):
    kept, sent = refs[-2:]
    at, totals = 0, []
    for count in counts:
        total = refs[at][...]
        for ref in refs[at + 1 : at + count]:
            total = total + ref[...].astype(f32)
        at += count
        totals.append(total)
    if len(totals) == 1:
        total, totals, row = totals[0], [], 0
        for height in heights:
            totals.append(total[row : row + height])
            row += height
    bit = where[SUM + 1]

    def fill(side):
        row = 0
        for total, height in zip(totals, heights):
            half = height // 2
            kept[row : row + half] = total[side * half : (side + 1) * half]
            sent[row : row + half] = total[(1 - side) * half : (2 - side) * half].astype(bf16)
            row += half

    for side in range(2):
        pl.when(bit == side)(functools.partial(fill, side))


def chip_grad_kernel(where, left, left_other, right, right_other, kept, sent):
    factor = chip_factor(right, right_other, where[CORE])
    kept[...] = dot(chip_factor(left, left_other, where[ACT]), factor, 0, 0)
    sent[...] = dot(chip_factor(left, left_other, 1 - where[ACT]), factor, 0, 0).astype(bf16)


def far_grad_kernel(shards, planes, where, *refs):
    left, left_other, left_far = refs[:3]
    rights = refs[3:7]
    along, (sent, kept, grad) = refs[7:-3], refs[-3:]
    width = kept.shape[-1]
    grad[...] = dot(
        jnp.concatenate([chip_factor(left, left_other, where[ACT]), left_far[...]], axis=0),
        jnp.concatenate([right[...] for right in rights], axis=0),
        0,
        0,
    )
    height = grad.shape[0] // shards // (planes // 2)
    chunks = grad.shape[1] // width

    def block(row, k):
        rows = slice(row, row + height)
        if k == chunks:
            return along[0][rows] + along[1][rows].astype(f32)
        return grad[rows, k * width : (k + 1) * width]

    def fill(bit):
        for k in range(chunks + bool(along)):
            rows = slice(k * height, (k + 1) * height)
            for s in range(shards):
                for j in range(planes // 2):
                    side, rest = divmod(j, planes // 4)
                    value = block((s * (planes // 2) + j) * height, k)
                    if side == bit:
                        kept[s, rest, rows] = value
                    else:
                        sent[s, rest, rows] = value.astype(bf16)

    for bit in range(2):
        pl.when(where[SUM] == bit)(functools.partial(fill, bit))


def total_kernel(shards, where, kept, got, *refs):
    if len(refs) > shards:
        *gains, own, own_gains = refs[:4]
        sends, found = refs[4:-1], refs[-1]
        size = found.shape[2]
        for i, gain in enumerate(gains):
            for s in range(shards):
                found[s, i : i + 1] = gain[:, s * size : (s + 1) * size]
        own_gains[...] = found[where[SHARD]]
    else:
        own, sends, found = refs[0], refs[1:], None
    shard, first = where[SHARD], sends[0].shape[0] - own.shape[0]
    own[...] = kept[shard, 0] + got[shard, 0].astype(f32)
    for d, send in enumerate(sends):
        row = lax.rem(shard + d + 1, shards)
        send[first:] = (kept[row, 0] + got[row, 0].astype(f32)).astype(bf16)
        if found is not None:
            send[:2, :size] = found[row].astype(bf16)


def far_grad(place, width, left, rights, along=(), after=()):
    shards, planes = place.shards, place.planes
    rows, columns = left[0].shape[2], rights[0].shape[1]
    total = rows // shards // (planes // 2) * (columns // width + bool(along))
    packed = (shards, planes // 4, total, width)
    sent, kept = call(
        functools.partial(far_grad_kernel, shards, planes),
        place.where,
        [*left, *rights, *along],
        [like(packed, bf16), like(packed, f32)],
        scratch=[pltpu.VMEM((rows, columns), f32)],
        after=after,
        cost=2.0,
    )
    got = place.from_bit(sent, 1)
    for step in range(2, place.bits):
        whole = (kept + got.astype(f32)).reshape(shards, 2, -1, total, width)
        kept = pick(whole, place.bit(step), 1)
        got = place.from_bit(pick(whole, 1 - place.bit(step), 1).astype(bf16), step)
    return kept, sent, got


def shard_sums(place, kept, got, gains=(), after=()):
    shards, (_, _, total, width) = place.shards, kept.shape
    outs, scratch = [like((total, width), f32)], []
    if gains:
        size = gains[0].shape[1] // shards
        outs.append(like((len(gains), size), f32))
        scratch.append(pltpu.VMEM((shards, len(gains), size), f32))
    own = call(
        functools.partial(total_kernel, shards),
        place.where,
        [kept, got, *gains],
        outs + [like((total + GAIN_ROWS * bool(gains), width), bf16)] * (shards - 1),
        scratch=scratch,
        after=after,
    )
    own, sends = list(own[: len(outs)]), own[len(outs) :]
    return own, [
        place.permute(send, lambda s, p, c, d=d: (s - d - 1, p)) for d, send in enumerate(sends)
    ]


def round_kernel(counts, first, where, *refs):
    out, at, row = refs[-1], 0, first
    for count in counts:
        total = refs[at][...]
        for ref in refs[at + 1 : at + count]:
            total = total + ref[first:].astype(f32)
        out[row : row + total.shape[0]] = total.astype(bf16)
        row += total.shape[0]
        at += count
    if first:
        total = refs[at][...]
        rows, columns = total.shape
        for ref in refs[1 : counts[0]]:
            total = total + ref[:rows, :columns].astype(f32)
        out[:rows, :columns] = total.astype(bf16)


def place_kernel(orders, bits, first, heights, chunks, where, whole, *outs):
    planes = 1 << bits
    width = whole.shape[-1]
    for plane in range(planes):
        for side in range(2):
            part = whole.at[2 * plane + side]
            spot = sum(
                ((plane >> at) & 1) << (bits - 1 - step) for step, at in enumerate(orders[side])
            )
            row = first
            for out, height, chunk in zip(outs, heights, chunks):
                for k in range(chunk):
                    lanes = slice((side * chunk + k) * width, (side * chunk + k + 1) * width)
                    out[spot, :, lanes] = part[row : row + height].astype(f32)
                    row += height
    if first:
        rows, columns = outs[-1].shape
        total = 0.0
        for rep in range(2 * planes):
            total = total + whole[rep, :rows, :columns].astype(f32)
        outs[-1][...] = total


def spread_kernel(orders, bits, first, heights, chunks, where, *refs):
    planes = 1 << bits
    mine, other, outs = refs[:planes], refs[planes : 2 * planes], refs[2 * planes :]
    width = mine[0].shape[-1]
    starts = []
    for order in orders:
        start = 0
        for step, at in enumerate(order):
            start = start + (((where[PLANE] >> at) & 1) << (bits - 1 - step))
        starts.append(start)

    def fill(core):
        arrays = (other, mine) if core else (mine, other)
        for p in range(planes):
            at = first
            for out, height, chunk in zip(outs, heights, chunks):
                for k in range(chunk):
                    rows = slice(at, at + height)
                    for side in range(2):
                        lanes = slice((side * chunk + k) * width, (side * chunk + k + 1) * width)
                        out[p ^ starts[side], :, lanes] = arrays[side][p][rows].astype(f32)
                    at += height
            if first:
                rows, columns = outs[-2].shape
                for side in range(2):
                    outs[-1][side, p ^ starts[side]] = arrays[side][p][:rows, :columns].astype(f32)

    for core in range(2):
        pl.when(where[CORE] == core)(functools.partial(fill, core))
    if first:
        total = 0.0
        for side in range(2):
            for p in range(planes):
                total = total + outs[-1][side, p]
        outs[-2][...] = total


def spread_grads(place, width, groups, heights, chunks, gains=None, after=(), at_once=False):
    planes = place.planes
    first = 0 if gains is None else GAIN_ROWS
    total = sum(height * chunk for height, chunk in zip(heights, chunks))
    extra = [] if gains is None else [gains]
    mine = list(
        call(
            functools.partial(round_kernel, [len(group) for group in groups], first),
            place.where,
            [array for group in groups for array in group] + extra,
            [like((first + total, width), bf16)],
            after=after,
        )
    )
    part = mine[0]
    if at_once:
        outs = call(
            functools.partial(place_kernel, place.orders, place.bits, first, heights, chunks),
            place.where,
            [lax.all_gather(part, "rep")],
            [
                like((planes, height, 2 * chunk * width), f32)
                for height, chunk in zip(heights, chunks)
            ]
            + [like(array.shape, f32) for array in extra],
            cost=2.0,
        )
        count = len(heights)
        return [out.reshape(-1, out.shape[2]) for out in outs[:count]], list(outs[count:]), part
    for step in reversed(range(place.bits)):
        mine = mine + [place.from_bit(array, step) for array in mine]
    other = [place.from_core(array) for array in mine]
    outs = call(
        functools.partial(spread_kernel, place.orders, place.bits, first, heights, chunks),
        place.where,
        mine + other,
        [
            like((planes, height, 2 * chunk * width), f32)
            for height, chunk in zip(heights, chunks)
        ]
        + [like(array.shape, f32) for array in extra],
        scratch=[pltpu.VMEM((2, planes) + array.shape, f32) for array in extra],
        cost=2.0,
    )
    count = len(heights)
    return [out.reshape(-1, out.shape[2]) for out in outs[:count]], list(outs[count:]), part


def body(
    shards,
    reps,
    tokens,
    segment_ids,
    attn_gain,
    qkv_weight,
    attn_out_weight,
    mlp_gain,
    in_weight,
    out_weight,
    cotangent,
):
    place = Place(shards, reps)
    where = place.where
    tokens, documents, cotangent = tokens[0], segment_ids[0], cotangent[0]
    length, model = tokens.shape
    heads, size = model // HD, out_weight.shape[0] * shards
    width = model // 2
    rows = lambda columns, kind=bf16: like((length, columns), kind)
    halves = lambda columns: like((2, length, columns // 2), bf16)
    padded = like((2, length, -(-size // 2 // 128) * 128), bf16)

    *first, piece, part = pieces(
        place, [qkv_weight], width, gains=jnp.stack([attn_gain, mlp_gain])
    )
    *second, later_piece, later_part = pieces(
        place, [attn_out_weight, in_weight, out_weight], width
    )
    later = from_shards(place, later_piece, later_part)
    (weight_qkv,), (gain_attn, gain_mlp), through = finish_gather(
        place,
        *first,
        from_shards(place, piece, part),
        after=[later_piece],
        relay=later[:-1],
    )
    later = hold(place, later, after=through)

    across, down = documents[:, None], documents[None, :]
    normed_one, one_parts, cotangent_halves, cotangent_sent, cosine, sine = call(
        functools.partial(start_kernel, shards),
        where,
        [tokens, gain_attn, cotangent, across, down],
        [rows(model), halves(model), halves(model), rows(width)] + [rows(PAIR, f32)] * 2,
        cost=2.0,
    )
    cotangent_factor = (cotangent_halves, place.from_core(cotangent_sent))
    one_factor = (one_parts, place.from_core(one_parts))
    one_factor = one_factor + left_from_chip(place, one_factor)[1:]

    queries, keys, values, attended, attended_parts, probs = call(
        functools.partial(attend_kernel, shards),
        where,
        [normed_one, weight_qkv, cosine, sine, across, down],
        [rows(model)] * 4 + [halves(model), like((heads, length, length), f32)],
        scratch=[pltpu.VMEM((length, 3 * model), f32)],
        after=[cotangent_factor[1]],
        cost=5.0,
    )
    attended_factor = (attended_parts, place.from_core(attended_parts))
    (weight_attn, weight_in, weight_out), _, _ = finish_gather(place, *second, later)
    middle, two_parts, by_gate, by_up, hidden, hidden_parts = call(
        functools.partial(hidden_kernel, shards),
        where,
        [tokens, attended, weight_attn, gain_mlp, weight_in],
        [rows(model, f32), halves(model), rows(size, f32), rows(size, f32), rows(size), padded],
        after=[attended_factor[1], one_factor[2]],
        cost=4.0,
    )
    two_factor = (two_parts, place.from_core(two_parts))
    hidden_factor = (hidden_parts, place.from_core(hidden_parts))
    out_group = near_grad(place, hidden_factor, cotangent_factor, size // shards)
    output, gate_up_halves, gate_up_kept, gate_up_sent = call(
        output_kernel,
        where,
        [middle, hidden, weight_out, cotangent, by_gate, by_up],
        [rows(model), halves(2 * size), rows(size), rows(size)],
        after=[out_group[0]],
        cost=3.0,
    )
    gate_up_other = place.from_core(gate_up_sent)
    message, two_far = left_from_chip(place, two_factor, after=[gate_up_kept])
    two_factor = two_factor + (two_far,)
    gate_up_far = right_from_chip(place, gate_up_kept, gate_up_other)
    grad_middle, low_halves, low_sent, grad_attended, mlp_gain_part = call(
        middle_kernel,
        where,
        [gate_up_halves, weight_in, middle, gain_mlp, cotangent, weight_attn],
        [rows(model, f32), halves(model), rows(width), rows(model), like((1, model), f32)],
        after=[gate_up_other, message],
        cost=3.0,
    )
    low_factor = (low_halves, place.from_core(low_sent))
    projected_halves, projected_kept, projected_sent = call(
        attend_back_kernel,
        where,
        [grad_attended, queries, keys, values, probs, cosine, sine],
        [halves(3 * model), rows(3 * width), rows(3 * width)],
        after=[gate_up_far[0], two_far],
        cost=3.0,
    )
    projected_other = place.from_core(projected_sent)
    projected_far = right_from_chip(place, projected_kept, projected_other)
    attn_kept, attn_sent = call(
        chip_grad_kernel,
        where,
        [*attended_factor, *low_factor],
        [like((width, width), f32), like((width, width), bf16)],
        after=[projected_other],
        cost=1.0,
    )
    attn_got = place.from_bit(attn_sent, 0)
    qkv_kept, qkv_sent, qkv_got = far_grad(
        place,
        width,
        one_factor,
        [projected_kept, projected_other, *projected_far],
        after=[attn_sent],
    )
    in_kept, in_sent, in_got = far_grad(
        place,
        width,
        two_factor,
        [gate_up_kept, gate_up_other, *gate_up_far],
        along=[attn_kept, attn_got],
        after=[qkv_sent],
    )
    grad_tokens, attn_gain_part = call(
        tokens_kernel,
        where,
        [projected_halves, weight_qkv, tokens, gain_attn, grad_middle],
        [rows(model, f32), like((1, model), f32)],
        after=[in_sent],
        cost=3.0,
    )
    (qkv_own, gains), qkv_arrived = shard_sums(
        place, qkv_kept, qkv_got, gains=[attn_gain_part, mlp_gain_part]
    )
    (in_own,), in_arrived = shard_sums(place, in_kept, in_got, after=[qkv_own])
    height = size // shards
    for step in range(place.bits):
        kept, sent = call(
            functools.partial(halve_kernel, [len(out_group)], [height]),
            jnp.concatenate([where, place.bit(step).astype(jnp.int32)[None]]),
            out_group,
            [like((height // 2, width), f32), like((height // 2, width), bf16)],
            after=[in_sent],
        )
        out_group, height = [kept, place.from_bit(sent, step)], height // 2
    part = model // shards // place.planes
    (qkv_weight_g,), (gains_g,), early = spread_grads(
        place, width, [[qkv_own, *qkv_arrived]], [part], [3 * model // 2 // width], gains=gains
    )
    (in_weight_g, attn_out_g, out_weight_g), _, _ = spread_grads(
        place,
        width,
        [[in_own, *in_arrived], out_group],
        [part, part, height],
        [size // width, 1, 1],
        after=[early],
    )
    return (
        output[None],
        grad_tokens[None],
        gains_g[0],
        qkv_weight_g,
        attn_out_g,
        gains_g[1],
        in_weight_g,
        out_weight_g,
    )


def solution(mesh):
    return jax.shard_map(
        functools.partial(body, mesh.shape["shard"], mesh.shape["rep"]),
        mesh=mesh,
        in_specs=(
            P(("rep", "shard"), None, None),
            P(("rep", "shard"), None),
            P("shard"),
            P("shard", None),
            P("shard", None),
            P("shard"),
            P("shard", None),
            P("shard", None),
            P(("rep", "shard"), None, None),
        ),
        out_specs=(
            P(("rep", "shard"), None, None),
            P(("rep", "shard"), None, None),
            P("shard"),
            P("shard", None),
            P("shard", None),
            P("shard"),
            P("shard", None),
            P("shard", None),
        ),
        check_vma=False,
    )
```

```python
import functools
import math

import jax
import jax.numpy as jnp
from jax import lax
from jax.experimental import pallas as pl
from jax.experimental.pallas import tpu as pltpu
from jax.sharding import PartitionSpec as P

HD = 64
PAIR = 2 * HD


rope_base = 160000.0
epsilon = 1e-05
VMEM = pl.BlockSpec(memory_space=pltpu.VMEM)
SMEM = pl.BlockSpec(memory_space=pltpu.SMEM)
ANY = pl.BlockSpec(memory_space=pl.ANY)
SHARD, PLANE, CORE, ACT, SUM = range(5)
GAIN_ROWS = 16
f32, bf16 = jnp.float32, jnp.bfloat16


def like(shape, dtype):
    return jax.ShapeDtypeStruct(tuple(shape), dtype)


def padded_bytes(array):
    *lead, rows, columns = array.shape
    tile = 8 * 4 // array.dtype.itemsize
    return (
        math.prod(lead) * -(-rows // tile) * tile * -(-columns // 128) * 128 * array.dtype.itemsize
    )


def call(kernel, where, operands, outs, scratch=(), after=(), cost=1.0):
    count, late = len(operands), len(operands) + len(after)
    room = sum(padded_bytes(array) for array in [*operands, *outs, *scratch])

    def inner(where_ref, *refs):
        kernel(where_ref, *refs[:count], *refs[late:])

    return pl.pallas_call(
        inner,
        out_shape=list(outs),
        in_specs=[SMEM] + [VMEM] * count + [ANY] * len(after),
        out_specs=[VMEM] * len(outs),
        scratch_shapes=list(scratch),
        compiler_params=pltpu.CompilerParams(vmem_limit_bytes=room + 6 * 2**20),
        cost_estimate=pl.CostEstimate(
            flops=int(cost * 1.1e9), bytes_accessed=0, transcendentals=0
        ),
    )(where, *operands, *after)


class Place:
    def __init__(self, shards, reps):
        self.shards, self.planes = shards, reps // 2
        self.bits = self.planes.bit_length() - 1
        if self.planes != 1 << self.bits or self.bits % 2 or shards % 2:
            raise ValueError("mesh sizes")
        pairs = range(0, self.bits, 2)
        self.orders = tuple([i + k for i in pairs for k in turn] for turn in ((0, 1), (1, 0)))
        rep = lax.axis_index("rep")
        self.shard, self.plane, self.core = lax.axis_index("shard"), rep // 2, rep % 2
        self.first = self.core == 0
        self.where = jnp.stack(
            [self.shard, self.plane, self.core, self.bit(0), self.bit(1)]
        ).astype(jnp.int32)

    def permute(self, array, source):
        flat = lambda s, p, c: (2 * p + c) * self.shards + s
        pairs = []
        for p in range(self.planes):
            for c in range(2):
                for s in range(self.shards):
                    from_s, from_p = source(s, p, c)
                    pairs.append((flat(from_s % self.shards, from_p, c), flat(s, p, c)))
        return lax.ppermute(array, ("rep", "shard"), pairs)

    def from_core(self, array):
        return lax.ppermute(array, "rep", [(r, r ^ 1) for r in range(2 * self.planes)])

    def from_bit(self, array, step):
        return self.permute(array, lambda s, p, c: (s, p ^ (1 << self.orders[c][step])))

    def bit(self, step):
        at = jnp.where(self.first, self.orders[0][step], self.orders[1][step])
        return (self.plane >> at) & 1

    def both(self, mine, other):
        return jnp.where(self.first, mine, other), jnp.where(self.first, other, mine)


def pick(array, index, axis=0):
    return lax.dynamic_index_in_dim(array, index, axis, keepdims=False)


def segments(blocks, width, height):
    found, at = [], 0
    for number, block in enumerate(blocks):
        for k in range(block.shape[2] // width):
            row, left = 0, block.shape[1]
            while left:
                rows = min(left, height - at % height)
                lanes = slice(k * width, (k + 1) * width)
                found.append((at // height, at % height, number, lanes, row, rows))
                at, row, left = at + rows, row + rows, left - rows
    return found


def piece_kernel(width, with_gains, where, *refs):
    blocks, piece, part = refs[:-2], refs[-2], refs[-1]
    if with_gains:
        *blocks, gains = blocks
        rows, columns = gains.shape
        piece[piece.shape[0] - 1, :rows, :columns] = gains[...]
        part[part.shape[0] - 1, :rows, :columns] = gains[...]
    more = part.shape[0] - with_gains
    less = piece.shape[0] - with_gains - more
    for chunk, first, number, lanes, row, rows in segments(blocks, width, piece.shape[1]):
        block = blocks[number]
        plane = lax.rem(where[PLANE], block.shape[0])
        piece[chunk, first : first + rows] = block[plane, row : row + rows, lanes]
    for i in range(more):
        part[i] = piece[i + less * where[CORE]]


def column_kernel(shards, with_gains, where, *refs):
    count = shards // 2
    mine, other = refs[:count], refs[count : 2 * count]
    refs = refs[2 * count :]
    gains = None
    if with_gains:
        gains, refs = refs[0], refs[1:]
    ahead, behind = refs[:2]
    more, less = ahead.shape[2], behind.shape[2]

    def fill(core):
        near, far = (other, mine) if core else (mine, other)
        first, second = (other[-1], mine[-1]) if core else (mine[-1], other[-1])

        def put(out, i, k):
            for d in range(1, count):
                out[0, d - 1, i] = near[d - 1][k]
                out[0, shards - d - 1, i] = far[d - 1][k]
            out[0, count - 1, i] = first[k] if k < more else second[k - less]

        for i in range(more):
            put(ahead, i, i + less * core)
        for i in range(less):
            put(behind, i, i if core else i + more)
        if with_gains:
            found = refs[-1]
            rows, columns = gains.shape
            found[where[SHARD]] = gains[...].astype(f32)

            def keep(d, value):
                found[lax.rem(where[SHARD] + d, shards)] = value[:rows, :columns].astype(f32)

            for d in range(1, count):
                keep(d, near[d - 1][more + less])
                keep(shards - d, far[d - 1][more + less])
            keep(count, mine[-1][more])

    for core in range(2):
        pl.when(where[CORE] == core)(functools.partial(fill, core))
    if with_gains:
        found = refs[-1]
        size = found.shape[2]
        for i, out in enumerate(refs[2:-1]):
            for s in range(shards):
                out[:, s * size : (s + 1) * size] = found[s, i : i + 1]


def pass_kernel(where, *refs):
    half = len(refs) // 2
    for source, out in zip(refs[:half], refs[half:]):
        out[...] = source[...]


def direct_kernel(shards, where, own, *refs):
    count = shards // 2
    mine, other, out = refs[:count], refs[count : 2 * count], refs[-1]
    total, half, width = mine[0].shape[0], mine[-1].shape[0], mine[0].shape[-1]
    out[where[SHARD]] = own[0]

    def fill(core):
        near, far = (other, mine) if core else (mine, other)
        middle = (other[-1], mine[-1]) if core else (mine[-1], other[-1])
        for k in range(2 * half):
            lanes = slice(k * width, (k + 1) * width)
            row = lambda d: lax.rem(where[SHARD] + d, shards)
            for d in range(1, count):
                out[row(d), :, lanes] = near[d - 1][k]
                out[row(shards - d), :, lanes] = far[d - 1][k]
            out[row(count), :, lanes] = middle[k // half][k % half]

    for core in range(2):
        pl.when(where[CORE] == core)(functools.partial(fill, core))


def join_kernel(shards, where, *refs):
    count = (len(refs) - 8) // 2
    owns, outs = refs[:count], refs[count + 8 :]
    ahead, behind, mine_a, mine_b, mine_far, other_a, other_b, other_far = refs[
        count : count + 8
    ]
    inner, more, height, width = ahead.shape[0], ahead.shape[2], *ahead.shape[3:]
    less = behind.shape[2]
    shard, plane = where[SHARD], where[PLANE]
    for own, out in zip(owns, outs):
        out[shard] = own[...]

    def fill(core):
        mine, other = (mine_a, mine_b), (other_a, other_b)
        low, high = (other, mine) if core else (mine, other)
        far = (other_far, mine_far) if core else (mine_far, other_far)

        def put(d, i, chunk, first, number, lanes, row, rows):
            def read(pair, order):
                early = chunk < more if order == 0 else chunk >= less
                at = chunk - less * order if early else chunk - more * (1 - order)
                return pair[0 if early else 1][i, d, at, first : first + rows]

            out, shard_at = outs[number], lax.rem(shard + d + 1, shards)
            spot = slice(row, row + rows)
            out[shard_at, plane ^ i, spot, lanes] = read((ahead, behind), core)
            out[shard_at, plane ^ (inner + i), spot, lanes] = read(low, 0)
            out[shard_at, plane ^ (2 * inner + i), spot, lanes] = read(high, 1)
            at = chunk if chunk < more else chunk - less
            source = far[0 if chunk < more else 1]
            out[shard_at, plane ^ (3 * inner + i), spot, lanes] = source[
                i, d, at, first : first + rows
            ]

        for d in range(shards - 1):
            for i in range(inner):
                for segment in segments(owns, width, height):
                    put(d, i, *segment)

    for core in range(2):
        pl.when(where[CORE] == core)(functools.partial(fill, core))


def pieces(place, weights, width, gains=None, after=(), planes=None):
    planes = planes or place.planes
    blocks = [weight.reshape(planes, -1, weight.shape[1]) for weight in weights]
    height = min(block.shape[1] for block in blocks)
    total = sum(block.shape[1] * block.shape[2] for block in blocks) // width // height
    extra = [] if gains is None else [gains]
    piece, part = call(
        functools.partial(piece_kernel, width, len(extra)),
        place.where,
        blocks + extra,
        [
            like((total + len(extra), height, width), bf16),
            like(((total + 1) // 2 + len(extra), height, width), bf16),
        ],
        after=after,
    )
    return blocks, extra, total, piece, part


def from_shards(place, piece, part):
    found = [
        place.permute(piece, lambda s, p, c, d=d: (s - d if c else s + d, p))
        for d in range(1, place.shards // 2)
    ]
    return found + [place.permute(part, lambda s, p, c: (s + place.shards // 2, p))]


def hold(place, arrays, after):
    outs = [like(array.shape, array.dtype) for array in arrays]
    return list(call(pass_kernel, place.where, arrays, outs, after=after))


def finish_direct(place, blocks, mine):
    other = [place.from_core(array) for array in mine]
    (whole,) = call(
        functools.partial(direct_kernel, place.shards),
        place.where,
        blocks + mine + other,
        [like((place.shards,) + blocks[0].shape[1:], bf16)],
        cost=2.0,
    )
    return whole.reshape(-1, whole.shape[2])


def finish_gather(place, blocks, extra, total, mine, after=(), relay=(), late=()):
    shards = place.shards
    height, width = mine[-1].shape[1:]
    less, more = total // 2, (total + 1) // 2
    with_gains = len(extra)
    other = [place.from_core(array) for array in mine]
    outs = [like((1, shards - 1, count, height, width), bf16) for count in (more, less)]
    scratch = []
    if extra:
        count, size = extra[0].shape
        outs = outs + [like((1, shards * size), f32)] * count
        scratch = [pltpu.VMEM((shards, count, size), f32)]
    ahead, behind, *gains = call(
        functools.partial(column_kernel, shards, with_gains),
        place.where,
        mine + other + extra,
        outs,
        scratch=scratch,
        after=after,
    )
    for level in range(0, place.bits, 2):
        mine_a = place.from_bit(ahead, level)
        if relay:
            (mine_a,) = hold(place, [mine_a], after=relay)
        mine_far = place.from_bit(mine_a, level + 1)
        mine_b = place.from_bit(behind, level)
        other_a, other_far, other_b = (
            place.from_core(mine_a),
            place.from_core(mine_far),
            place.from_core(mine_b),
        )
        if level + 2 < place.bits:
            first = place.first
            join = lambda *parts: jnp.concatenate(parts, axis=2)
            whole = jnp.concatenate(
                [
                    jnp.where(first, join(ahead, behind), join(behind, ahead)),
                    jnp.where(first, join(mine_a, mine_b), join(other_a, other_b)),
                    jnp.where(first, join(other_b, other_a), join(mine_b, mine_a)),
                    jnp.where(
                        first,
                        join(mine_far, other_far[:, :, more - less :]),
                        join(other_far, mine_far[:, :, more - less :]),
                    ),
                ]
            )
            ahead = jnp.where(first, whole[:, :, :more], whole[:, :, less:])
            behind = jnp.where(first, whole[:, :, more:], whole[:, :, :less])
    wholes = call(
        functools.partial(join_kernel, shards),
        place.where,
        blocks + [ahead, behind, mine_a, mine_b, mine_far, other_a, other_b, other_far],
        [like((shards,) + block.shape, bf16) for block in blocks],
        after=late,
        cost=2.0,
    )
    wholes = [whole.reshape(-1, whole.shape[3]) for whole in wholes]
    return wholes, gains, [mine_a, mine_b, mine_far]


def lane_of(array):
    return lax.broadcasted_iota(jnp.int32, array.shape, len(array.shape) - 1)


def swap_halves(array):
    lane = lane_of(array)
    return jnp.where(
        lane % HD < HD // 2,
        pltpu.roll(array, PAIR - HD // 2, 1),
        pltpu.roll(array, HD // 2, 1),
    )


def only(array, head):
    return jnp.where(lane_of(array) // HD == head, array, jnp.zeros_like(array))


def dot(left, right, left_axis=1, right_axis=0):
    return lax.dot_general(
        left, right, (((left_axis,), (right_axis,)), ((), ())), preferred_element_type=f32
    )


def normalise(values):
    centred = values - jnp.mean(values, axis=-1, keepdims=True)
    scale = lax.rsqrt(jnp.mean(centred * centred, axis=-1, keepdims=True) + epsilon)
    return centred * scale, scale


def norm_back(values, gain, grad):
    normal, scale = normalise(values)
    scaled = grad * gain
    inner = jnp.mean(scaled * normal, axis=-1, keepdims=True)
    back = scale * (scaled - jnp.mean(scaled, axis=-1, keepdims=True) - normal * inner)
    return back, jnp.sum(grad * normal, axis=0, keepdims=True)


def split_shards(array, out, shards):
    size = array.shape[1] // shards // 2
    for half in range(2):
        out[half, :, : shards * size] = jnp.concatenate(
            [array[:, (2 * s + half) * size : (2 * s + half + 1) * size] for s in range(shards)],
            axis=1,
        )


def start_kernel(
    shards, where, tokens, gain, cotangent, across, down, normed, parts, halves, sent, cosine, sine
):
    value = (normalise(tokens[...].astype(f32))[0] * gain[...]).astype(bf16)
    normed[...] = value
    split_shards(value, parts, shards)
    width = halves.shape[2]
    for half in range(2):
        halves[half] = cotangent[:, half * width : (half + 1) * width]
    sent[...] = halves[1 - where[CORE]]
    same = across[...] == down[...]
    before = lane_of(same) < lax.broadcasted_iota(jnp.int32, same.shape, 0)
    position = jnp.sum(jnp.where(same & before, 1.0, 0.0), axis=1, keepdims=True)
    lane = lax.broadcasted_iota(jnp.int32, cosine.shape, 1)
    frequency = jnp.exp((lane % (HD // 2)).astype(f32) * (-2.0 / HD * math.log(rope_base)))
    angles = position * frequency
    cosine[...] = jnp.cos(angles)
    turn = jnp.sin(angles)
    sine[...] = jnp.where(lane % HD < HD // 2, -turn, turn)


def attend_kernel(
    shards, where, normed, weight, cosine, sine, across, down, queries, keys, values, attended,
    parts, probs, projected,
):
    width = normed.shape[1]
    projected[...] = dot(normed[...], weight[...])
    same = across[...] == down[...]
    for pair in range(width // PAIR):
        lanes = slice(pair * PAIR, (pair + 1) * PAIR)

        def turned(start):
            vector = projected[:, start + pair * PAIR : start + (pair + 1) * PAIR]
            return (vector * cosine[...] + swap_halves(vector) * sine[...]).astype(bf16)

        query, key = turned(0), turned(width)
        value = projected[:, 2 * width + pair * PAIR : 2 * width + (pair + 1) * PAIR].astype(bf16)
        queries[:, lanes], keys[:, lanes], values[:, lanes] = query, key, value
        total = 0.0
        for head in range(2):
            scores = dot(only(query, head), key, 1, 1) * HD**-0.5
            scores = jnp.where(same, scores, -1000000000.0)
            exponent = jnp.exp(scores - jnp.max(scores, axis=-1, keepdims=True))
            prob = exponent / jnp.sum(exponent, axis=-1, keepdims=True)
            probs[2 * pair + head] = prob
            total = total + dot(prob.astype(bf16), only(value, head))
        attended[:, lanes] = total.astype(bf16)
    split_shards(attended[...], parts, shards)


def hidden_kernel(
    shards, where, tokens, attended, weight_attn, gain, weight_in, middle, normed_parts, by_gate,
    by_up, hidden, hidden_parts,
):
    value = tokens[...].astype(f32) + dot(attended[...], weight_attn[...])
    middle[...] = value
    normed = (normalise(value)[0] * gain[...]).astype(bf16)
    split_shards(normed, normed_parts, shards)
    size = hidden.shape[1]
    gate, up = dot(normed, weight_in[:, :size]), dot(normed, weight_in[:, size:])
    below = 0.5 * (1.0 + lax.erf(gate * math.sqrt(0.5)))
    active = gate * below
    by_up[...] = active
    by_gate[...] = up * (
        below + gate * jnp.exp(-0.5 * gate * gate) * (1.0 / math.sqrt(2.0 * math.pi))
    )
    low = (active * up).astype(bf16)
    hidden[...] = low
    split_shards(low, hidden_parts, shards)


def output_kernel(
    where, middle, hidden, weight_out, cotangent, by_gate, by_up, output, grad_halves, grad_kept,
    grad_sent,
):
    output[...] = (middle[...] + dot(hidden[...], weight_out[...])).astype(bf16)
    grad = dot(cotangent[...], weight_out[...], 1, 1).astype(bf16).astype(f32)
    grad_halves[0] = (grad * by_gate[...]).astype(bf16)
    grad_halves[1] = (grad * by_up[...]).astype(bf16)
    grad_kept[...] = grad_halves[where[CORE]]
    grad_sent[...] = grad_halves[1 - where[CORE]]


def middle_kernel(
    where, grad_halves, weight_in, middle, gain, cotangent, weight_attn, grad_middle, low_halves,
    low_sent, grad_attended, grad_gain,
):
    size = grad_halves.shape[2]
    grad = dot(grad_halves[0], weight_in[:, :size], 1, 1)
    grad = grad + dot(grad_halves[1], weight_in[:, size:], 1, 1)
    back, gain_part = norm_back(middle[...], gain[...], grad)
    grad_gain[...] = gain_part
    total = cotangent[...].astype(f32) + back
    grad_middle[...] = total
    low = total.astype(bf16)
    half = low.shape[1] // 2
    low_halves[0], low_halves[1] = low[:, :half], low[:, half:]
    low_sent[...] = low_halves[1 - where[CORE]]
    grad_attended[...] = dot(low, weight_attn[...], 1, 1).astype(bf16)


def attend_back_kernel(
    where, grad_attended, queries, keys, values, probs, cosine, sine, grad_halves, grad_kept,
    grad_sent,
):
    width = queries.shape[1]
    half = grad_halves.shape[2]

    def store(start, grad):
        side, rest = divmod(start, half)
        grad_halves[side, :, rest : rest + PAIR] = grad.astype(bf16)

    for pair in range(width // PAIR):
        lanes = slice(pair * PAIR, (pair + 1) * PAIR)
        query, key, value = queries[:, lanes], keys[:, lanes], values[:, lanes]
        above = grad_attended[:, lanes]
        by_query, by_key, by_value = 0.0, 0.0, 0.0
        for head in range(2):
            own = only(above, head)
            grad = dot(own, value, 1, 1)
            prob = probs[2 * pair + head]
            weighted = jnp.sum(prob * grad, axis=-1, keepdims=True)
            grad = (prob * (grad - weighted)).astype(bf16)
            by_query = by_query + dot(grad, only(key, head))
            by_key = by_key + dot(grad, only(query, head), 0, 0)
            by_value = by_value + dot(prob.astype(bf16), own, 0, 0)

        def back(grad):
            grad = grad * HD**-0.5
            return grad * cosine[...] - swap_halves(grad) * sine[...]

        store(pair * PAIR, back(by_query))
        store(width + pair * PAIR, back(by_key))
        store(2 * width + pair * PAIR, by_value)
    grad_kept[...] = grad_halves[where[CORE]]
    grad_sent[...] = grad_halves[1 - where[CORE]]


def tokens_kernel(where, grad_halves, weight, tokens, gain, grad_middle, grad_tokens, grad_gain):
    half = grad_halves.shape[2]
    grad = dot(grad_halves[0], weight[:, :half], 1, 1)
    grad = grad + dot(grad_halves[1], weight[:, half:], 1, 1)
    back, gain_part = norm_back(tokens[...].astype(f32), gain[...], grad)
    grad_gain[...] = gain_part
    grad_tokens[...] = grad_middle[...] + back


def message_kernel(where, own, other, out):
    rows = out.shape[0] // 2
    out[:rows] = own[1 - where[ACT]]
    out[rows:] = other[1 - where[ACT]]


def left_from_chip(place, left, after=()):
    _, rows, columns = left[0].shape
    (message,) = call(
        message_kernel, place.where, left, [like((2 * rows, columns), bf16)], after=after
    )
    return message, place.from_bit(message, 0)


def right_from_chip(place, kept, other):
    return place.from_bit(kept, 0), place.from_bit(other, 0)


def chip_factor(own, other, index):
    far = other[index] if len(other.shape) == 3 else other[...]
    return jnp.concatenate([own[index], far], axis=0)


def near_grad_kernel(shards, where, left, left_other, right, right_other, own, *refs):
    sends, grad = refs[:-1], refs[-1]
    height = grad.shape[1] // 2
    factor = chip_factor(right, right_other, where[CORE])
    for half in range(2):
        value = dot(chip_factor(left, left_other, half), factor, 0, 0)
        for s in range(shards):
            grad[s, half * height : (half + 1) * height] = value[s * height : (s + 1) * height]
    own[...] = grad[where[SHARD]]
    for d, send in enumerate(sends):
        send[...] = grad[lax.rem(where[SHARD] + d + 1, shards)].astype(bf16)


def near_grad(place, left, right, height, after=()):
    shape, width = (height, right[0].shape[2]), right[0].shape[2]
    own, *sends = call(
        functools.partial(near_grad_kernel, place.shards),
        place.where,
        [*left, *right],
        [like(shape, f32)] + [like(shape, bf16)] * (place.shards - 1),
        scratch=[pltpu.VMEM((place.shards, height, width), f32)],
        after=after,
        cost=2.0,
    )
    return [own] + [
        place.permute(send, lambda s, p, c, d=d: (s - d - 1, p)) for d, send in enumerate(sends)
    ]


def halve_kernel(counts, heights, where, *refs):
    kept, sent = refs[-2:]
    at, totals = 0, []
    for count in counts:
        total = refs[at][...]
        for ref in refs[at + 1 : at + count]:
            total = total + ref[...].astype(f32)
        at += count
        totals.append(total)
    if len(totals) == 1:
        total, totals, row = totals[0], [], 0
        for height in heights:
            totals.append(total[row : row + height])
            row += height
    bit = where[SUM + 1]

    def fill(side):
        row = 0
        for total, height in zip(totals, heights):
            half = height // 2
            kept[row : row + half] = total[side * half : (side + 1) * half]
            sent[row : row + half] = total[(1 - side) * half : (2 - side) * half].astype(bf16)
            row += half

    for side in range(2):
        pl.when(bit == side)(functools.partial(fill, side))


def chip_grad_kernel(where, left, left_other, right, right_other, kept, sent):
    factor = chip_factor(right, right_other, where[CORE])
    kept[...] = dot(chip_factor(left, left_other, where[ACT]), factor, 0, 0)
    sent[...] = dot(chip_factor(left, left_other, 1 - where[ACT]), factor, 0, 0).astype(bf16)


def far_grad_kernel(shards, planes, where, *refs):
    left, left_other, left_far = refs[:3]
    rights = refs[3:7]
    along, (sent, kept, grad) = refs[7:-3], refs[-3:]
    width = kept.shape[-1]
    grad[...] = dot(
        jnp.concatenate([chip_factor(left, left_other, where[ACT]), left_far[...]], axis=0),
        jnp.concatenate([right[...] for right in rights], axis=0),
        0,
        0,
    )
    height = grad.shape[0] // shards // (planes // 2)
    chunks = grad.shape[1] // width

    def block(row, k):
        rows = slice(row, row + height)
        if k == chunks:
            return along[0][rows] + along[1][rows].astype(f32)
        return grad[rows, k * width : (k + 1) * width]

    def fill(bit):
        for k in range(chunks + bool(along)):
            rows = slice(k * height, (k + 1) * height)
            for s in range(shards):
                for j in range(planes // 2):
                    side, rest = divmod(j, planes // 4)
                    value = block((s * (planes // 2) + j) * height, k)
                    if side == bit:
                        kept[s, rest, rows] = value
                    else:
                        sent[s, rest, rows] = value.astype(bf16)

    for bit in range(2):
        pl.when(where[SUM] == bit)(functools.partial(fill, bit))


def total_kernel(shards, where, kept, got, *refs):
    if len(refs) > shards:
        *gains, own, own_gains = refs[:4]
        sends, found = refs[4:-1], refs[-1]
        size = found.shape[2]
        for i, gain in enumerate(gains):
            for s in range(shards):
                found[s, i : i + 1] = gain[:, s * size : (s + 1) * size]
        own_gains[...] = found[where[SHARD]]
    else:
        own, sends, found = refs[0], refs[1:], None
    shard, first = where[SHARD], sends[0].shape[0] - own.shape[0]
    own[...] = kept[shard, 0] + got[shard, 0].astype(f32)
    for d, send in enumerate(sends):
        row = lax.rem(shard + d + 1, shards)
        send[first:] = (kept[row, 0] + got[row, 0].astype(f32)).astype(bf16)
        if found is not None:
            send[:2, :size] = found[row].astype(bf16)


def far_grad(place, width, left, rights, along=(), after=()):
    shards, planes = place.shards, place.planes
    rows, columns = left[0].shape[2], rights[0].shape[1]
    total = rows // shards // (planes // 2) * (columns // width + bool(along))
    packed = (shards, planes // 4, total, width)
    sent, kept = call(
        functools.partial(far_grad_kernel, shards, planes),
        place.where,
        [*left, *rights, *along],
        [like(packed, bf16), like(packed, f32)],
        scratch=[pltpu.VMEM((rows, columns), f32)],
        after=after,
        cost=2.0,
    )
    got = place.from_bit(sent, 1)
    for step in range(2, place.bits):
        whole = (kept + got.astype(f32)).reshape(shards, 2, -1, total, width)
        kept = pick(whole, place.bit(step), 1)
        got = place.from_bit(pick(whole, 1 - place.bit(step), 1).astype(bf16), step)
    return kept, sent, got


def shard_sums(place, kept, got, gains=(), after=()):
    shards, (_, _, total, width) = place.shards, kept.shape
    outs, scratch = [like((total, width), f32)], []
    if gains:
        size = gains[0].shape[1] // shards
        outs.append(like((len(gains), size), f32))
        scratch.append(pltpu.VMEM((shards, len(gains), size), f32))
    own = call(
        functools.partial(total_kernel, shards),
        place.where,
        [kept, got, *gains],
        outs + [like((total + GAIN_ROWS * bool(gains), width), bf16)] * (shards - 1),
        scratch=scratch,
        after=after,
    )
    own, sends = list(own[: len(outs)]), own[len(outs) :]
    return own, [
        place.permute(send, lambda s, p, c, d=d: (s - d - 1, p)) for d, send in enumerate(sends)
    ]


def round_kernel(counts, first, where, *refs):
    out, at, row = refs[-1], 0, first
    for count in counts:
        total = refs[at][...]
        for ref in refs[at + 1 : at + count]:
            total = total + ref[first:].astype(f32)
        out[row : row + total.shape[0]] = total.astype(bf16)
        row += total.shape[0]
        at += count
    if first:
        total = refs[at][...]
        rows, columns = total.shape
        for ref in refs[1 : counts[0]]:
            total = total + ref[:rows, :columns].astype(f32)
        out[:rows, :columns] = total.astype(bf16)


def place_kernel(orders, bits, first, heights, chunks, where, whole, *outs):
    planes = 1 << bits
    width = whole.shape[-1]
    for plane in range(planes):
        for side in range(2):
            part = whole.at[2 * plane + side]
            spot = sum(
                ((plane >> at) & 1) << (bits - 1 - step) for step, at in enumerate(orders[side])
            )
            row = first
            for out, height, chunk in zip(outs, heights, chunks):
                for k in range(chunk):
                    lanes = slice((side * chunk + k) * width, (side * chunk + k + 1) * width)
                    out[spot, :, lanes] = part[row : row + height].astype(f32)
                    row += height
    if first:
        rows, columns = outs[-1].shape
        total = 0.0
        for rep in range(2 * planes):
            total = total + whole[rep, :rows, :columns].astype(f32)
        outs[-1][...] = total


def spread_kernel(orders, bits, first, heights, chunks, where, *refs):
    planes = 1 << bits
    mine, other, outs = refs[:planes], refs[planes : 2 * planes], refs[2 * planes :]
    width = mine[0].shape[-1]
    starts = []
    for order in orders:
        start = 0
        for step, at in enumerate(order):
            start = start + (((where[PLANE] >> at) & 1) << (bits - 1 - step))
        starts.append(start)

    def fill(core):
        arrays = (other, mine) if core else (mine, other)
        for p in range(planes):
            at = first
            for out, height, chunk in zip(outs, heights, chunks):
                for k in range(chunk):
                    rows = slice(at, at + height)
                    for side in range(2):
                        lanes = slice((side * chunk + k) * width, (side * chunk + k + 1) * width)
                        out[p ^ starts[side], :, lanes] = arrays[side][p][rows].astype(f32)
                    at += height
            if first:
                rows, columns = outs[-2].shape
                for side in range(2):
                    outs[-1][side, p ^ starts[side]] = arrays[side][p][:rows, :columns].astype(f32)

    for core in range(2):
        pl.when(where[CORE] == core)(functools.partial(fill, core))
    if first:
        total = 0.0
        for side in range(2):
            for p in range(planes):
                total = total + outs[-1][side, p]
        outs[-2][...] = total


def spread_grads(place, width, groups, heights, chunks, gains=None, after=(), at_once=False):
    planes = place.planes
    first = 0 if gains is None else GAIN_ROWS
    total = sum(height * chunk for height, chunk in zip(heights, chunks))
    extra = [] if gains is None else [gains]
    mine = list(
        call(
            functools.partial(round_kernel, [len(group) for group in groups], first),
            place.where,
            [array for group in groups for array in group] + extra,
            [like((first + total, width), bf16)],
            after=after,
        )
    )
    part = mine[0]
    if at_once:
        outs = call(
            functools.partial(place_kernel, place.orders, place.bits, first, heights, chunks),
            place.where,
            [lax.all_gather(part, "rep")],
            [
                like((planes, height, 2 * chunk * width), f32)
                for height, chunk in zip(heights, chunks)
            ]
            + [like(array.shape, f32) for array in extra],
            cost=2.0,
        )
        count = len(heights)
        return [out.reshape(-1, out.shape[2]) for out in outs[:count]], list(outs[count:]), part
    for step in reversed(range(place.bits)):
        mine = mine + [place.from_bit(array, step) for array in mine]
    other = [place.from_core(array) for array in mine]
    outs = call(
        functools.partial(spread_kernel, place.orders, place.bits, first, heights, chunks),
        place.where,
        mine + other,
        [
            like((planes, height, 2 * chunk * width), f32)
            for height, chunk in zip(heights, chunks)
        ]
        + [like(array.shape, f32) for array in extra],
        scratch=[pltpu.VMEM((2, planes) + array.shape, f32) for array in extra],
        cost=2.0,
    )
    count = len(heights)
    return [out.reshape(-1, out.shape[2]) for out in outs[:count]], list(outs[count:]), part


def body(
    shards,
    reps,
    tokens,
    segment_ids,
    attn_gain,
    qkv_weight,
    attn_out_weight,
    mlp_gain,
    in_weight,
    out_weight,
    cotangent,
):
    place = Place(shards, reps)
    where = place.where
    tokens, documents, cotangent = tokens[0], segment_ids[0], cotangent[0]
    length, model = tokens.shape
    heads, size = model // HD, out_weight.shape[0] * shards
    width = model // 2
    rows = lambda columns, kind=bf16: like((length, columns), kind)
    halves = lambda columns: like((2, length, columns // 2), bf16)
    padded = like((2, length, -(-size // 2 // 128) * 128), bf16)

    *first, piece, part = pieces(
        place, [qkv_weight], width, gains=jnp.stack([attn_gain, mlp_gain])
    )
    *second, later_piece, later_part = pieces(
        place, [attn_out_weight, in_weight], width
    )
    later = from_shards(place, later_piece, later_part)
    (weight_qkv,), (gain_attn, gain_mlp), through = finish_gather(
        place,
        *first,
        from_shards(place, piece, part),
        after=[later_piece],
        relay=later[:-1],
    )
    later = hold(place, later, after=through)
    (out_block,), _, _, out_piece, out_part = pieces(
        place, [out_weight], width, after=later, planes=1
    )
    out_arrived = from_shards(place, out_piece, out_part)

    across, down = documents[:, None], documents[None, :]
    normed_one, one_parts, cotangent_halves, cotangent_sent, cosine, sine = call(
        functools.partial(start_kernel, shards),
        where,
        [tokens, gain_attn, cotangent, across, down],
        [rows(model), halves(model), halves(model), rows(width)] + [rows(PAIR, f32)] * 2,
        cost=2.0,
    )
    cotangent_factor = (cotangent_halves, place.from_core(cotangent_sent))
    one_factor = (one_parts, place.from_core(one_parts))
    one_factor = one_factor + left_from_chip(place, one_factor)[1:]

    queries, keys, values, attended, attended_parts, probs = call(
        functools.partial(attend_kernel, shards),
        where,
        [normed_one, weight_qkv, cosine, sine, across, down],
        [rows(model)] * 4 + [halves(model), like((heads, length, length), f32)],
        scratch=[pltpu.VMEM((length, 3 * model), f32)],
        after=[cotangent_factor[1]],
        cost=5.0,
    )
    attended_factor = (attended_parts, place.from_core(attended_parts))
    (weight_attn, weight_in), _, _ = finish_gather(
        place, *second, later, after=[out_piece], relay=[attended, *out_arrived[:-1]], late=out_arrived[-1:]
    )
    weight_out = finish_direct(place, [out_block], out_arrived)
    middle, two_parts, by_gate, by_up, hidden, hidden_parts = call(
        functools.partial(hidden_kernel, shards),
        where,
        [tokens, attended, weight_attn, gain_mlp, weight_in],
        [rows(model, f32), halves(model), rows(size, f32), rows(size, f32), rows(size), padded],
        after=[attended_factor[1], one_factor[2]],
        cost=4.0,
    )
    two_factor = (two_parts, place.from_core(two_parts))
    hidden_factor = (hidden_parts, place.from_core(hidden_parts))
    output, gate_up_halves, gate_up_kept, gate_up_sent = call(
        output_kernel,
        where,
        [middle, hidden, weight_out, cotangent, by_gate, by_up],
        [rows(model), halves(2 * size), rows(size), rows(size)],
        cost=3.0,
    )
    gate_up_other = place.from_core(gate_up_sent)
    message, two_far = left_from_chip(place, two_factor, after=[gate_up_kept])
    two_factor = two_factor + (two_far,)
    gate_up_far = right_from_chip(place, gate_up_kept, gate_up_other)
    out_group = near_grad(
        place, hidden_factor, cotangent_factor, size // shards, after=[message]
    )
    grad_middle, low_halves, low_sent, grad_attended, mlp_gain_part = call(
        middle_kernel,
        where,
        [gate_up_halves, weight_in, middle, gain_mlp, cotangent, weight_attn],
        [rows(model, f32), halves(model), rows(width), rows(model), like((1, model), f32)],
        after=[gate_up_other, out_group[0]],
        cost=3.0,
    )
    low_factor = (low_halves, place.from_core(low_sent))
    projected_halves, projected_kept, projected_sent = call(
        attend_back_kernel,
        where,
        [grad_attended, queries, keys, values, probs, cosine, sine],
        [halves(3 * model), rows(3 * width), rows(3 * width)],
        after=[gate_up_far[0], two_far],
        cost=3.0,
    )
    projected_other = place.from_core(projected_sent)
    projected_far = right_from_chip(place, projected_kept, projected_other)
    attn_kept, attn_sent = call(
        chip_grad_kernel,
        where,
        [*attended_factor, *low_factor],
        [like((width, width), f32), like((width, width), bf16)],
        after=[projected_other],
        cost=1.0,
    )
    attn_got = place.from_bit(attn_sent, 0)
    qkv_kept, qkv_sent, qkv_got = far_grad(
        place,
        width,
        one_factor,
        [projected_kept, projected_other, *projected_far],
        after=[attn_sent],
    )
    in_kept, in_sent, in_got = far_grad(
        place,
        width,
        two_factor,
        [gate_up_kept, gate_up_other, *gate_up_far],
        along=[attn_kept, attn_got],
        after=[qkv_sent],
    )
    grad_tokens, attn_gain_part = call(
        tokens_kernel,
        where,
        [projected_halves, weight_qkv, tokens, gain_attn, grad_middle],
        [rows(model, f32), like((1, model), f32)],
        after=[in_sent],
        cost=3.0,
    )
    (qkv_own, gains), qkv_arrived = shard_sums(
        place, qkv_kept, qkv_got, gains=[attn_gain_part, mlp_gain_part]
    )
    (in_own,), in_arrived = shard_sums(place, in_kept, in_got, after=[qkv_own])
    height = size // shards
    for step in range(place.bits):
        kept, sent = call(
            functools.partial(halve_kernel, [len(out_group)], [height]),
            jnp.concatenate([where, place.bit(step).astype(jnp.int32)[None]]),
            out_group,
            [like((height // 2, width), f32), like((height // 2, width), bf16)],
            after=[in_sent],
        )
        out_group, height = [kept, place.from_bit(sent, step)], height // 2
    part = model // shards // place.planes
    (qkv_weight_g,), (gains_g,), early = spread_grads(
        place, width, [[qkv_own, *qkv_arrived]], [part], [3 * model // 2 // width], gains=gains
    )
    (in_weight_g, attn_out_g, out_weight_g), _, _ = spread_grads(
        place,
        width,
        [[in_own, *in_arrived], out_group],
        [part, part, height],
        [size // width, 1, 1],
        after=[early],
    )
    return (
        output[None],
        grad_tokens[None],
        gains_g[0],
        qkv_weight_g,
        attn_out_g,
        gains_g[1],
        in_weight_g,
        out_weight_g,
    )


def solution(mesh):
    return jax.shard_map(
        functools.partial(body, mesh.shape["shard"], mesh.shape["rep"]),
        mesh=mesh,
        in_specs=(
            P(("rep", "shard"), None, None),
            P(("rep", "shard"), None),
            P("shard"),
            P("shard", None),
            P("shard", None),
            P("shard"),
            P("shard", None),
            P("shard", None),
            P(("rep", "shard"), None, None),
        ),
        out_specs=(
            P(("rep", "shard"), None, None),
            P(("rep", "shard"), None, None),
            P("shard"),
            P("shard", None),
            P("shard", None),
            P("shard"),
            P("shard", None),
            P("shard", None),
        ),
        check_vma=False,
    )
```

```python
import functools
import math

import jax
import jax.numpy as jnp
from jax import lax
from jax.experimental import pallas as pl
from jax.experimental.pallas import tpu as pltpu
from jax.sharding import PartitionSpec as P

HD = 64
PAIR = 2 * HD


rope_base = 160000.0
epsilon = 1e-05
VMEM = pl.BlockSpec(memory_space=pltpu.VMEM)
SMEM = pl.BlockSpec(memory_space=pltpu.SMEM)
ANY = pl.BlockSpec(memory_space=pl.ANY)
SHARD, PLANE, CORE, ACT, SUM = range(5)
GAIN_ROWS = 16
f32, bf16 = jnp.float32, jnp.bfloat16


def like(shape, dtype):
    return jax.ShapeDtypeStruct(tuple(shape), dtype)


def padded_bytes(array):
    *lead, rows, columns = array.shape
    tile = 8 * 4 // array.dtype.itemsize
    return (
        math.prod(lead) * -(-rows // tile) * tile * -(-columns // 128) * 128 * array.dtype.itemsize
    )


def call(kernel, where, operands, outs, scratch=(), after=(), cost=1.0):
    count, late = len(operands), len(operands) + len(after)
    room = sum(padded_bytes(array) for array in [*operands, *outs, *scratch])

    def inner(where_ref, *refs):
        kernel(where_ref, *refs[:count], *refs[late:])

    return pl.pallas_call(
        inner,
        out_shape=list(outs),
        in_specs=[SMEM] + [VMEM] * count + [ANY] * len(after),
        out_specs=[VMEM] * len(outs),
        scratch_shapes=list(scratch),
        compiler_params=pltpu.CompilerParams(vmem_limit_bytes=room + 6 * 2**20),
        cost_estimate=pl.CostEstimate(
            flops=int(cost * 1.1e9), bytes_accessed=0, transcendentals=0
        ),
    )(where, *operands, *after)


class Place:
    def __init__(self, shards, reps):
        self.shards, self.planes = shards, reps // 2
        self.bits = self.planes.bit_length() - 1
        if self.planes != 1 << self.bits or self.bits % 2 or shards % 2:
            raise ValueError("mesh sizes")
        pairs = range(0, self.bits, 2)
        self.orders = tuple([i + k for i in pairs for k in turn] for turn in ((0, 1), (1, 0)))
        rep = lax.axis_index("rep")
        self.shard, self.plane, self.core = lax.axis_index("shard"), rep // 2, rep % 2
        self.first = self.core == 0
        self.where = jnp.stack(
            [self.shard, self.plane, self.core, self.bit(0), self.bit(1)]
        ).astype(jnp.int32)

    def permute(self, array, source):
        flat = lambda s, p, c: (2 * p + c) * self.shards + s
        pairs = []
        for p in range(self.planes):
            for c in range(2):
                for s in range(self.shards):
                    from_s, from_p = source(s, p, c)
                    pairs.append((flat(from_s % self.shards, from_p, c), flat(s, p, c)))
        return lax.ppermute(array, ("rep", "shard"), pairs)

    def from_core(self, array):
        return lax.ppermute(array, "rep", [(r, r ^ 1) for r in range(2 * self.planes)])

    def from_bit(self, array, step):
        return self.permute(array, lambda s, p, c: (s, p ^ (1 << self.orders[c][step])))

    def bit(self, step):
        at = jnp.where(self.first, self.orders[0][step], self.orders[1][step])
        return (self.plane >> at) & 1

    def both(self, mine, other):
        return jnp.where(self.first, mine, other), jnp.where(self.first, other, mine)


def pick(array, index, axis=0):
    return lax.dynamic_index_in_dim(array, index, axis, keepdims=False)


def segments(blocks, width, height):
    found, at = [], 0
    for number, block in enumerate(blocks):
        for k in range(block.shape[2] // width):
            row, left = 0, block.shape[1]
            while left:
                rows = min(left, height - at % height)
                lanes = slice(k * width, (k + 1) * width)
                found.append((at // height, at % height, number, lanes, row, rows))
                at, row, left = at + rows, row + rows, left - rows
    return found


def piece_kernel(width, with_gains, where, *refs):
    blocks, piece, part = refs[:-2], refs[-2], refs[-1]
    if with_gains:
        *blocks, gains = blocks
        rows, columns = gains.shape
        piece[piece.shape[0] - 1, :rows, :columns] = gains[...]
        part[part.shape[0] - 1, :rows, :columns] = gains[...]
    more = part.shape[0] - with_gains
    less = piece.shape[0] - with_gains - more
    for chunk, first, number, lanes, row, rows in segments(blocks, width, piece.shape[1]):
        block = blocks[number]
        plane = lax.rem(where[PLANE], block.shape[0])
        piece[chunk, first : first + rows] = block[plane, row : row + rows, lanes]
    for i in range(more):
        part[i] = piece[i + less * where[CORE]]


def column_kernel(shards, with_gains, where, *refs):
    count = shards // 2
    mine, other = refs[:count], refs[count : 2 * count]
    refs = refs[2 * count :]
    gains = None
    if with_gains:
        gains, refs = refs[0], refs[1:]
    ahead, behind = refs[:2]
    more, less = ahead.shape[2], behind.shape[2]

    def fill(core):
        near, far = (other, mine) if core else (mine, other)
        first, second = (other[-1], mine[-1]) if core else (mine[-1], other[-1])

        def put(out, i, k):
            for d in range(1, count):
                out[0, d - 1, i] = near[d - 1][k]
                out[0, shards - d - 1, i] = far[d - 1][k]
            out[0, count - 1, i] = first[k] if k < more else second[k - less]

        for i in range(more):
            put(ahead, i, i + less * core)
        for i in range(less):
            put(behind, i, i if core else i + more)
        if with_gains:
            found = refs[-1]
            rows, columns = gains.shape
            found[where[SHARD]] = gains[...].astype(f32)

            def keep(d, value):
                found[lax.rem(where[SHARD] + d, shards)] = value[:rows, :columns].astype(f32)

            for d in range(1, count):
                keep(d, near[d - 1][more + less])
                keep(shards - d, far[d - 1][more + less])
            keep(count, mine[-1][more])

    for core in range(2):
        pl.when(where[CORE] == core)(functools.partial(fill, core))
    if with_gains:
        found = refs[-1]
        size = found.shape[2]
        for i, out in enumerate(refs[2:-1]):
            for s in range(shards):
                out[:, s * size : (s + 1) * size] = found[s, i : i + 1]


def pass_kernel(where, *refs):
    half = len(refs) // 2
    for source, out in zip(refs[:half], refs[half:]):
        out[...] = source[...]


def direct_kernel(shards, where, own, *refs):
    count = shards // 2
    mine, other, out = refs[:count], refs[count : 2 * count], refs[-1]
    total, half, width = mine[0].shape[0], mine[-1].shape[0], mine[0].shape[-1]
    out[where[SHARD]] = own[0]

    def fill(core):
        near, far = (other, mine) if core else (mine, other)
        middle = (other[-1], mine[-1]) if core else (mine[-1], other[-1])
        for k in range(2 * half):
            lanes = slice(k * width, (k + 1) * width)
            row = lambda d: lax.rem(where[SHARD] + d, shards)
            for d in range(1, count):
                out[row(d), :, lanes] = near[d - 1][k]
                out[row(shards - d), :, lanes] = far[d - 1][k]
            out[row(count), :, lanes] = middle[k // half][k % half]

    for core in range(2):
        pl.when(where[CORE] == core)(functools.partial(fill, core))


def join_kernel(shards, where, *refs):
    count = (len(refs) - 8) // 2
    owns, outs = refs[:count], refs[count + 8 :]
    ahead, behind, mine_a, mine_b, mine_far, other_a, other_b, other_far = refs[
        count : count + 8
    ]
    inner, more, height, width = ahead.shape[0], ahead.shape[2], *ahead.shape[3:]
    less = behind.shape[2]
    shard, plane = where[SHARD], where[PLANE]
    for own, out in zip(owns, outs):
        out[shard] = own[...]

    def fill(core):
        mine, other = (mine_a, mine_b), (other_a, other_b)
        low, high = (other, mine) if core else (mine, other)
        far = (other_far, mine_far) if core else (mine_far, other_far)

        def put(d, i, chunk, first, number, lanes, row, rows):
            def read(pair, order):
                early = chunk < more if order == 0 else chunk >= less
                at = chunk - less * order if early else chunk - more * (1 - order)
                return pair[0 if early else 1][i, d, at, first : first + rows]

            out, shard_at = outs[number], lax.rem(shard + d + 1, shards)
            spot = slice(row, row + rows)
            out[shard_at, plane ^ i, spot, lanes] = read((ahead, behind), core)
            out[shard_at, plane ^ (inner + i), spot, lanes] = read(low, 0)
            out[shard_at, plane ^ (2 * inner + i), spot, lanes] = read(high, 1)
            at = chunk if chunk < more else chunk - less
            source = far[0 if chunk < more else 1]
            out[shard_at, plane ^ (3 * inner + i), spot, lanes] = source[
                i, d, at, first : first + rows
            ]

        for d in range(shards - 1):
            for i in range(inner):
                for segment in segments(owns, width, height):
                    put(d, i, *segment)

    for core in range(2):
        pl.when(where[CORE] == core)(functools.partial(fill, core))


def pieces(place, weights, width, gains=None, after=(), planes=None):
    planes = planes or place.planes
    blocks = [weight.reshape(planes, -1, weight.shape[1]) for weight in weights]
    height = min(block.shape[1] for block in blocks)
    total = sum(block.shape[1] * block.shape[2] for block in blocks) // width // height
    extra = [] if gains is None else [gains]
    piece, part = call(
        functools.partial(piece_kernel, width, len(extra)),
        place.where,
        blocks + extra,
        [
            like((total + len(extra), height, width), bf16),
            like(((total + 1) // 2 + len(extra), height, width), bf16),
        ],
        after=after,
    )
    return blocks, extra, total, piece, part


def from_shards(place, piece, part):
    found = [
        place.permute(piece, lambda s, p, c, d=d: (s - d if c else s + d, p))
        for d in range(1, place.shards // 2)
    ]
    return found + [place.permute(part, lambda s, p, c: (s + place.shards // 2, p))]


def hold(place, arrays, after):
    outs = [like(array.shape, array.dtype) for array in arrays]
    return list(call(pass_kernel, place.where, arrays, outs, after=after))


def finish_direct(place, blocks, mine):
    other = [place.from_core(array) for array in mine]
    (whole,) = call(
        functools.partial(direct_kernel, place.shards),
        place.where,
        blocks + mine + other,
        [like((place.shards,) + blocks[0].shape[1:], bf16)],
        cost=2.0,
    )
    return whole.reshape(-1, whole.shape[2])


def column_of(place, extra, total, mine, after=()):
    shards = place.shards
    height, width = mine[-1].shape[1:]
    less, more = total // 2, (total + 1) // 2
    with_gains = len(extra)
    other = [place.from_core(array) for array in mine]
    outs = [like((1, shards - 1, count, height, width), bf16) for count in (more, less)]
    scratch = []
    if extra:
        count, size = extra[0].shape
        outs = outs + [like((1, shards * size), f32)] * count
        scratch = [pltpu.VMEM((shards, count, size), f32)]
    ahead, behind, *gains = call(
        functools.partial(column_kernel, shards, with_gains),
        place.where,
        mine + other + extra,
        outs,
        scratch=scratch,
        after=after,
    )
    return ahead, behind, gains


def finish_gather(place, blocks, ahead, behind, relay=(), late=()):
    shards, more, less = place.shards, ahead.shape[2], behind.shape[2]
    for level in range(0, place.bits, 2):
        mine_a = place.from_bit(ahead, level)
        if relay:
            (mine_a,) = hold(place, [mine_a], after=relay)
        mine_far = place.from_bit(mine_a, level + 1)
        mine_b = place.from_bit(behind, level)
        other_a, other_far, other_b = (
            place.from_core(mine_a),
            place.from_core(mine_far),
            place.from_core(mine_b),
        )
        if level + 2 < place.bits:
            first = place.first
            join = lambda *parts: jnp.concatenate(parts, axis=2)
            whole = jnp.concatenate(
                [
                    jnp.where(first, join(ahead, behind), join(behind, ahead)),
                    jnp.where(first, join(mine_a, mine_b), join(other_a, other_b)),
                    jnp.where(first, join(other_b, other_a), join(mine_b, mine_a)),
                    jnp.where(
                        first,
                        join(mine_far, other_far[:, :, more - less :]),
                        join(other_far, mine_far[:, :, more - less :]),
                    ),
                ]
            )
            ahead = jnp.where(first, whole[:, :, :more], whole[:, :, less:])
            behind = jnp.where(first, whole[:, :, more:], whole[:, :, :less])
    wholes = call(
        functools.partial(join_kernel, shards),
        place.where,
        blocks + [ahead, behind, mine_a, mine_b, mine_far, other_a, other_b, other_far],
        [like((shards,) + block.shape, bf16) for block in blocks],
        after=late,
        cost=2.0,
    )
    wholes = [whole.reshape(-1, whole.shape[3]) for whole in wholes]
    return wholes, [mine_a, mine_b, mine_far]


def lane_of(array):
    return lax.broadcasted_iota(jnp.int32, array.shape, len(array.shape) - 1)


def swap_halves(array):
    lane = lane_of(array)
    return jnp.where(
        lane % HD < HD // 2,
        pltpu.roll(array, PAIR - HD // 2, 1),
        pltpu.roll(array, HD // 2, 1),
    )


def only(array, head):
    return jnp.where(lane_of(array) // HD == head, array, jnp.zeros_like(array))


def dot(left, right, left_axis=1, right_axis=0):
    return lax.dot_general(
        left, right, (((left_axis,), (right_axis,)), ((), ())), preferred_element_type=f32
    )


def normalise(values):
    centred = values - jnp.mean(values, axis=-1, keepdims=True)
    scale = lax.rsqrt(jnp.mean(centred * centred, axis=-1, keepdims=True) + epsilon)
    return centred * scale, scale


def norm_back(values, gain, grad):
    normal, scale = normalise(values)
    scaled = grad * gain
    inner = jnp.mean(scaled * normal, axis=-1, keepdims=True)
    back = scale * (scaled - jnp.mean(scaled, axis=-1, keepdims=True) - normal * inner)
    return back, jnp.sum(grad * normal, axis=0, keepdims=True)


def split_shards(array, out, shards):
    size = array.shape[1] // shards // 2
    for half in range(2):
        out[half, :, : shards * size] = jnp.concatenate(
            [array[:, (2 * s + half) * size : (2 * s + half + 1) * size] for s in range(shards)],
            axis=1,
        )


def start_kernel(
    shards, where, tokens, gain, cotangent, across, down, normed, parts, halves, sent, cosine, sine
):
    value = (normalise(tokens[...].astype(f32))[0] * gain[...]).astype(bf16)
    normed[...] = value
    split_shards(value, parts, shards)
    width = halves.shape[2]
    for half in range(2):
        halves[half] = cotangent[:, half * width : (half + 1) * width]
    sent[...] = halves[1 - where[CORE]]
    same = across[...] == down[...]
    before = lane_of(same) < lax.broadcasted_iota(jnp.int32, same.shape, 0)
    position = jnp.sum(jnp.where(same & before, 1.0, 0.0), axis=1, keepdims=True)
    lane = lax.broadcasted_iota(jnp.int32, cosine.shape, 1)
    frequency = jnp.exp((lane % (HD // 2)).astype(f32) * (-2.0 / HD * math.log(rope_base)))
    angles = position * frequency
    cosine[...] = jnp.cos(angles)
    turn = jnp.sin(angles)
    sine[...] = jnp.where(lane % HD < HD // 2, -turn, turn)


def attend_kernel(
    shards, where, normed, weight, cosine, sine, across, down, queries, keys, values, attended,
    parts, probs, projected,
):
    width = normed.shape[1]
    projected[...] = dot(normed[...], weight[...])
    same = across[...] == down[...]
    for pair in range(width // PAIR):
        lanes = slice(pair * PAIR, (pair + 1) * PAIR)

        def turned(start):
            vector = projected[:, start + pair * PAIR : start + (pair + 1) * PAIR]
            return (vector * cosine[...] + swap_halves(vector) * sine[...]).astype(bf16)

        query, key = turned(0), turned(width)
        value = projected[:, 2 * width + pair * PAIR : 2 * width + (pair + 1) * PAIR].astype(bf16)
        queries[:, lanes], keys[:, lanes], values[:, lanes] = query, key, value
        total = 0.0
        for head in range(2):
            scores = dot(only(query, head), key, 1, 1) * HD**-0.5
            scores = jnp.where(same, scores, -1000000000.0)
            exponent = jnp.exp(scores - jnp.max(scores, axis=-1, keepdims=True))
            prob = exponent / jnp.sum(exponent, axis=-1, keepdims=True)
            probs[2 * pair + head] = prob
            total = total + dot(prob.astype(bf16), only(value, head))
        attended[:, lanes] = total.astype(bf16)
    split_shards(attended[...], parts, shards)


def hidden_kernel(
    shards, where, tokens, attended, weight_attn, gain, weight_in, middle, normed_parts, by_gate,
    by_up, hidden, hidden_parts,
):
    value = tokens[...].astype(f32) + dot(attended[...], weight_attn[...])
    middle[...] = value
    normed = (normalise(value)[0] * gain[...]).astype(bf16)
    split_shards(normed, normed_parts, shards)
    size = hidden.shape[1]
    gate, up = dot(normed, weight_in[:, :size]), dot(normed, weight_in[:, size:])
    below = 0.5 * (1.0 + lax.erf(gate * math.sqrt(0.5)))
    active = gate * below
    by_up[...] = active
    by_gate[...] = up * (
        below + gate * jnp.exp(-0.5 * gate * gate) * (1.0 / math.sqrt(2.0 * math.pi))
    )
    low = (active * up).astype(bf16)
    hidden[...] = low
    split_shards(low, hidden_parts, shards)


def output_kernel(
    where, middle, hidden, weight_out, cotangent, by_gate, by_up, output, grad_halves, grad_kept,
    grad_sent,
):
    output[...] = (middle[...] + dot(hidden[...], weight_out[...])).astype(bf16)
    grad = dot(cotangent[...], weight_out[...], 1, 1).astype(bf16).astype(f32)
    grad_halves[0] = (grad * by_gate[...]).astype(bf16)
    grad_halves[1] = (grad * by_up[...]).astype(bf16)
    grad_kept[...] = grad_halves[where[CORE]]
    grad_sent[...] = grad_halves[1 - where[CORE]]


def middle_kernel(
    where, grad_halves, weight_in, middle, gain, cotangent, weight_attn, grad_middle, low_halves,
    low_sent, grad_attended, grad_gain,
):
    size = grad_halves.shape[2]
    grad = dot(grad_halves[0], weight_in[:, :size], 1, 1)
    grad = grad + dot(grad_halves[1], weight_in[:, size:], 1, 1)
    back, gain_part = norm_back(middle[...], gain[...], grad)
    grad_gain[...] = gain_part
    total = cotangent[...].astype(f32) + back
    grad_middle[...] = total
    low = total.astype(bf16)
    half = low.shape[1] // 2
    low_halves[0], low_halves[1] = low[:, :half], low[:, half:]
    low_sent[...] = low_halves[1 - where[CORE]]
    grad_attended[...] = dot(low, weight_attn[...], 1, 1).astype(bf16)


def attend_back_kernel(
    where, grad_attended, queries, keys, values, probs, cosine, sine, grad_halves, grad_kept,
    grad_sent,
):
    width = queries.shape[1]
    half = grad_halves.shape[2]

    def store(start, grad):
        side, rest = divmod(start, half)
        grad_halves[side, :, rest : rest + PAIR] = grad.astype(bf16)

    for pair in range(width // PAIR):
        lanes = slice(pair * PAIR, (pair + 1) * PAIR)
        query, key, value = queries[:, lanes], keys[:, lanes], values[:, lanes]
        above = grad_attended[:, lanes]
        by_query, by_key, by_value = 0.0, 0.0, 0.0
        for head in range(2):
            own = only(above, head)
            grad = dot(own, value, 1, 1)
            prob = probs[2 * pair + head]
            weighted = jnp.sum(prob * grad, axis=-1, keepdims=True)
            grad = (prob * (grad - weighted)).astype(bf16)
            by_query = by_query + dot(grad, only(key, head))
            by_key = by_key + dot(grad, only(query, head), 0, 0)
            by_value = by_value + dot(prob.astype(bf16), own, 0, 0)

        def back(grad):
            grad = grad * HD**-0.5
            return grad * cosine[...] - swap_halves(grad) * sine[...]

        store(pair * PAIR, back(by_query))
        store(width + pair * PAIR, back(by_key))
        store(2 * width + pair * PAIR, by_value)
    grad_kept[...] = grad_halves[where[CORE]]
    grad_sent[...] = grad_halves[1 - where[CORE]]


def tokens_kernel(where, grad_halves, weight, tokens, gain, grad_middle, grad_tokens, grad_gain):
    half = grad_halves.shape[2]
    grad = dot(grad_halves[0], weight[:, :half], 1, 1)
    grad = grad + dot(grad_halves[1], weight[:, half:], 1, 1)
    back, gain_part = norm_back(tokens[...].astype(f32), gain[...], grad)
    grad_gain[...] = gain_part
    grad_tokens[...] = grad_middle[...] + back


def message_kernel(where, own, other, out):
    rows = out.shape[0] // 2
    out[:rows] = own[1 - where[ACT]]
    out[rows:] = other[1 - where[ACT]]


def left_from_chip(place, left, after=()):
    _, rows, columns = left[0].shape
    (message,) = call(
        message_kernel, place.where, left, [like((2 * rows, columns), bf16)], after=after
    )
    return message, place.from_bit(message, 0)


def right_from_chip(place, kept, other):
    return place.from_bit(kept, 0), place.from_bit(other, 0)


def chip_factor(own, other, index):
    far = other[index] if len(other.shape) == 3 else other[...]
    return jnp.concatenate([own[index], far], axis=0)


def near_grad_kernel(shards, where, left, left_other, right, right_other, own, *refs):
    sends, grad = refs[:-1], refs[-1]
    height = grad.shape[1] // 2
    factor = chip_factor(right, right_other, where[CORE])
    for half in range(2):
        value = dot(chip_factor(left, left_other, half), factor, 0, 0)
        for s in range(shards):
            grad[s, half * height : (half + 1) * height] = value[s * height : (s + 1) * height]
    own[...] = grad[where[SHARD]]
    for d, send in enumerate(sends):
        send[...] = grad[lax.rem(where[SHARD] + d + 1, shards)].astype(bf16)


def near_grad(place, left, right, height, after=()):
    shape, width = (height, right[0].shape[2]), right[0].shape[2]
    own, *sends = call(
        functools.partial(near_grad_kernel, place.shards),
        place.where,
        [*left, *right],
        [like(shape, f32)] + [like(shape, bf16)] * (place.shards - 1),
        scratch=[pltpu.VMEM((place.shards, height, width), f32)],
        after=after,
        cost=2.0,
    )
    return [own] + [
        place.permute(send, lambda s, p, c, d=d: (s - d - 1, p)) for d, send in enumerate(sends)
    ]


def halve_kernel(counts, heights, where, *refs):
    kept, sent = refs[-2:]
    at, totals = 0, []
    for count in counts:
        total = refs[at][...]
        for ref in refs[at + 1 : at + count]:
            total = total + ref[...].astype(f32)
        at += count
        totals.append(total)
    if len(totals) == 1:
        total, totals, row = totals[0], [], 0
        for height in heights:
            totals.append(total[row : row + height])
            row += height
    bit = where[SUM + 1]

    def fill(side):
        row = 0
        for total, height in zip(totals, heights):
            half = height // 2
            kept[row : row + half] = total[side * half : (side + 1) * half]
            sent[row : row + half] = total[(1 - side) * half : (2 - side) * half].astype(bf16)
            row += half

    for side in range(2):
        pl.when(bit == side)(functools.partial(fill, side))


def chip_grad_kernel(where, left, left_other, right, right_other, kept, sent):
    factor = chip_factor(right, right_other, where[CORE])
    kept[...] = dot(chip_factor(left, left_other, where[ACT]), factor, 0, 0)
    sent[...] = dot(chip_factor(left, left_other, 1 - where[ACT]), factor, 0, 0).astype(bf16)


def far_grad_kernel(shards, planes, where, *refs):
    left, left_other, left_far = refs[:3]
    rights = refs[3:7]
    along, (sent, kept, grad) = refs[7:-3], refs[-3:]
    width = kept.shape[-1]
    grad[...] = dot(
        jnp.concatenate([chip_factor(left, left_other, where[ACT]), left_far[...]], axis=0),
        jnp.concatenate([right[...] for right in rights], axis=0),
        0,
        0,
    )
    height = grad.shape[0] // shards // (planes // 2)
    chunks = grad.shape[1] // width

    def block(row, k):
        rows = slice(row, row + height)
        if k == chunks:
            return along[0][rows] + along[1][rows].astype(f32)
        return grad[rows, k * width : (k + 1) * width]

    def fill(bit):
        for k in range(chunks + bool(along)):
            rows = slice(k * height, (k + 1) * height)
            for s in range(shards):
                for j in range(planes // 2):
                    side, rest = divmod(j, planes // 4)
                    value = block((s * (planes // 2) + j) * height, k)
                    if side == bit:
                        kept[s, rest, rows] = value
                    else:
                        sent[s, rest, rows] = value.astype(bf16)

    for bit in range(2):
        pl.when(where[SUM] == bit)(functools.partial(fill, bit))


def total_kernel(shards, where, kept, got, *refs):
    if len(refs) > shards:
        *gains, own, own_gains = refs[:4]
        sends, found = refs[4:-1], refs[-1]
        size = found.shape[2]
        for i, gain in enumerate(gains):
            for s in range(shards):
                found[s, i : i + 1] = gain[:, s * size : (s + 1) * size]
        own_gains[...] = found[where[SHARD]]
    else:
        own, sends, found = refs[0], refs[1:], None
    shard, first = where[SHARD], sends[0].shape[0] - own.shape[0]
    own[...] = kept[shard, 0] + got[shard, 0].astype(f32)
    for d, send in enumerate(sends):
        row = lax.rem(shard + d + 1, shards)
        send[first:] = (kept[row, 0] + got[row, 0].astype(f32)).astype(bf16)
        if found is not None:
            send[:2, :size] = found[row].astype(bf16)


def far_grad(place, width, left, rights, along=(), after=()):
    shards, planes = place.shards, place.planes
    rows, columns = left[0].shape[2], rights[0].shape[1]
    total = rows // shards // (planes // 2) * (columns // width + bool(along))
    packed = (shards, planes // 4, total, width)
    sent, kept = call(
        functools.partial(far_grad_kernel, shards, planes),
        place.where,
        [*left, *rights, *along],
        [like(packed, bf16), like(packed, f32)],
        scratch=[pltpu.VMEM((rows, columns), f32)],
        after=after,
        cost=2.0,
    )
    got = place.from_bit(sent, 1)
    for step in range(2, place.bits):
        whole = (kept + got.astype(f32)).reshape(shards, 2, -1, total, width)
        kept = pick(whole, place.bit(step), 1)
        got = place.from_bit(pick(whole, 1 - place.bit(step), 1).astype(bf16), step)
    return kept, sent, got


def shard_sums(place, kept, got, gains=(), after=()):
    shards, (_, _, total, width) = place.shards, kept.shape
    outs, scratch = [like((total, width), f32)], []
    if gains:
        size = gains[0].shape[1] // shards
        outs.append(like((len(gains), size), f32))
        scratch.append(pltpu.VMEM((shards, len(gains), size), f32))
    own = call(
        functools.partial(total_kernel, shards),
        place.where,
        [kept, got, *gains],
        outs + [like((total + GAIN_ROWS * bool(gains), width), bf16)] * (shards - 1),
        scratch=scratch,
        after=after,
    )
    own, sends = list(own[: len(outs)]), own[len(outs) :]
    return own, [
        place.permute(send, lambda s, p, c, d=d: (s - d - 1, p)) for d, send in enumerate(sends)
    ]


def round_kernel(counts, first, where, *refs):
    out, at, row = refs[-1], 0, first
    for count in counts:
        total = refs[at][...]
        for ref in refs[at + 1 : at + count]:
            total = total + ref[first:].astype(f32)
        out[row : row + total.shape[0]] = total.astype(bf16)
        row += total.shape[0]
        at += count
    if first:
        total = refs[at][...]
        rows, columns = total.shape
        for ref in refs[1 : counts[0]]:
            total = total + ref[:rows, :columns].astype(f32)
        out[:rows, :columns] = total.astype(bf16)


def place_kernel(orders, bits, first, heights, chunks, where, whole, *outs):
    planes = 1 << bits
    width = whole.shape[-1]
    for plane in range(planes):
        for side in range(2):
            part = whole.at[2 * plane + side]
            spot = sum(
                ((plane >> at) & 1) << (bits - 1 - step) for step, at in enumerate(orders[side])
            )
            row = first
            for out, height, chunk in zip(outs, heights, chunks):
                for k in range(chunk):
                    lanes = slice((side * chunk + k) * width, (side * chunk + k + 1) * width)
                    out[spot, :, lanes] = part[row : row + height].astype(f32)
                    row += height
    if first:
        rows, columns = outs[-1].shape
        total = 0.0
        for rep in range(2 * planes):
            total = total + whole[rep, :rows, :columns].astype(f32)
        outs[-1][...] = total


def spread_kernel(orders, bits, first, heights, chunks, where, *refs):
    planes = 1 << bits
    mine, other, outs = refs[:planes], refs[planes : 2 * planes], refs[2 * planes :]
    width = mine[0].shape[-1]
    starts = []
    for order in orders:
        start = 0
        for step, at in enumerate(order):
            start = start + (((where[PLANE] >> at) & 1) << (bits - 1 - step))
        starts.append(start)

    def fill(core):
        arrays = (other, mine) if core else (mine, other)
        for p in range(planes):
            at = first
            for out, height, chunk in zip(outs, heights, chunks):
                for k in range(chunk):
                    rows = slice(at, at + height)
                    for side in range(2):
                        lanes = slice((side * chunk + k) * width, (side * chunk + k + 1) * width)
                        out[p ^ starts[side], :, lanes] = arrays[side][p][rows].astype(f32)
                    at += height
            if first:
                rows, columns = outs[-2].shape
                for side in range(2):
                    outs[-1][side, p ^ starts[side]] = arrays[side][p][:rows, :columns].astype(f32)

    for core in range(2):
        pl.when(where[CORE] == core)(functools.partial(fill, core))
    if first:
        total = 0.0
        for side in range(2):
            for p in range(planes):
                total = total + outs[-1][side, p]
        outs[-2][...] = total


def spread_grads(place, width, groups, heights, chunks, gains=None, after=(), at_once=False):
    planes = place.planes
    first = 0 if gains is None else GAIN_ROWS
    total = sum(height * chunk for height, chunk in zip(heights, chunks))
    extra = [] if gains is None else [gains]
    mine = list(
        call(
            functools.partial(round_kernel, [len(group) for group in groups], first),
            place.where,
            [array for group in groups for array in group] + extra,
            [like((first + total, width), bf16)],
            after=after,
        )
    )
    part = mine[0]
    if at_once:
        outs = call(
            functools.partial(place_kernel, place.orders, place.bits, first, heights, chunks),
            place.where,
            [lax.all_gather(part, "rep")],
            [
                like((planes, height, 2 * chunk * width), f32)
                for height, chunk in zip(heights, chunks)
            ]
            + [like(array.shape, f32) for array in extra],
            cost=2.0,
        )
        count = len(heights)
        return [out.reshape(-1, out.shape[2]) for out in outs[:count]], list(outs[count:]), part
    for step in reversed(range(place.bits)):
        mine = mine + [place.from_bit(array, step) for array in mine]
    other = [place.from_core(array) for array in mine]
    outs = call(
        functools.partial(spread_kernel, place.orders, place.bits, first, heights, chunks),
        place.where,
        mine + other,
        [
            like((planes, height, 2 * chunk * width), f32)
            for height, chunk in zip(heights, chunks)
        ]
        + [like(array.shape, f32) for array in extra],
        scratch=[pltpu.VMEM((2, planes) + array.shape, f32) for array in extra],
        cost=2.0,
    )
    count = len(heights)
    return [out.reshape(-1, out.shape[2]) for out in outs[:count]], list(outs[count:]), part


def body(
    shards,
    reps,
    tokens,
    segment_ids,
    attn_gain,
    qkv_weight,
    attn_out_weight,
    mlp_gain,
    in_weight,
    out_weight,
    cotangent,
):
    place = Place(shards, reps)
    where = place.where
    tokens, documents, cotangent = tokens[0], segment_ids[0], cotangent[0]
    length, model = tokens.shape
    heads, size = model // HD, out_weight.shape[0] * shards
    width = model // 2
    rows = lambda columns, kind=bf16: like((length, columns), kind)
    halves = lambda columns: like((2, length, columns // 2), bf16)
    padded = like((2, length, -(-size // 2 // 128) * 128), bf16)

    blocks, extra, total, piece, part = pieces(place, [qkv_weight], width)
    gains = jnp.stack([attn_gain, mlp_gain])
    later_blocks, later_extra, later_total, later_piece, later_part = pieces(
        place, [attn_out_weight, in_weight], width, gains=gains
    )
    later = from_shards(place, later_piece, later_part)
    ahead, behind, _ = column_of(
        place, extra, total, from_shards(place, piece, part), after=[later_piece]
    )
    (weight_qkv,), through = finish_gather(place, blocks, ahead, behind, relay=later[:-1])
    later = hold(place, later, after=through)
    (out_block,), _, _, out_piece, out_part = pieces(
        place, [out_weight], width, after=later, planes=1
    )
    out_arrived = from_shards(place, out_piece, out_part)
    ahead, behind, (gain_attn, gain_mlp) = column_of(
        place, later_extra, later_total, later, after=[out_piece]
    )

    across, down = documents[:, None], documents[None, :]
    normed_one, one_parts, cotangent_halves, cotangent_sent, cosine, sine = call(
        functools.partial(start_kernel, shards),
        where,
        [tokens, gain_attn, cotangent, across, down],
        [rows(model), halves(model), halves(model), rows(width)] + [rows(PAIR, f32)] * 2,
        cost=2.0,
    )
    cotangent_factor = (cotangent_halves, place.from_core(cotangent_sent))
    one_factor = (one_parts, place.from_core(one_parts))
    one_factor = one_factor + left_from_chip(place, one_factor)[1:]

    queries, keys, values, attended, attended_parts, probs = call(
        functools.partial(attend_kernel, shards),
        where,
        [normed_one, weight_qkv, cosine, sine, across, down],
        [rows(model)] * 4 + [halves(model), like((heads, length, length), f32)],
        scratch=[pltpu.VMEM((length, 3 * model), f32)],
        after=[cotangent_factor[1]],
        cost=5.0,
    )
    attended_factor = (attended_parts, place.from_core(attended_parts))
    (weight_attn, weight_in), _ = finish_gather(
        place,
        later_blocks,
        ahead,
        behind,
        relay=[attended, one_factor[2], *out_arrived[:-1]],
    )
    weight_out = finish_direct(place, [out_block], out_arrived)
    middle, two_parts, by_gate, by_up, hidden, hidden_parts = call(
        functools.partial(hidden_kernel, shards),
        where,
        [tokens, attended, weight_attn, gain_mlp, weight_in],
        [rows(model, f32), halves(model), rows(size, f32), rows(size, f32), rows(size), padded],
        after=[attended_factor[1]],
        cost=4.0,
    )
    two_factor = (two_parts, place.from_core(two_parts))
    hidden_factor = (hidden_parts, place.from_core(hidden_parts))
    output, gate_up_halves, gate_up_kept, gate_up_sent = call(
        output_kernel,
        where,
        [middle, hidden, weight_out, cotangent, by_gate, by_up],
        [rows(model), halves(2 * size), rows(size), rows(size)],
        cost=3.0,
    )
    gate_up_other = place.from_core(gate_up_sent)
    message, two_far = left_from_chip(place, two_factor, after=[gate_up_kept])
    two_factor = two_factor + (two_far,)
    gate_up_far = right_from_chip(place, gate_up_kept, gate_up_other)
    out_group = near_grad(
        place, hidden_factor, cotangent_factor, size // shards, after=[message]
    )
    grad_middle, low_halves, low_sent, grad_attended, mlp_gain_part = call(
        middle_kernel,
        where,
        [gate_up_halves, weight_in, middle, gain_mlp, cotangent, weight_attn],
        [rows(model, f32), halves(model), rows(width), rows(model), like((1, model), f32)],
        after=[gate_up_other, out_group[0]],
        cost=3.0,
    )
    low_factor = (low_halves, place.from_core(low_sent))
    projected_halves, projected_kept, projected_sent = call(
        attend_back_kernel,
        where,
        [grad_attended, queries, keys, values, probs, cosine, sine],
        [halves(3 * model), rows(3 * width), rows(3 * width)],
        after=[gate_up_far[0], two_far],
        cost=3.0,
    )
    projected_other = place.from_core(projected_sent)
    projected_far = right_from_chip(place, projected_kept, projected_other)
    attn_kept, attn_sent = call(
        chip_grad_kernel,
        where,
        [*attended_factor, *low_factor],
        [like((width, width), f32), like((width, width), bf16)],
        after=[projected_other],
        cost=1.0,
    )
    attn_got = place.from_bit(attn_sent, 0)
    qkv_kept, qkv_sent, qkv_got = far_grad(
        place,
        width,
        one_factor,
        [projected_kept, projected_other, *projected_far],
        after=[attn_sent],
    )
    in_kept, in_sent, in_got = far_grad(
        place,
        width,
        two_factor,
        [gate_up_kept, gate_up_other, *gate_up_far],
        along=[attn_kept, attn_got],
        after=[qkv_sent],
    )
    grad_tokens, attn_gain_part = call(
        tokens_kernel,
        where,
        [projected_halves, weight_qkv, tokens, gain_attn, grad_middle],
        [rows(model, f32), like((1, model), f32)],
        after=[in_sent],
        cost=3.0,
    )
    (qkv_own, gains), qkv_arrived = shard_sums(
        place, qkv_kept, qkv_got, gains=[attn_gain_part, mlp_gain_part]
    )
    (in_own,), in_arrived = shard_sums(place, in_kept, in_got, after=[qkv_own])
    height = size // shards
    for step in range(place.bits):
        kept, sent = call(
            functools.partial(halve_kernel, [len(out_group)], [height]),
            jnp.concatenate([where, place.bit(step).astype(jnp.int32)[None]]),
            out_group,
            [like((height // 2, width), f32), like((height // 2, width), bf16)],
            after=[in_sent],
        )
        out_group, height = [kept, place.from_bit(sent, step)], height // 2
    part = model // shards // place.planes
    (qkv_weight_g,), (gains_g,), early = spread_grads(
        place, width, [[qkv_own, *qkv_arrived]], [part], [3 * model // 2 // width], gains=gains
    )
    (in_weight_g, attn_out_g, out_weight_g), _, _ = spread_grads(
        place,
        width,
        [[in_own, *in_arrived], out_group],
        [part, part, height],
        [size // width, 1, 1],
        after=[early],
    )
    return (
        output[None],
        grad_tokens[None],
        gains_g[0],
        qkv_weight_g,
        attn_out_g,
        gains_g[1],
        in_weight_g,
        out_weight_g,
    )


def solution(mesh):
    return jax.shard_map(
        functools.partial(body, mesh.shape["shard"], mesh.shape["rep"]),
        mesh=mesh,
        in_specs=(
            P(("rep", "shard"), None, None),
            P(("rep", "shard"), None),
            P("shard"),
            P("shard", None),
            P("shard", None),
            P("shard"),
            P("shard", None),
            P("shard", None),
            P(("rep", "shard"), None, None),
        ),
        out_specs=(
            P(("rep", "shard"), None, None),
            P(("rep", "shard"), None, None),
            P("shard"),
            P("shard", None),
            P("shard", None),
            P("shard"),
            P("shard", None),
            P("shard", None),
        ),
        check_vma=False,
    )
```

```python
import functools
import math

import jax
import jax.numpy as jnp
from jax import lax
from jax.experimental import pallas as pl
from jax.experimental.pallas import tpu as pltpu
from jax.sharding import PartitionSpec as P

HD = 64
PAIR = 2 * HD


rope_base = 160000.0
epsilon = 1e-05
VMEM = pl.BlockSpec(memory_space=pltpu.VMEM)
SMEM = pl.BlockSpec(memory_space=pltpu.SMEM)
ANY = pl.BlockSpec(memory_space=pl.ANY)
SHARD, PLANE, CORE, ACT, SUM = range(5)
GAIN_ROWS = 16
f32, bf16 = jnp.float32, jnp.bfloat16


def like(shape, dtype):
    return jax.ShapeDtypeStruct(tuple(shape), dtype)


def padded_bytes(array):
    *lead, rows, columns = array.shape
    tile = 8 * 4 // array.dtype.itemsize
    return (
        math.prod(lead) * -(-rows // tile) * tile * -(-columns // 128) * 128 * array.dtype.itemsize
    )


def call(kernel, where, operands, outs, scratch=(), after=(), cost=1.0):
    count, late = len(operands), len(operands) + len(after)
    room = sum(padded_bytes(array) for array in [*operands, *outs, *scratch])

    def inner(where_ref, *refs):
        kernel(where_ref, *refs[:count], *refs[late:])

    return pl.pallas_call(
        inner,
        out_shape=list(outs),
        in_specs=[SMEM] + [VMEM] * count + [ANY] * len(after),
        out_specs=[VMEM] * len(outs),
        scratch_shapes=list(scratch),
        compiler_params=pltpu.CompilerParams(vmem_limit_bytes=room + 6 * 2**20),
        cost_estimate=pl.CostEstimate(
            flops=int(cost * 1.1e9), bytes_accessed=0, transcendentals=0
        ),
    )(where, *operands, *after)


class Place:
    def __init__(self, shards, reps):
        self.shards, self.planes = shards, reps // 2
        self.bits = self.planes.bit_length() - 1
        if self.planes != 1 << self.bits or self.bits % 2 or shards % 2:
            raise ValueError("mesh sizes")
        pairs = range(0, self.bits, 2)
        self.orders = tuple([i + k for i in pairs for k in turn] for turn in ((0, 1), (1, 0)))
        rep = lax.axis_index("rep")
        self.shard, self.plane, self.core = lax.axis_index("shard"), rep // 2, rep % 2
        self.first = self.core == 0
        self.where = jnp.stack(
            [self.shard, self.plane, self.core, self.bit(0), self.bit(1)]
        ).astype(jnp.int32)

    def permute(self, array, source):
        flat = lambda s, p, c: (2 * p + c) * self.shards + s
        pairs = []
        for p in range(self.planes):
            for c in range(2):
                for s in range(self.shards):
                    from_s, from_p = source(s, p, c)
                    pairs.append((flat(from_s % self.shards, from_p, c), flat(s, p, c)))
        return lax.ppermute(array, ("rep", "shard"), pairs)

    def from_core(self, array):
        return lax.ppermute(array, "rep", [(r, r ^ 1) for r in range(2 * self.planes)])

    def from_bit(self, array, step):
        return self.permute(array, lambda s, p, c: (s, p ^ (1 << self.orders[c][step])))

    def bit(self, step):
        at = jnp.where(self.first, self.orders[0][step], self.orders[1][step])
        return (self.plane >> at) & 1

    def both(self, mine, other):
        return jnp.where(self.first, mine, other), jnp.where(self.first, other, mine)


def pick(array, index, axis=0):
    return lax.dynamic_index_in_dim(array, index, axis, keepdims=False)


def segments(blocks, width, height):
    found, at = [], 0
    for number, block in enumerate(blocks):
        for k in range(block.shape[2] // width):
            row, left = 0, block.shape[1]
            while left:
                rows = min(left, height - at % height)
                lanes = slice(k * width, (k + 1) * width)
                found.append((at // height, at % height, number, lanes, row, rows))
                at, row, left = at + rows, row + rows, left - rows
    return found


def piece_kernel(width, with_gains, where, *refs):
    blocks, piece, part = refs[:-2], refs[-2], refs[-1]
    if with_gains:
        *blocks, gains = blocks
        rows, columns = gains.shape
        piece[piece.shape[0] - 1, :rows, :columns] = gains[...]
        part[part.shape[0] - 1, :rows, :columns] = gains[...]
    more = part.shape[0] - with_gains
    less = piece.shape[0] - with_gains - more
    for chunk, first, number, lanes, row, rows in segments(blocks, width, piece.shape[1]):
        block = blocks[number]
        plane = lax.rem(where[PLANE], block.shape[0])
        piece[chunk, first : first + rows] = block[plane, row : row + rows, lanes]
    for i in range(more):
        part[i] = piece[i + less * where[CORE]]


def column_kernel(shards, with_gains, where, *refs):
    count = shards // 2
    mine, other = refs[:count], refs[count : 2 * count]
    refs = refs[2 * count :]
    gains = None
    if with_gains:
        gains, refs = refs[0], refs[1:]
    ahead, behind = refs[:2]
    more, less = ahead.shape[2], behind.shape[2]

    def fill(core):
        near, far = (other, mine) if core else (mine, other)
        first, second = (other[-1], mine[-1]) if core else (mine[-1], other[-1])

        def put(out, i, k):
            for d in range(1, count):
                out[0, d - 1, i] = near[d - 1][k]
                out[0, shards - d - 1, i] = far[d - 1][k]
            out[0, count - 1, i] = first[k] if k < more else second[k - less]

        for i in range(more):
            put(ahead, i, i + less * core)
        for i in range(less):
            put(behind, i, i if core else i + more)
        if with_gains:
            found = refs[-1]
            rows, columns = gains.shape
            found[where[SHARD]] = gains[...].astype(f32)

            def keep(d, value):
                found[lax.rem(where[SHARD] + d, shards)] = value[:rows, :columns].astype(f32)

            for d in range(1, count):
                keep(d, near[d - 1][more + less])
                keep(shards - d, far[d - 1][more + less])
            keep(count, mine[-1][more])

    for core in range(2):
        pl.when(where[CORE] == core)(functools.partial(fill, core))
    if with_gains:
        found = refs[-1]
        size = found.shape[2]
        for i, out in enumerate(refs[2:-1]):
            for s in range(shards):
                out[:, s * size : (s + 1) * size] = found[s, i : i + 1]


def pass_kernel(where, *refs):
    half = len(refs) // 2
    for source, out in zip(refs[:half], refs[half:]):
        out[...] = source[...]


def direct_kernel(shards, where, own, *refs):
    count = shards // 2
    mine, other, out = refs[:count], refs[count : 2 * count], refs[-1]
    total, half, width = mine[0].shape[0], mine[-1].shape[0], mine[0].shape[-1]
    out[where[SHARD]] = own[0]

    def fill(core):
        near, far = (other, mine) if core else (mine, other)
        middle = (other[-1], mine[-1]) if core else (mine[-1], other[-1])
        for k in range(2 * half):
            lanes = slice(k * width, (k + 1) * width)
            row = lambda d: lax.rem(where[SHARD] + d, shards)
            for d in range(1, count):
                out[row(d), :, lanes] = near[d - 1][k]
                out[row(shards - d), :, lanes] = far[d - 1][k]
            out[row(count), :, lanes] = middle[k // half][k % half]

    for core in range(2):
        pl.when(where[CORE] == core)(functools.partial(fill, core))


def join_kernel(shards, where, *refs):
    count = (len(refs) - 8) // 2
    owns, outs = refs[:count], refs[count + 8 :]
    ahead, behind, mine_a, mine_b, mine_far, other_a, other_b, other_far = refs[
        count : count + 8
    ]
    inner, more, height, width = ahead.shape[0], ahead.shape[2], *ahead.shape[3:]
    less = behind.shape[2]
    shard, plane = where[SHARD], where[PLANE]
    for own, out in zip(owns, outs):
        out[shard] = own[...]

    def fill(core):
        mine, other = (mine_a, mine_b), (other_a, other_b)
        low, high = (other, mine) if core else (mine, other)
        far = (other_far, mine_far) if core else (mine_far, other_far)

        def put(d, i, chunk, first, number, lanes, row, rows):
            def read(pair, order):
                early = chunk < more if order == 0 else chunk >= less
                at = chunk - less * order if early else chunk - more * (1 - order)
                return pair[0 if early else 1][i, d, at, first : first + rows]

            out, shard_at = outs[number], lax.rem(shard + d + 1, shards)
            spot = slice(row, row + rows)
            out[shard_at, plane ^ i, spot, lanes] = read((ahead, behind), core)
            out[shard_at, plane ^ (inner + i), spot, lanes] = read(low, 0)
            out[shard_at, plane ^ (2 * inner + i), spot, lanes] = read(high, 1)
            at = chunk if chunk < more else chunk - less
            source = far[0 if chunk < more else 1]
            out[shard_at, plane ^ (3 * inner + i), spot, lanes] = source[
                i, d, at, first : first + rows
            ]

        for d in range(shards - 1):
            for i in range(inner):
                for segment in segments(owns, width, height):
                    put(d, i, *segment)

    for core in range(2):
        pl.when(where[CORE] == core)(functools.partial(fill, core))


def pieces(place, weights, width, gains=None, after=(), planes=None):
    planes = planes or place.planes
    blocks = [weight.reshape(planes, -1, weight.shape[1]) for weight in weights]
    height = min(block.shape[1] for block in blocks)
    total = sum(block.shape[1] * block.shape[2] for block in blocks) // width // height
    extra = [] if gains is None else [gains]
    piece, part = call(
        functools.partial(piece_kernel, width, len(extra)),
        place.where,
        blocks + extra,
        [
            like((total + len(extra), height, width), bf16),
            like(((total + 1) // 2 + len(extra), height, width), bf16),
        ],
        after=after,
    )
    return blocks, extra, total, piece, part


def from_shards(place, piece, part):
    found = [
        place.permute(piece, lambda s, p, c, d=d: (s - d if c else s + d, p))
        for d in range(1, place.shards // 2)
    ]
    return found + [place.permute(part, lambda s, p, c: (s + place.shards // 2, p))]


def hold(place, arrays, after):
    outs = [like(array.shape, array.dtype) for array in arrays]
    return list(call(pass_kernel, place.where, arrays, outs, after=after))


def finish_direct(place, blocks, mine):
    other = [place.from_core(array) for array in mine]
    (whole,) = call(
        functools.partial(direct_kernel, place.shards),
        place.where,
        blocks + mine + other,
        [like((place.shards,) + blocks[0].shape[1:], bf16)],
        cost=2.0,
    )
    return whole.reshape(-1, whole.shape[2])


def column_of(place, extra, total, mine, after=()):
    shards = place.shards
    height, width = mine[-1].shape[1:]
    less, more = total // 2, (total + 1) // 2
    with_gains = len(extra)
    other = [place.from_core(array) for array in mine]
    outs = [like((1, shards - 1, count, height, width), bf16) for count in (more, less)]
    scratch = []
    if extra:
        count, size = extra[0].shape
        outs = outs + [like((1, shards * size), f32)] * count
        scratch = [pltpu.VMEM((shards, count, size), f32)]
    ahead, behind, *gains = call(
        functools.partial(column_kernel, shards, with_gains),
        place.where,
        mine + other + extra,
        outs,
        scratch=scratch,
        after=after,
    )
    return ahead, behind, gains


def finish_gather(place, blocks, ahead, behind, relay=(), late=()):
    shards, more, less = place.shards, ahead.shape[2], behind.shape[2]
    for level in range(0, place.bits, 2):
        mine_a = place.from_bit(ahead, level)
        if relay:
            (mine_a,) = hold(place, [mine_a], after=relay)
        mine_far = place.from_bit(mine_a, level + 1)
        mine_b = place.from_bit(behind, level)
        other_a, other_far, other_b = (
            place.from_core(mine_a),
            place.from_core(mine_far),
            place.from_core(mine_b),
        )
        if level + 2 < place.bits:
            first = place.first
            join = lambda *parts: jnp.concatenate(parts, axis=2)
            whole = jnp.concatenate(
                [
                    jnp.where(first, join(ahead, behind), join(behind, ahead)),
                    jnp.where(first, join(mine_a, mine_b), join(other_a, other_b)),
                    jnp.where(first, join(other_b, other_a), join(mine_b, mine_a)),
                    jnp.where(
                        first,
                        join(mine_far, other_far[:, :, more - less :]),
                        join(other_far, mine_far[:, :, more - less :]),
                    ),
                ]
            )
            ahead = jnp.where(first, whole[:, :, :more], whole[:, :, less:])
            behind = jnp.where(first, whole[:, :, more:], whole[:, :, :less])
    wholes = call(
        functools.partial(join_kernel, shards),
        place.where,
        blocks + [ahead, behind, mine_a, mine_b, mine_far, other_a, other_b, other_far],
        [like((shards,) + block.shape, bf16) for block in blocks],
        after=late,
        cost=2.0,
    )
    wholes = [whole.reshape(-1, whole.shape[3]) for whole in wholes]
    return wholes, [mine_a, mine_b, mine_far]


def lane_of(array):
    return lax.broadcasted_iota(jnp.int32, array.shape, len(array.shape) - 1)


def swap_halves(array):
    lane = lane_of(array)
    return jnp.where(
        lane % HD < HD // 2,
        pltpu.roll(array, PAIR - HD // 2, 1),
        pltpu.roll(array, HD // 2, 1),
    )


def only(array, head):
    return jnp.where(lane_of(array) // HD == head, array, jnp.zeros_like(array))


def dot(left, right, left_axis=1, right_axis=0):
    return lax.dot_general(
        left, right, (((left_axis,), (right_axis,)), ((), ())), preferred_element_type=f32
    )


def normalise(values):
    centred = values - jnp.mean(values, axis=-1, keepdims=True)
    scale = lax.rsqrt(jnp.mean(centred * centred, axis=-1, keepdims=True) + epsilon)
    return centred * scale, scale


def norm_back(values, gain, grad):
    normal, scale = normalise(values)
    scaled = grad * gain
    inner = jnp.mean(scaled * normal, axis=-1, keepdims=True)
    back = scale * (scaled - jnp.mean(scaled, axis=-1, keepdims=True) - normal * inner)
    return back, jnp.sum(grad * normal, axis=0, keepdims=True)


def split_shards(array, out, shards):
    size = array.shape[1] // shards // 2
    for half in range(2):
        out[half, :, : shards * size] = jnp.concatenate(
            [array[:, (2 * s + half) * size : (2 * s + half + 1) * size] for s in range(shards)],
            axis=1,
        )


def start_kernel(
    shards, where, tokens, gain, cotangent, across, down, normed, parts, halves, sent, cosine, sine
):
    value = (normalise(tokens[...].astype(f32))[0] * gain[...]).astype(bf16)
    normed[...] = value
    split_shards(value, parts, shards)
    width = halves.shape[2]
    for half in range(2):
        halves[half] = cotangent[:, half * width : (half + 1) * width]
    sent[...] = halves[1 - where[CORE]]
    same = across[...] == down[...]
    before = lane_of(same) < lax.broadcasted_iota(jnp.int32, same.shape, 0)
    position = jnp.sum(jnp.where(same & before, 1.0, 0.0), axis=1, keepdims=True)
    lane = lax.broadcasted_iota(jnp.int32, cosine.shape, 1)
    frequency = jnp.exp((lane % (HD // 2)).astype(f32) * (-2.0 / HD * math.log(rope_base)))
    angles = position * frequency
    cosine[...] = jnp.cos(angles)
    turn = jnp.sin(angles)
    sine[...] = jnp.where(lane % HD < HD // 2, -turn, turn)


def attend_kernel(
    shards, where, normed, weight, cosine, sine, across, down, queries, keys, values, attended,
    parts, probs, projected,
):
    width = normed.shape[1]
    projected[...] = dot(normed[...], weight[...])
    same = across[...] == down[...]
    for pair in range(width // PAIR):
        lanes = slice(pair * PAIR, (pair + 1) * PAIR)

        def turned(start):
            vector = projected[:, start + pair * PAIR : start + (pair + 1) * PAIR]
            return (vector * cosine[...] + swap_halves(vector) * sine[...]).astype(bf16)

        query, key = turned(0), turned(width)
        value = projected[:, 2 * width + pair * PAIR : 2 * width + (pair + 1) * PAIR].astype(bf16)
        queries[:, lanes], keys[:, lanes], values[:, lanes] = query, key, value
        total = 0.0
        for head in range(2):
            scores = dot(only(query, head), key, 1, 1) * HD**-0.5
            scores = jnp.where(same, scores, -1000000000.0)
            exponent = jnp.exp(scores - jnp.max(scores, axis=-1, keepdims=True))
            prob = exponent / jnp.sum(exponent, axis=-1, keepdims=True)
            probs[2 * pair + head] = prob
            total = total + dot(prob.astype(bf16), only(value, head))
        attended[:, lanes] = total.astype(bf16)
    split_shards(attended[...], parts, shards)


def hidden_kernel(
    shards, where, tokens, attended, weight_attn, gain, weight_in, middle, normed_parts, by_gate,
    by_up, hidden, hidden_parts,
):
    value = tokens[...].astype(f32) + dot(attended[...], weight_attn[...])
    middle[...] = value
    normed = (normalise(value)[0] * gain[...]).astype(bf16)
    split_shards(normed, normed_parts, shards)
    size = hidden.shape[1]
    gate, up = dot(normed, weight_in[:, :size]), dot(normed, weight_in[:, size:])
    below = 0.5 * (1.0 + lax.erf(gate * math.sqrt(0.5)))
    active = gate * below
    by_up[...] = active
    by_gate[...] = up * (
        below + gate * jnp.exp(-0.5 * gate * gate) * (1.0 / math.sqrt(2.0 * math.pi))
    )
    low = (active * up).astype(bf16)
    hidden[...] = low
    split_shards(low, hidden_parts, shards)


def output_kernel(
    where, middle, hidden, weight_out, cotangent, by_gate, by_up, output, grad_halves, grad_kept,
    grad_sent,
):
    output[...] = (middle[...] + dot(hidden[...], weight_out[...])).astype(bf16)
    grad = dot(cotangent[...], weight_out[...], 1, 1).astype(bf16).astype(f32)
    grad_halves[0] = (grad * by_gate[...]).astype(bf16)
    grad_halves[1] = (grad * by_up[...]).astype(bf16)
    grad_kept[...] = grad_halves[where[CORE]]
    grad_sent[...] = grad_halves[1 - where[CORE]]


def middle_kernel(
    where, grad_halves, weight_in, middle, gain, cotangent, weight_attn, grad_middle, low_halves,
    low_sent, grad_attended, grad_gain,
):
    size = grad_halves.shape[2]
    grad = dot(grad_halves[0], weight_in[:, :size], 1, 1)
    grad = grad + dot(grad_halves[1], weight_in[:, size:], 1, 1)
    back, gain_part = norm_back(middle[...], gain[...], grad)
    grad_gain[...] = gain_part
    total = cotangent[...].astype(f32) + back
    grad_middle[...] = total
    low = total.astype(bf16)
    half = low.shape[1] // 2
    low_halves[0], low_halves[1] = low[:, :half], low[:, half:]
    low_sent[...] = low_halves[1 - where[CORE]]
    grad_attended[...] = dot(low, weight_attn[...], 1, 1).astype(bf16)


def attend_back_kernel(
    where, grad_attended, queries, keys, values, probs, cosine, sine, grad_halves, grad_kept,
    grad_sent,
):
    width = queries.shape[1]
    half = grad_halves.shape[2]

    def store(start, grad):
        side, rest = divmod(start, half)
        grad_halves[side, :, rest : rest + PAIR] = grad.astype(bf16)

    for pair in range(width // PAIR):
        lanes = slice(pair * PAIR, (pair + 1) * PAIR)
        query, key, value = queries[:, lanes], keys[:, lanes], values[:, lanes]
        above = grad_attended[:, lanes]
        by_query, by_key, by_value = 0.0, 0.0, 0.0
        for head in range(2):
            own = only(above, head)
            grad = dot(own, value, 1, 1)
            prob = probs[2 * pair + head]
            weighted = jnp.sum(prob * grad, axis=-1, keepdims=True)
            grad = (prob * (grad - weighted)).astype(bf16)
            by_query = by_query + dot(grad, only(key, head))
            by_key = by_key + dot(grad, only(query, head), 0, 0)
            by_value = by_value + dot(prob.astype(bf16), own, 0, 0)

        def back(grad):
            grad = grad * HD**-0.5
            return grad * cosine[...] - swap_halves(grad) * sine[...]

        store(pair * PAIR, back(by_query))
        store(width + pair * PAIR, back(by_key))
        store(2 * width + pair * PAIR, by_value)
    grad_kept[...] = grad_halves[where[CORE]]
    grad_sent[...] = grad_halves[1 - where[CORE]]


def tokens_kernel(where, grad_halves, weight, tokens, gain, grad_middle, grad_tokens, grad_gain):
    half = grad_halves.shape[2]
    grad = dot(grad_halves[0], weight[:, :half], 1, 1)
    grad = grad + dot(grad_halves[1], weight[:, half:], 1, 1)
    back, gain_part = norm_back(tokens[...].astype(f32), gain[...], grad)
    grad_gain[...] = gain_part
    grad_tokens[...] = grad_middle[...] + back


def message_kernel(where, own, other, out):
    rows = out.shape[0] // 2
    out[:rows] = own[1 - where[ACT]]
    out[rows:] = other[1 - where[ACT]]


def left_from_chip(place, left, after=()):
    _, rows, columns = left[0].shape
    (message,) = call(
        message_kernel, place.where, left, [like((2 * rows, columns), bf16)], after=after
    )
    return message, place.from_bit(message, 0)


def right_from_chip(place, kept, other):
    return place.from_bit(kept, 0), place.from_bit(other, 0)


def chip_factor(own, other, index):
    far = other[index] if len(other.shape) == 3 else other[...]
    return jnp.concatenate([own[index], far], axis=0)


def near_grad_kernel(shards, where, left, left_other, right, right_other, own, *refs):
    sends, grad = refs[:-1], refs[-1]
    height = grad.shape[1] // 2
    factor = chip_factor(right, right_other, where[CORE])
    for half in range(2):
        value = dot(chip_factor(left, left_other, half), factor, 0, 0)
        for s in range(shards):
            grad[s, half * height : (half + 1) * height] = value[s * height : (s + 1) * height]
    own[...] = grad[where[SHARD]]
    for d, send in enumerate(sends):
        send[...] = grad[lax.rem(where[SHARD] + d + 1, shards)].astype(bf16)


def near_grad(place, left, right, height, after=()):
    shape, width = (height, right[0].shape[2]), right[0].shape[2]
    own, *sends = call(
        functools.partial(near_grad_kernel, place.shards),
        place.where,
        [*left, *right],
        [like(shape, f32)] + [like(shape, bf16)] * (place.shards - 1),
        scratch=[pltpu.VMEM((place.shards, height, width), f32)],
        after=after,
        cost=2.0,
    )
    return [own] + [
        place.permute(send, lambda s, p, c, d=d: (s - d - 1, p)) for d, send in enumerate(sends)
    ]


def halve_kernel(counts, heights, where, *refs):
    kept, sent = refs[-2:]
    at, totals = 0, []
    for count in counts:
        total = refs[at][...]
        for ref in refs[at + 1 : at + count]:
            total = total + ref[...].astype(f32)
        at += count
        totals.append(total)
    if len(totals) == 1:
        total, totals, row = totals[0], [], 0
        for height in heights:
            totals.append(total[row : row + height])
            row += height
    bit = where[SUM + 1]

    def fill(side):
        row = 0
        for total, height in zip(totals, heights):
            half = height // 2
            kept[row : row + half] = total[side * half : (side + 1) * half]
            sent[row : row + half] = total[(1 - side) * half : (2 - side) * half].astype(bf16)
            row += half

    for side in range(2):
        pl.when(bit == side)(functools.partial(fill, side))


def chip_grad_kernel(where, left, left_other, right, right_other, kept, sent):
    factor = chip_factor(right, right_other, where[CORE])
    kept[...] = dot(chip_factor(left, left_other, where[ACT]), factor, 0, 0)
    sent[...] = dot(chip_factor(left, left_other, 1 - where[ACT]), factor, 0, 0).astype(bf16)


def far_grad_kernel(shards, planes, where, *refs):
    left, left_other, left_far = refs[:3]
    rights = refs[3:7]
    along, (sent, kept, grad) = refs[7:-3], refs[-3:]
    width = kept.shape[-1]
    grad[...] = dot(
        jnp.concatenate([chip_factor(left, left_other, where[ACT]), left_far[...]], axis=0),
        jnp.concatenate([right[...] for right in rights], axis=0),
        0,
        0,
    )
    height = grad.shape[0] // shards // (planes // 2)
    chunks = grad.shape[1] // width

    def block(row, k):
        rows = slice(row, row + height)
        if k == chunks:
            return along[0][rows] + along[1][rows].astype(f32)
        return grad[rows, k * width : (k + 1) * width]

    def fill(bit):
        for k in range(chunks + bool(along)):
            rows = slice(k * height, (k + 1) * height)
            for s in range(shards):
                for j in range(planes // 2):
                    side, rest = divmod(j, planes // 4)
                    value = block((s * (planes // 2) + j) * height, k)
                    if side == bit:
                        kept[s, rest, rows] = value
                    else:
                        sent[s, rest, rows] = value.astype(bf16)

    for bit in range(2):
        pl.when(where[SUM] == bit)(functools.partial(fill, bit))


def total_kernel(shards, where, kept, got, *refs):
    if len(refs) > shards:
        *gains, own, own_gains = refs[:4]
        sends, found = refs[4:-1], refs[-1]
        size = found.shape[2]
        for i, gain in enumerate(gains):
            for s in range(shards):
                found[s, i : i + 1] = gain[:, s * size : (s + 1) * size]
        own_gains[...] = found[where[SHARD]]
    else:
        own, sends, found = refs[0], refs[1:], None
    shard, first = where[SHARD], sends[0].shape[0] - own.shape[0]
    own[...] = kept[shard, 0] + got[shard, 0].astype(f32)
    for d, send in enumerate(sends):
        row = lax.rem(shard + d + 1, shards)
        send[first:] = (kept[row, 0] + got[row, 0].astype(f32)).astype(bf16)
        if found is not None:
            send[:2, :size] = found[row].astype(bf16)


def far_grad(place, width, left, rights, along=(), after=()):
    shards, planes = place.shards, place.planes
    rows, columns = left[0].shape[2], rights[0].shape[1]
    total = rows // shards // (planes // 2) * (columns // width + bool(along))
    packed = (shards, planes // 4, total, width)
    sent, kept = call(
        functools.partial(far_grad_kernel, shards, planes),
        place.where,
        [*left, *rights, *along],
        [like(packed, bf16), like(packed, f32)],
        scratch=[pltpu.VMEM((rows, columns), f32)],
        after=after,
        cost=2.0,
    )
    got = place.from_bit(sent, 1)
    for step in range(2, place.bits):
        whole = (kept + got.astype(f32)).reshape(shards, 2, -1, total, width)
        kept = pick(whole, place.bit(step), 1)
        got = place.from_bit(pick(whole, 1 - place.bit(step), 1).astype(bf16), step)
    return kept, sent, got


def shard_sums(place, kept, got, gains=(), after=()):
    shards, (_, _, total, width) = place.shards, kept.shape
    outs, scratch = [like((total, width), f32)], []
    if gains:
        size = gains[0].shape[1] // shards
        outs.append(like((len(gains), size), f32))
        scratch.append(pltpu.VMEM((shards, len(gains), size), f32))
    own = call(
        functools.partial(total_kernel, shards),
        place.where,
        [kept, got, *gains],
        outs + [like((total + GAIN_ROWS * bool(gains), width), bf16)] * (shards - 1),
        scratch=scratch,
        after=after,
    )
    own, sends = list(own[: len(outs)]), own[len(outs) :]
    return own, [
        place.permute(send, lambda s, p, c, d=d: (s - d - 1, p)) for d, send in enumerate(sends)
    ]


def round_kernel(counts, first, where, *refs):
    out, at, row = refs[-1], 0, first
    for count in counts:
        total = refs[at][...]
        for ref in refs[at + 1 : at + count]:
            total = total + ref[first:].astype(f32)
        out[row : row + total.shape[0]] = total.astype(bf16)
        row += total.shape[0]
        at += count
    if first:
        total = refs[at][...]
        rows, columns = total.shape
        for ref in refs[1 : counts[0]]:
            total = total + ref[:rows, :columns].astype(f32)
        out[:rows, :columns] = total.astype(bf16)


def place_kernel(orders, bits, first, heights, chunks, where, whole, *outs):
    planes = 1 << bits
    width = whole.shape[-1]
    for plane in range(planes):
        for side in range(2):
            part = whole.at[2 * plane + side]
            spot = sum(
                ((plane >> at) & 1) << (bits - 1 - step) for step, at in enumerate(orders[side])
            )
            row = first
            for out, height, chunk in zip(outs, heights, chunks):
                for k in range(chunk):
                    lanes = slice((side * chunk + k) * width, (side * chunk + k + 1) * width)
                    out[spot, :, lanes] = part[row : row + height].astype(f32)
                    row += height
    if first:
        rows, columns = outs[-1].shape
        total = 0.0
        for rep in range(2 * planes):
            total = total + whole[rep, :rows, :columns].astype(f32)
        outs[-1][...] = total


def spread_kernel(orders, bits, first, heights, chunks, where, *refs):
    planes = 1 << bits
    mine, other, outs = refs[:planes], refs[planes : 2 * planes], refs[2 * planes :]
    width = mine[0].shape[-1]
    starts = []
    for order in orders:
        start = 0
        for step, at in enumerate(order):
            start = start + (((where[PLANE] >> at) & 1) << (bits - 1 - step))
        starts.append(start)

    def fill(core):
        arrays = (other, mine) if core else (mine, other)
        for p in range(planes):
            at = first
            for out, height, chunk in zip(outs, heights, chunks):
                for k in range(chunk):
                    rows = slice(at, at + height)
                    for side in range(2):
                        lanes = slice((side * chunk + k) * width, (side * chunk + k + 1) * width)
                        out[p ^ starts[side], :, lanes] = arrays[side][p][rows].astype(f32)
                    at += height
            if first:
                rows, columns = outs[-2].shape
                for side in range(2):
                    outs[-1][side, p ^ starts[side]] = arrays[side][p][:rows, :columns].astype(f32)

    for core in range(2):
        pl.when(where[CORE] == core)(functools.partial(fill, core))
    if first:
        total = 0.0
        for side in range(2):
            for p in range(planes):
                total = total + outs[-1][side, p]
        outs[-2][...] = total


def spread_grads(place, width, groups, heights, chunks, gains=None, after=(), at_once=False):
    planes = place.planes
    first = 0 if gains is None else GAIN_ROWS
    total = sum(height * chunk for height, chunk in zip(heights, chunks))
    extra = [] if gains is None else [gains]
    mine = list(
        call(
            functools.partial(round_kernel, [len(group) for group in groups], first),
            place.where,
            [array for group in groups for array in group] + extra,
            [like((first + total, width), bf16)],
            after=after,
        )
    )
    part = mine[0]
    if at_once:
        outs = call(
            functools.partial(place_kernel, place.orders, place.bits, first, heights, chunks),
            place.where,
            [lax.all_gather(part, "rep")],
            [
                like((planes, height, 2 * chunk * width), f32)
                for height, chunk in zip(heights, chunks)
            ]
            + [like(array.shape, f32) for array in extra],
            cost=2.0,
        )
        count = len(heights)
        return [out.reshape(-1, out.shape[2]) for out in outs[:count]], list(outs[count:]), part
    for step in reversed(range(place.bits)):
        mine = mine + [place.from_bit(array, step) for array in mine]
    other = [place.from_core(array) for array in mine]
    outs = call(
        functools.partial(spread_kernel, place.orders, place.bits, first, heights, chunks),
        place.where,
        mine + other,
        [
            like((planes, height, 2 * chunk * width), f32)
            for height, chunk in zip(heights, chunks)
        ]
        + [like(array.shape, f32) for array in extra],
        scratch=[pltpu.VMEM((2, planes) + array.shape, f32) for array in extra],
        cost=2.0,
    )
    count = len(heights)
    return [out.reshape(-1, out.shape[2]) for out in outs[:count]], list(outs[count:]), part


def body(
    shards,
    reps,
    tokens,
    segment_ids,
    attn_gain,
    qkv_weight,
    attn_out_weight,
    mlp_gain,
    in_weight,
    out_weight,
    cotangent,
):
    place = Place(shards, reps)
    where = place.where
    tokens, documents, cotangent = tokens[0], segment_ids[0], cotangent[0]
    length, model = tokens.shape
    heads, size = model // HD, out_weight.shape[0] * shards
    width = model // 2
    rows = lambda columns, kind=bf16: like((length, columns), kind)
    halves = lambda columns: like((2, length, columns // 2), bf16)
    padded = like((2, length, -(-size // 2 // 128) * 128), bf16)

    blocks, extra, total, piece, part = pieces(place, [qkv_weight], width)
    gains = jnp.stack([attn_gain, mlp_gain])
    later_blocks, later_extra, later_total, later_piece, later_part = pieces(
        place, [attn_out_weight, in_weight], width, gains=gains
    )
    later = from_shards(place, later_piece, later_part)
    ahead, behind, _ = column_of(
        place, extra, total, from_shards(place, piece, part), after=[later_piece]
    )
    (weight_qkv,), through = finish_gather(place, blocks, ahead, behind, relay=later[:-1])
    later = hold(place, later, after=through)
    (out_block,), _, _, out_piece, out_part = pieces(
        place, [out_weight], width, after=later, planes=1
    )
    out_arrived = from_shards(place, out_piece, out_part)
    ahead, behind, (gain_attn, gain_mlp) = column_of(
        place, later_extra, later_total, later, after=[out_piece]
    )

    across, down = documents[:, None], documents[None, :]
    normed_one, one_parts, cotangent_halves, cotangent_sent, cosine, sine = call(
        functools.partial(start_kernel, shards),
        where,
        [tokens, gain_attn, cotangent, across, down],
        [rows(model), halves(model), halves(model), rows(width)] + [rows(PAIR, f32)] * 2,
        cost=2.0,
    )
    cotangent_factor = (cotangent_halves, place.from_core(cotangent_sent))
    one_factor = (one_parts, place.from_core(one_parts))
    one_factor = one_factor + left_from_chip(place, one_factor)[1:]

    queries, keys, values, attended, attended_parts, probs = call(
        functools.partial(attend_kernel, shards),
        where,
        [normed_one, weight_qkv, cosine, sine, across, down],
        [rows(model)] * 4 + [halves(model), like((heads, length, length), f32)],
        scratch=[pltpu.VMEM((length, 3 * model), f32)],
        after=[cotangent_factor[1]],
        cost=5.0,
    )
    attended_factor = (attended_parts, place.from_core(attended_parts))
    (weight_attn, weight_in), _ = finish_gather(
        place,
        later_blocks,
        ahead,
        behind,
        relay=[attended, one_factor[2], *out_arrived[:-1]],
    )
    weight_out = finish_direct(place, [out_block], out_arrived)
    middle, two_parts, by_gate, by_up, hidden, hidden_parts = call(
        functools.partial(hidden_kernel, shards),
        where,
        [tokens, attended, weight_attn, gain_mlp, weight_in],
        [rows(model, f32), halves(model), rows(size, f32), rows(size, f32), rows(size), padded],
        after=[attended_factor[1]],
        cost=4.0,
    )
    two_factor = (two_parts, place.from_core(two_parts))
    hidden_factor = (hidden_parts, place.from_core(hidden_parts))
    output, gate_up_halves, gate_up_kept, gate_up_sent = call(
        output_kernel,
        where,
        [middle, hidden, weight_out, cotangent, by_gate, by_up],
        [rows(model), halves(2 * size), rows(size), rows(size)],
        cost=3.0,
    )
    gate_up_other = place.from_core(gate_up_sent)
    message, two_far = left_from_chip(place, two_factor, after=[gate_up_kept])
    two_factor = two_factor + (two_far,)
    gate_up_far = right_from_chip(place, gate_up_kept, gate_up_other)
    out_group = near_grad(
        place, hidden_factor, cotangent_factor, size // shards, after=[message]
    )
    grad_middle, low_halves, low_sent, grad_attended, mlp_gain_part = call(
        middle_kernel,
        where,
        [gate_up_halves, weight_in, middle, gain_mlp, cotangent, weight_attn],
        [rows(model, f32), halves(model), rows(width), rows(model), like((1, model), f32)],
        after=[gate_up_other, out_group[0]],
        cost=3.0,
    )
    low_factor = (low_halves, place.from_core(low_sent))
    projected_halves, projected_kept, projected_sent = call(
        attend_back_kernel,
        where,
        [grad_attended, queries, keys, values, probs, cosine, sine],
        [halves(3 * model), rows(3 * width), rows(3 * width)],
        after=[two_far],
        cost=3.0,
    )
    projected_other = place.from_core(projected_sent)
    projected_far = right_from_chip(place, projected_kept, projected_other)
    attn_kept, attn_sent = call(
        chip_grad_kernel,
        where,
        [*attended_factor, *low_factor],
        [like((width, width), f32), like((width, width), bf16)],
        after=[projected_other],
        cost=1.0,
    )
    attn_got = place.from_bit(attn_sent, 0)
    qkv_kept, qkv_sent, qkv_got = far_grad(
        place,
        width,
        one_factor,
        [projected_kept, projected_other, *projected_far],
        after=[attn_sent],
    )
    in_kept, in_sent, in_got = far_grad(
        place,
        width,
        two_factor,
        [gate_up_kept, gate_up_other, *gate_up_far],
        along=[attn_kept, attn_got],
        after=[qkv_sent],
    )
    grad_tokens, attn_gain_part = call(
        tokens_kernel,
        where,
        [projected_halves, weight_qkv, tokens, gain_attn, grad_middle],
        [rows(model, f32), like((1, model), f32)],
        after=[in_sent],
        cost=3.0,
    )
    (qkv_own, gains), qkv_arrived = shard_sums(
        place, qkv_kept, qkv_got, gains=[attn_gain_part, mlp_gain_part]
    )
    (in_own,), in_arrived = shard_sums(place, in_kept, in_got, after=[qkv_own])
    height = size // shards
    for step in range(place.bits):
        kept, sent = call(
            functools.partial(halve_kernel, [len(out_group)], [height]),
            jnp.concatenate([where, place.bit(step).astype(jnp.int32)[None]]),
            out_group,
            [like((height // 2, width), f32), like((height // 2, width), bf16)],
            after=[in_sent],
        )
        out_group, height = [kept, place.from_bit(sent, step)], height // 2
    part = model // shards // place.planes
    (qkv_weight_g,), (gains_g,), early = spread_grads(
        place, width, [[qkv_own, *qkv_arrived]], [part], [3 * model // 2 // width], gains=gains
    )
    (in_weight_g, attn_out_g, out_weight_g), _, _ = spread_grads(
        place,
        width,
        [[in_own, *in_arrived], out_group],
        [part, part, height],
        [size // width, 1, 1],
        after=[early],
    )
    return (
        output[None],
        grad_tokens[None],
        gains_g[0],
        qkv_weight_g,
        attn_out_g,
        gains_g[1],
        in_weight_g,
        out_weight_g,
    )


def solution(mesh):
    return jax.shard_map(
        functools.partial(body, mesh.shape["shard"], mesh.shape["rep"]),
        mesh=mesh,
        in_specs=(
            P(("rep", "shard"), None, None),
            P(("rep", "shard"), None),
            P("shard"),
            P("shard", None),
            P("shard", None),
            P("shard"),
            P("shard", None),
            P("shard", None),
            P(("rep", "shard"), None, None),
        ),
        out_specs=(
            P(("rep", "shard"), None, None),
            P(("rep", "shard"), None, None),
            P("shard"),
            P("shard", None),
            P("shard", None),
            P("shard"),
            P("shard", None),
            P("shard", None),
        ),
        check_vma=False,
    )
```
